32 devices in a mesh: pipe: 4 (over z), dp: 4 (over y, x), tensor: 2 (over core).
Axes of the slice: x: 2, y: 2, z: 4, core: 2. Of those that a mesh axis runs over, the one named last changes fastest.
Arguments:
- queries: bfloat16 [4, 512, 8192], P('pipe', 'dp', 'tensor'), may hold values from -5.5 to 5.5
- cache_keys: bfloat16 [512, 2, 4, 1024], P('dp', 'tensor', 'pipe'), may hold values from -5.5 to 5.5
- cache_values: bfloat16 [512, 2, 4, 1024], P('dp', 'tensor', 'pipe'), may hold values from -40 to 40
- doc_lengths: int32 [4, 6], P('dp'), may hold values from 1 to 64, 128 in all within a row
- row_counts: int32 [4, 4], replicated, may hold values from 24 to 40, as said below
- out_gain: bfloat16 [8192], P('tensor'), may hold values from 0.099609375 to 1.8984375
Outputs:
- regrouped: bfloat16 [4, 512, 8192], P('pipe', 'dp', 'tensor')
The draws below stay inside these ranges and needn't reach their ends.
Inputs may be any that keep to these rules, and one draw needn't show every extreme that they name: row_counts[i, j] is how many rows data group i sends to data group j; each row and each column of row_counts sums to 128; some entry equals 40 in every draw.
All inputs are finite; a program needn't handle non-finite values.
Results may differ from the reference program's by a relative error of at most 0.0085.
Values may be sent and summed in bfloat16 or wider, within the bound.
No kernel may reach another device: no remote copies, remote signals or barrier semaphores. Data moves between devices by JAX's collectives and lax.ppermute only.
A program may use at most 64 MiB of HBM per device.

```python
import math
import jax
import jax.numpy as jnp
import numpy as np
from jax import lax

HEADS = 64
HEAD_DIM = 128
SEQ = 128
NDOC = 6
MOST = 64
TOKENS = 512
N_PIPE = 4
N_DP = 4
N_TENSOR = 2


def shared_keys(key):
    base = jax.random.normal(jax.random.fold_in(key, 11), (TOKENS, HEADS * HEAD_DIM), jnp.float32)
    base = jnp.clip(base, -5.5, 5.5)
    return base


def draw_cache_keys(key, part):
    return shared_keys(key).reshape(TOKENS, N_TENSOR, N_PIPE, HEADS * HEAD_DIM // (N_TENSOR * N_PIPE)).astype(jnp.bfloat16)


def draw_queries(key, part):
    query = jax.random.normal(jax.random.fold_in(key, 13), (N_PIPE, TOKENS, HEADS * HEAD_DIM), jnp.float32)
    query = jnp.clip(query, -5.5, 5.5)
    return query.astype(jnp.bfloat16)


def draw_cache_values(key, part):
    values = jax.random.normal(jax.random.fold_in(key, 21), (TOKENS, HEADS, HEAD_DIM), jnp.float32)
    values = jnp.clip(values, -4.0, 4.0)
    spread = jax.random.uniform(jax.random.fold_in(key, 22), (HEADS,), jnp.float32)
    head_scale = 10.0 ** (0.5 * jnp.arange(HEADS, dtype=jnp.float32) / (HEADS - 1) + 0.5 * spread)
    row_scale = 10.0 ** jax.random.uniform(jax.random.fold_in(key, 23), (TOKENS,), jnp.float32)
    values = values * head_scale[None, :, None] * row_scale[:, None, None] / 10.0
    return values.reshape(TOKENS, N_TENSOR, N_PIPE, HEADS * HEAD_DIM // (N_TENSOR * N_PIPE)).astype(jnp.bfloat16)


def draw_row_counts(key, part):
    base = SEQ // N_DP
    quarter = base // 4
    offsets = jax.random.randint(jax.random.fold_in(key, 31), (N_DP // 2,), 0, quarter + 1)
    offsets = offsets.at[0].set(quarter)
    loads = jnp.stack([base + offsets, base - offsets], axis=1).reshape(N_DP)
    order = jax.random.permutation(jax.random.fold_in(key, 32), N_DP)
    loads = loads[order]
    rows = jnp.arange(N_DP)[:, None]
    cols = jnp.arange(N_DP)[None, :]
    return loads[(cols - rows) % N_DP].astype(jnp.int32)


def profile(number_of, total, reach, lean):
    weights = [(1 << 20) // math.isqrt(rank ** lean) + 1 for rank in range(2, number_of + 1)]
    spare, counts = total - reach - (number_of - 1), [1] * (number_of - 1)
    while spare > 0:
        movable = [i for i in range(number_of - 1) if counts[i] < reach]
        whole, budget = sum([weights[i] for i in movable]), spare
        for i in movable:
            extra = min(reach - counts[i], max(1, budget * weights[i] // whole), spare)
            counts[i] = counts[i] + extra
            spare = spare - extra
    return np.array([reach] + counts)


def ragged_sizes(stream_key, count, total, reach, skew):
    if count == 2:
        one = jax.random.randint(stream_key, (), max(1, total - reach), min(reach, total - 1) + 1)
        return jnp.stack([one, total - one])
    sizes = jnp.asarray(profile(count, total, reach, skew), jnp.int32)
    couples = (count - 1) // 2
    source_of, receiver = sizes[1:1 + 2 * couples:2], sizes[2:2 + 2 * couples:2]
    margin = jnp.minimum(source_of - 1, reach - receiver)
    moved = jax.random.randint(jax.random.fold_in(stream_key, 1), (couples,), 0, 1 << 20) % (margin + 1)
    sizes = sizes.at[1:1 + 2 * couples:2].set(source_of - moved).at[2:2 + 2 * couples:2].set(receiver + moved)
    return sizes[jax.random.permutation(jax.random.fold_in(stream_key, 2), count)]


def setup_inputs(seed: int = 0) -> dict:
    arg_keys = jax.random.split(jax.random.key(seed), 7)
    queries = draw_queries(jax.random.fold_in(arg_keys[6], 71), 0)
    cache_keys = draw_cache_keys(jax.random.fold_in(arg_keys[6], 71), 0)
    cache_values = draw_cache_values(jax.random.fold_in(arg_keys[6], 71), 0)
    doc_lengths = jax.vmap(lambda own: ragged_sizes(own, NDOC, SEQ, MOST, 2))(jax.random.split(arg_keys[3], N_DP)).reshape((N_DP, NDOC)).astype(jnp.int32)
    row_counts = draw_row_counts(jax.random.fold_in(arg_keys[6], 71), 0)
    out_gain = jnp.clip(1.0 + 0.18 * jax.random.normal(arg_keys[5], (HEADS * HEAD_DIM,), jnp.float32), 0.099609375, 1.8984375).astype(jnp.bfloat16)
    return {"queries": queries, "cache_keys": cache_keys, "cache_values": cache_values, "doc_lengths": doc_lengths, "row_counts": row_counts, "out_gain": out_gain}


masked_fill = -1e+30
norm_eps = 1e-06

def doc_ids(lengths, positions):
    ends = jnp.cumsum(lengths).astype(jnp.int32)
    return lax.optimization_barrier(jnp.sum((positions[:, None] >= ends[None, :]).astype(jnp.int32), axis=1))

def regroup_table(row_counts):
    send_start = jnp.cumsum(row_counts, axis=1).astype(jnp.int32) - row_counts
    col_end = jnp.cumsum(row_counts, axis=0).astype(jnp.int32)
    recv_start = col_end - row_counts
    positions = jnp.arange(SEQ, dtype=jnp.int32)
    source = lax.optimization_barrier(jnp.sum((positions[None, :, None] >= col_end.T[:, None, :]).astype(jnp.int32), axis=2))
    onehot = (source[:, :, None] == jnp.arange(N_DP, dtype=jnp.int32)[None, None, :]).astype(jnp.int32)
    begin = lax.optimization_barrier(jnp.sum(onehot * (send_start.T - recv_start.T)[:, None, :], axis=2))
    return (source * SEQ + positions[None, :] + begin).astype(jnp.int32)

def reference(queries, cache_keys, cache_values, doc_lengths, row_counts, out_gain):
    width = HEADS * HEAD_DIM
    scale = 1.0 / HEAD_DIM ** 0.5
    positions = jnp.arange(SEQ, dtype=jnp.int32)
    gain = out_gain.astype(jnp.float32)
    table = regroup_table(row_counts).reshape(-1)
    flat_keys = cache_keys.reshape(TOKENS, width)
    flat_values = cache_values.reshape(TOKENS, width)

    def one_group(section, group):
        start = (group * SEQ).astype(jnp.int32)
        keys = lax.dynamic_slice_in_dim(flat_keys, start, SEQ, 0).astype(jnp.float32).reshape(SEQ, HEADS, HEAD_DIM)
        values = lax.dynamic_slice_in_dim(flat_values, start, SEQ, 0).astype(jnp.float32).reshape(SEQ, HEADS, HEAD_DIM)
        query = lax.dynamic_slice(queries, (section, start, jnp.int32(0)), (1, SEQ, width))[0]
        query = query.astype(jnp.float32).reshape(SEQ, HEADS, HEAD_DIM)
        docs = doc_ids(lax.dynamic_index_in_dim(doc_lengths, group, 0, keepdims=False), positions)
        allowed = (docs[:, None] == docs[None, :]) & (positions[None, :] <= positions[:, None])
        scores = jnp.einsum('qhd,khd->hqk', query, keys, precision=lax.Precision.HIGHEST) * scale
        scores = jnp.where(allowed[None], scores, masked_fill)
        top = lax.optimization_barrier(jnp.max(scores, axis=2))
        weights = jnp.where(allowed[None], jnp.exp(scores - top[:, :, None]), 0.0)
        total = lax.optimization_barrier(jnp.sum(weights, axis=2))
        rounded = lax.optimization_barrier(weights.astype(jnp.bfloat16)).astype(jnp.float32)
        accum = jnp.einsum('hqk,khd->hqd', rounded, values, precision=lax.Precision.HIGHEST)
        attn = (accum / total[:, :, None]).transpose(1, 0, 2).reshape(SEQ, width).astype(jnp.bfloat16)
        wide = attn.astype(jnp.float32)
        mean_sq = lax.optimization_barrier(jnp.sum(wide * wide, axis=1)) / width
        return (wide * lax.rsqrt(mean_sq + norm_eps)[:, None] * gain[None, :]).astype(jnp.bfloat16)

    def one_section(section):
        normed = lax.map(lambda group: one_group(section, group), jnp.arange(N_DP, dtype=jnp.int32))
        return jnp.take(normed.reshape(TOKENS, width), table, axis=0)
    return lax.map(one_section, jnp.arange(N_PIPE, dtype=jnp.int32))
```

```python
import functools

import jax
import jax.numpy as jnp
import numpy as np
from jax import lax
from jax.experimental import pallas as pl
from jax.experimental.pallas import tpu as pltpu
from jax.sharding import PartitionSpec as P

HEADS = 64
HEAD_DIM = 128

masked_fill = -1e30
norm_eps = 1e-06

VMEM = pl.BlockSpec(memory_space=pltpu.VMEM)
SMEM = pl.BlockSpec(memory_space=pltpu.SMEM)
SCOPED = 32 * 1024 * 1024


def iota(shape, dim):
    return lax.broadcasted_iota(jnp.int32, shape, dim)


def allowed_mask(docs, seq):
    rows, cols = iota((seq, seq), 0), iota((seq, seq), 1)
    row_doc = jnp.zeros((seq, seq), jnp.int32)
    col_doc = jnp.zeros((seq, seq), jnp.int32)
    end = jnp.int32(0)
    for k in range(docs.shape[1]):
        end = end + docs[0, k]
        row_doc = row_doc + (rows >= end).astype(jnp.int32)
        col_doc = col_doc + (cols >= end).astype(jnp.int32)
    return (row_doc == col_doc) & (cols <= rows)


def partner(own, step, pairwise):
    return jnp.bitwise_xor(own, step) if pairwise else jnp.int32(step)


def send_matrix(counts, own, seq, cap, pairwise):
    groups = counts.shape[0]
    rows, cols = iota((groups * cap, seq), 0), iota((groups * cap, seq), 1)
    target = jnp.full((groups * cap, seq), -1, jnp.int32)
    for i in range(groups):
        to = partner(own, i, pairwise)
        begin = jnp.int32(0)
        for j in range(groups):
            begin = begin + jnp.where(j < to, counts[own, j], 0)
        inside = (rows >= i * cap) & (rows < i * cap + counts[own, to])
        target = jnp.where(inside, rows - i * cap + begin, target)
    return (cols == target).astype(jnp.float32).astype(jnp.bfloat16)


def place_matrices(counts, own, seq, cap, pairwise, parts):
    groups = counts.shape[0]
    per = groups // parts
    matrices = []
    for part in range(parts):
        rows, cols = iota((seq, per * cap), 0), iota((seq, per * cap), 1)
        target = jnp.full((seq, per * cap), -1, jnp.int32)
        for slot in range(per):
            source = partner(own, part * per + slot, pairwise)
            begin = jnp.int32(0)
            for j in range(groups):
                begin = begin + jnp.where(j < source, counts[j, own], 0)
            inside = (cols >= slot * cap) & (cols < slot * cap + counts[source, own])
            target = jnp.where(inside, cols - slot * cap + begin, target)
        matrices.append((rows == target).astype(jnp.float32).astype(jnp.bfloat16))
    return matrices


def attend_kernel(jobs, parts, cap, pairwise, meta, docs, counts, *refs):
    count = 1 + sum(1 for job in jobs if job is None)
    queries, (k_ref, v_ref) = refs[:count], refs[count : count + 2]
    outs, attn = refs[count + 2 : -1], refs[-1]
    seq, block = k_ref.shape
    scale = 1.0 / HEAD_DIM**0.5
    mask = allowed_mask(docs, seq)
    extra = 0
    for n, job in enumerate(jobs):
        if job is None:
            extra += 1
            q_ref, base = queries[extra], None
        else:
            q_ref, base = queries[0], meta[0, job] * block
        for h in range(block // HEAD_DIM):
            cols = slice(h * HEAD_DIM, (h + 1) * HEAD_DIM)
            if base is None:
                q = q_ref[:, cols]
            else:
                q = q_ref[:, pl.ds(pl.multiple_of(base + h * HEAD_DIM, HEAD_DIM), HEAD_DIM)]
            scores = lax.dot_general(
                q, k_ref[:, cols], (((1,), (1,)), ((), ())), preferred_element_type=jnp.float32
            )
            scores = jnp.where(mask, scores * scale, masked_fill)
            top = jnp.max(scores, axis=1, keepdims=True)
            weights = jnp.exp(scores - top)
            total = jnp.sum(weights, axis=1, keepdims=True)
            accum = jnp.dot(
                weights.astype(jnp.bfloat16), v_ref[:, cols], preferred_element_type=jnp.float32
            )
            out_cols = slice(n * block + h * HEAD_DIM, n * block + (h + 1) * HEAD_DIM)
            attn[:, out_cols] = (accum * (1.0 / total)).astype(jnp.bfloat16)
    send = send_matrix(counts, meta[0, 0], seq, cap, pairwise)
    rows = send.shape[0] // parts
    picked = jnp.dot(send, attn[...], preferred_element_type=jnp.float32)
    for part in range(parts):
        outs[part][...] = picked[part * rows : (part + 1) * rows].astype(jnp.bfloat16)


def attend(plan, jobs, meta, docs, counts, queries, k, v):
    seq, block = k.shape
    width = len(jobs) * block
    rows = plan.groups * plan.cap // plan.parts
    return pl.pallas_call(
        functools.partial(attend_kernel, jobs, plan.parts, plan.cap, plan.pairwise),
        out_shape=[jax.ShapeDtypeStruct((rows, width), jnp.bfloat16)] * plan.parts,
        in_specs=[SMEM] * 3 + [VMEM] * (len(queries) + 2),
        out_specs=[VMEM] * plan.parts,
        scratch_shapes=[pltpu.VMEM((seq, width), jnp.bfloat16)],
        compiler_params=pltpu.CompilerParams(vmem_limit_bytes=SCOPED),
        name="attend",
    )(meta, docs, counts, *queries, k, v)


def squares_of(ref):
    seq, width = ref.shape
    total = jnp.zeros((seq, HEAD_DIM), jnp.float32)
    for c in range(width // HEAD_DIM):
        wide = ref[:, c * HEAD_DIM : (c + 1) * HEAD_DIM].astype(jnp.float32)
        total = total + wide * wide
    return total


def place_kernel(parts, cap, pairwise, others, meta, counts, *refs):
    got, rest = refs[:parts], refs[parts:]
    seq = rest[-1].shape[0]
    blocks, outs = rest[:others], rest[others:]
    squares = None
    if others:
        outs, squares = outs[:-1], outs[-1]
    matrices = place_matrices(counts, meta[0, 0], seq, cap, pairwise, parts)
    block = outs[0].shape[1]
    for n, out in enumerate(outs):
        cols = slice(n * block, (n + 1) * block)
        placed = jnp.zeros((seq, block), jnp.float32)
        for part in range(parts):
            placed = placed + jnp.dot(
                matrices[part], got[part][:, cols], preferred_element_type=jnp.float32
            )
        out[...] = placed.astype(jnp.bfloat16)
    if others:
        total = squares_of(outs[0])
        for ref in blocks:
            total = total + squares_of(ref)
        squares[...] = total


def place(plan, count, seq, meta, counts, got, others=()):
    block = got[0].shape[1] // count
    shapes = [jax.ShapeDtypeStruct((seq, block), jnp.bfloat16)] * count
    if others:
        shapes.append(jax.ShapeDtypeStruct((seq, HEAD_DIM), jnp.float32))
    return pl.pallas_call(
        functools.partial(place_kernel, plan.parts, plan.cap, plan.pairwise, len(others)),
        out_shape=shapes,
        in_specs=[SMEM] * 2 + [VMEM] * (len(got) + len(others)),
        out_specs=[VMEM] * len(shapes),
        compiler_params=pltpu.CompilerParams(vmem_limit_bytes=SCOPED),
        name="place",
    )(meta, counts, *got, *others)


def norm_kernel(slots, sums, meta, *refs):
    blocks, refs = refs[: len(slots)], refs[len(slots) :]
    squares, (gain, out) = refs[:sums], refs[sums:]
    width = HEADS * HEAD_DIM
    lanes = squares[0][...]
    for ref in squares[1:]:
        lanes = lanes + ref[...]
    mean = jnp.sum(lanes, axis=1, keepdims=True) / width
    factor = jnp.broadcast_to(lax.rsqrt(mean + norm_eps), lanes.shape)
    for slot, ref in zip(slots, blocks, strict=True):
        block = ref.shape[1]
        for c in range(block // HEAD_DIM):
            cols = slice(c * HEAD_DIM, (c + 1) * HEAD_DIM)
            at = pl.ds(pl.multiple_of(meta[0, slot] * block + c * HEAD_DIM, HEAD_DIM), HEAD_DIM)
            wide = ref[:, cols].astype(jnp.float32)
            out[:, at] = (wide * factor * gain[:, at]).astype(jnp.bfloat16)


def norm(slots, meta, blocks, squares, gain):
    seq = blocks[0].shape[0]
    return pl.pallas_call(
        functools.partial(norm_kernel, slots, len(squares)),
        out_shape=jax.ShapeDtypeStruct((seq, gain.shape[1]), jnp.bfloat16),
        in_specs=[SMEM] + [VMEM] * (len(blocks) + len(squares) + 1),
        out_specs=VMEM,
        compiler_params=pltpu.CompilerParams(vmem_limit_bytes=SCOPED),
        name="norm",
    )(meta, *blocks, *squares, gain)


class Plan:
    def __init__(self, mesh, seq):
        self.pipe, self.groups, self.tensor = (mesh.shape[a] for a in ("pipe", "dp", "tensor"))
        self.cap = 5 * seq // (4 * self.groups)
        self.pairwise = self.groups == 4 and self.cap % 8 == 0
        self.parts = self.groups if self.pairwise else 1
        n = self.pipe
        order = [0] + list(range(1, n, 2)) + [i for i in reversed(range(2, n)) if i % 2 == 0]
        self.ring = [(order[i], order[(i + 1) % n]) for i in range(n)]
        where = {d: i for i, d in enumerate(order)}
        back = [[order[(where[p] - t) % n] for t in range(n)] for p in range(n)]
        self.meta = np.array(
            [[g] + back[p] for p in range(n) for g in range(self.groups)], np.int32
        )

    def regroup(self, parts):
        if not self.pairwise:
            return [lax.all_to_all(parts[0], "dp", split_axis=0, concat_axis=0, tiled=True)]
        got = [parts[0]]
        for step in range(1, self.groups):
            pairs = [(g, g ^ step) for g in range(self.groups)]
            got.append(lax.ppermute(parts[step], "dp", pairs))
        return got


def body(mesh, queries, cache_keys, cache_values, doc_lengths, row_counts, out_gain):
    query = queries[0]
    seq, local_width = query.shape
    plan = Plan(mesh, seq)
    n = plan.pipe
    block = local_width // n
    forward, backward = plan.ring, [(b, a) for a, b in plan.ring]
    own = lax.axis_index("pipe") * plan.groups + lax.axis_index("dp")
    meta = lax.dynamic_slice_in_dim(jnp.asarray(plan.meta), own, 1, 0)
    keys, values = cache_keys.reshape(seq, block), cache_values.reshape(seq, block)
    gain = out_gain.astype(jnp.float32).reshape(1, local_width)
    run = functools.partial(attend, plan)

    ahead = lax.dynamic_slice_in_dim(query, meta[0, n] * block, block, 1)
    lent = lax.ppermute(ahead, "pipe", forward)
    k, v = lax.ppermute(keys, "pipe", forward), lax.ppermute(values, "pipe", forward)
    sent = run((1, None), meta, doc_lengths, row_counts, (query, lent), keys, values)
    mine, borrowed = place(plan, 2, seq, meta, row_counts, plan.regroup(sent))
    returned = lax.ppermute(borrowed, "pipe", backward)
    blocks = [mine]
    for t in range(1, n - 1):
        if t < n - 2:
            k_next, v_next = lax.ppermute(k, "pipe", forward), lax.ppermute(v, "pipe", forward)
        sent = run((1 + t,), meta, doc_lengths, row_counts, (query,), k, v)
        got = plan.regroup(sent)
        if t < n - 2:
            blocks += place(plan, 1, seq, meta, row_counts, got)
            k, v = k_next, v_next
    last, squares = place(plan, 1, seq, meta, row_counts, got, (*blocks, returned))
    if plan.tensor == 2:
        sums = [squares, lax.ppermute(squares, "tensor", [(0, 1), (1, 0)])]
    else:
        sums = [lax.psum(squares, "tensor")]
    slots = tuple(range(1, n + 1))
    return norm(slots, meta, (*blocks, last, returned), sums, gain)[None]


def solution(mesh):
    return jax.shard_map(
        functools.partial(body, mesh),
        mesh=mesh,
        in_specs=(
            P("pipe", "dp", "tensor"),
            P("dp", "tensor", "pipe", None),
            P("dp", "tensor", "pipe", None),
            P("dp", None),
            P(),
            P("tensor"),
        ),
        out_specs=P("pipe", "dp", "tensor"),
        check_vma=False,
    )
```

```python
import functools

import jax
import jax.numpy as jnp
from jax import lax
from jax.experimental import pallas as pl
from jax.experimental.pallas import tpu as pltpu
from jax.sharding import PartitionSpec as P

HEADS = 64
HEAD_DIM = 128

masked_fill = -1e30
norm_eps = 1e-06
log2_e = 1.4426950408889634

VMEM = pl.BlockSpec(memory_space=pltpu.VMEM)
SMEM = pl.BlockSpec(memory_space=pltpu.SMEM)
ANY = pl.BlockSpec(memory_space=pl.ANY)
PARAMS = pltpu.CompilerParams(vmem_limit_bytes=32 * 1024 * 1024)


def iota(shape, dim):
    return lax.broadcasted_iota(jnp.int32, shape, dim)


def pick(index, table):
    value = jnp.int32(table[0])
    for i, entry in enumerate(table[1:], 1):
        value = jnp.where(index == i, jnp.int32(entry), value)
    return value


def one_hot(condition):
    return condition.astype(jnp.float32).astype(jnp.bfloat16)


class Plan:
    def __init__(self, mesh, seq, local_width):
        self.pipe, self.groups, self.tensor = (mesh.shape[a] for a in ("pipe", "dp", "tensor"))
        self.seq, self.block = seq, local_width // self.pipe
        self.cap = 5 * seq // (4 * self.groups)
        self.pairwise = self.groups == 4 and self.cap % 8 == 0
        self.parts = self.groups if self.pairwise else 1
        self.rows = self.groups * self.cap // self.parts
        n = self.pipe
        order = [0] + list(range(1, n, 2)) + [i for i in reversed(range(2, n)) if i % 2 == 0]
        self.ring = [(order[i], order[(i + 1) % n]) for i in range(n)]
        where = {d: i for i, d in enumerate(order)}
        self.behind = [[order[(where[p] - t) % n] for p in range(n)] for t in range(n)]

    def partner(self, own, step):
        return jnp.bitwise_xor(own, step) if self.pairwise else jnp.int32(step)

    def regroup(self, parts):
        if not self.pairwise:
            return [lax.all_to_all(parts[0], "dp", split_axis=0, concat_axis=0, tiled=True)]
        got = [parts[0]] + [None] * (self.groups - 1)
        for step in reversed(range(1, self.groups)):
            pairs = [(g, g ^ step) for g in range(self.groups)]
            got[step] = lax.ppermute(parts[step], "dp", pairs)
        return got


def split_kernel(plan, query, *refs):
    outs, sems = refs[:-1], refs[-1]
    place = lax.axis_index("pipe")
    copies = []
    for t, out in enumerate(outs):
        begin = pl.multiple_of(pick(place, plan.behind[t]) * plan.block, plan.block)
        copies.append(
            pltpu.make_async_copy(query.at[:, pl.ds(begin, plan.block)], out, sems.at[t])
        )
        copies[-1].start()
    for copy in copies:
        copy.wait()


def split(plan, query):
    shape = jax.ShapeDtypeStruct((plan.seq, plan.block), query.dtype)
    return pl.pallas_call(
        functools.partial(split_kernel, plan),
        out_shape=[shape] * (plan.pipe - 1),
        in_specs=[ANY],
        out_specs=[VMEM] * (plan.pipe - 1),
        scratch_shapes=[pltpu.SemaphoreType.DMA((plan.pipe - 1,))],
        compiler_params=PARAMS,
        name="split",
    )(query)


def tables_kernel(plan, docs, counts, bias, send, *places):
    seq, cap, groups = plan.seq, plan.cap, plan.groups
    own = lax.axis_index("dp")
    rows, cols = iota((seq, seq), 0), iota((seq, seq), 1)
    row_doc = jnp.zeros((seq, seq), jnp.int32)
    col_doc = jnp.zeros((seq, seq), jnp.int32)
    end = jnp.int32(0)
    for k in range(docs.shape[1]):
        end = end + docs[0, k]
        row_doc = row_doc + (rows >= end).astype(jnp.int32)
        col_doc = col_doc + (cols >= end).astype(jnp.int32)
    bias[...] = jnp.where((row_doc == col_doc) & (rows <= cols), 0.0, masked_fill)
    rows, cols = iota((groups * cap, seq), 0), iota((groups * cap, seq), 1)
    target = jnp.full((groups * cap, seq), -1, jnp.int32)
    for i in range(groups):
        to = plan.partner(own, i)
        begin = jnp.int32(0)
        for j in range(groups):
            begin = begin + jnp.where(j < to, counts[own, j], 0)
        inside = (rows >= i * cap) & (rows < i * cap + counts[own, to])
        target = jnp.where(inside, rows - i * cap + begin, target)
    send[...] = one_hot(cols == target)
    per = groups // plan.parts
    for part, out in enumerate(places):
        rows, cols = iota(out.shape, 0), iota(out.shape, 1)
        target = jnp.full(out.shape, -1, jnp.int32)
        for slot in range(per):
            source = plan.partner(own, part * per + slot)
            begin = jnp.int32(0)
            for j in range(groups):
                begin = begin + jnp.where(j < source, counts[j, own], 0)
            inside = (cols >= slot * cap) & (cols < slot * cap + counts[source, own])
            target = jnp.where(inside, cols - slot * cap + begin, target)
        out[...] = one_hot(rows == target)


def tables(plan, docs, counts):
    shapes = [
        jax.ShapeDtypeStruct((plan.seq, plan.seq), jnp.float32),
        jax.ShapeDtypeStruct((plan.groups * plan.cap, plan.seq), jnp.bfloat16),
    ] + [jax.ShapeDtypeStruct((plan.seq, plan.rows), jnp.bfloat16)] * plan.parts
    bias, send, *places = pl.pallas_call(
        functools.partial(tables_kernel, plan),
        out_shape=shapes,
        in_specs=[SMEM] * 2,
        out_specs=[VMEM] * len(shapes),
        compiler_params=PARAMS,
        name="tables",
    )(docs, counts)
    return bias, send, places


def attend_kernel(plan, jobs, *refs):
    queries, (k_ref, v_ref, bias, send) = refs[:jobs], refs[jobs : jobs + 4]
    outs, attn = refs[jobs + 4 : -1], refs[-1]
    block = plan.block
    heads = [slice(h * HEAD_DIM, (h + 1) * HEAD_DIM) for h in range(block // HEAD_DIM)]
    scale = log2_e / HEAD_DIM**0.5
    for n, q_ref in enumerate(queries):
        scores = [
            lax.dot_general(
                k_ref[:, cols],
                q_ref[:, cols],
                (((1,), (1,)), ((), ())),
                preferred_element_type=jnp.float32,
            )
            for cols in heads
        ]
        weights, totals = [], []
        for score in scores:
            score = score * scale + bias[...]
            weight = jnp.exp2(score - jnp.max(score, axis=0, keepdims=True))
            totals.append(jnp.sum(weight, axis=0, keepdims=True))
            weights.append(weight.astype(jnp.bfloat16))
        for cols, weight, total in zip(heads, weights, totals, strict=True):
            accum = lax.dot_general(
                v_ref[:, cols],
                weight,
                (((0,), (0,)), ((), ())),
                preferred_element_type=jnp.float32,
            )
            rows = slice(n * block + cols.start, n * block + cols.stop)
            attn[rows, :] = (accum * (1.0 / total)).astype(jnp.bfloat16)
    picked = lax.dot_general(
        send[...], attn[...], (((1,), (1,)), ((), ())), preferred_element_type=jnp.float32
    )
    for part, out in enumerate(outs):
        out[...] = picked[part * plan.rows : (part + 1) * plan.rows].astype(jnp.bfloat16)


def attend(plan, queries, k, v, bias, send):
    width = len(queries) * plan.block
    return pl.pallas_call(
        functools.partial(attend_kernel, plan, len(queries)),
        out_shape=[jax.ShapeDtypeStruct((plan.rows, width), jnp.bfloat16)] * plan.parts,
        in_specs=[VMEM] * (len(queries) + 4),
        out_specs=[VMEM] * plan.parts,
        scratch_shapes=[pltpu.VMEM((width, plan.seq), jnp.bfloat16)],
        compiler_params=PARAMS,
        name="attend",
    )(*queries, k, v, bias, send)


def squares_of(ref):
    total = None
    for c in range(0, ref.shape[1], HEAD_DIM):
        wide = ref[:, c : c + HEAD_DIM].astype(jnp.float32)
        total = wide * wide if total is None else total + wide * wide
    return total


def place_kernel(plan, extra, sums, *refs):
    parts = plan.parts
    got, matrices, refs = refs[:parts], refs[parts : 2 * parts], refs[2 * parts :]
    blocks, earlier = refs[:extra], refs[extra : extra + sums]
    outs, squares = refs[extra + sums : -1], refs[-1]
    total = None
    for ref in blocks:
        more = squares_of(ref)
        total = more if total is None else total + more
    for ref in earlier:
        total = ref[...] if total is None else total + ref[...]
    for n, out in enumerate(outs):
        cols = slice(n * plan.block, (n + 1) * plan.block)
        placed = None
        for matrix, ref in zip(matrices, got, strict=True):
            more = jnp.dot(matrix[...], ref[:, cols], preferred_element_type=jnp.float32)
            placed = more if placed is None else placed + more
        out[...] = placed.astype(jnp.bfloat16)
        if n == 0:
            for c in range(0, plan.block, HEAD_DIM):
                wide = placed[:, c : c + HEAD_DIM]
                total = wide * wide if total is None else total + wide * wide
    squares[...] = total


def place(plan, got, matrices, blocks=(), sums=()):
    count = got[0].shape[1] // plan.block
    shapes = [jax.ShapeDtypeStruct((plan.seq, plan.block), jnp.bfloat16)] * count
    shapes.append(jax.ShapeDtypeStruct((plan.seq, HEAD_DIM), jnp.float32))
    args = (*got, *matrices, *blocks, *sums)
    return pl.pallas_call(
        functools.partial(place_kernel, plan, len(blocks), len(sums)),
        out_shape=shapes,
        in_specs=[VMEM] * len(args),
        out_specs=[VMEM] * len(shapes),
        compiler_params=PARAMS,
        name="place",
    )(*args)


def norm_kernel(plan, sums, *refs):
    blocks, refs = refs[: plan.pipe], refs[plan.pipe :]
    squares, (gain, out, held, sems) = refs[:sums], refs[sums:]
    width = HEADS * HEAD_DIM
    lanes = squares[0][...]
    for ref in squares[1:]:
        lanes = lanes + ref[...]
    mean = jnp.sum(lanes, axis=1, keepdims=True) / width
    factor = jnp.broadcast_to(lax.rsqrt(mean + norm_eps), lanes.shape)
    device = lax.axis_index("pipe")
    copies = []
    for t, ref in enumerate(blocks):
        begin = pl.multiple_of(pick(device, plan.behind[t]) * plan.block, plan.block)
        for c in range(0, plan.block, HEAD_DIM):
            cols = slice(c, c + HEAD_DIM)
            at = pl.ds(pl.multiple_of(begin + c, HEAD_DIM), HEAD_DIM)
            wide = ref[:, cols].astype(jnp.float32)
            held[t, :, cols] = (wide * factor * gain[:, at]).astype(jnp.bfloat16)
        copies.append(
            pltpu.make_async_copy(held.at[t], out.at[:, pl.ds(begin, plan.block)], sems.at[t])
        )
        copies[-1].start()
    for copy in copies:
        copy.wait()


def norm(plan, blocks, squares, gain):
    n = plan.pipe
    return pl.pallas_call(
        functools.partial(norm_kernel, plan, len(squares)),
        out_shape=jax.ShapeDtypeStruct((plan.seq, n * plan.block), jnp.bfloat16),
        in_specs=[VMEM] * (n + len(squares) + 1),
        out_specs=ANY,
        scratch_shapes=[
            pltpu.VMEM((n, plan.seq, plan.block), jnp.bfloat16),
            pltpu.SemaphoreType.DMA((n,)),
        ],
        compiler_params=PARAMS,
        name="norm",
    )(*blocks, *squares, gain)


def body(mesh, queries, cache_keys, cache_values, doc_lengths, row_counts, out_gain):
    query = queries[0]
    seq, local_width = query.shape
    plan = Plan(mesh, seq, local_width)
    n = plan.pipe
    forward, backward = plan.ring, [(b, a) for a, b in plan.ring]
    keys = cache_keys.reshape(seq, plan.block)
    values = cache_values.reshape(seq, plan.block)
    gain = out_gain.astype(jnp.float32).reshape(1, local_width)

    asked = split(plan, query)
    begin = pick(lax.axis_index("pipe"), plan.behind[n - 1]) * plan.block
    ahead = lax.dynamic_slice_in_dim(query, begin, plan.block, 1)
    bias, send, places = tables(plan, doc_lengths, row_counts)
    lent = lax.ppermute(ahead, "pipe", forward)
    k, v = lax.ppermute(keys, "pipe", forward), lax.ppermute(values, "pipe", forward)
    sent = attend(plan, (asked[0], lent), keys, values, bias, send)
    mine, borrowed, squares = place(plan, plan.regroup(sent), places)
    returned = lax.ppermute(borrowed, "pipe", backward)
    blocks = [mine]
    for t in range(1, n - 1):
        last = t == n - 2
        if not last:
            k_next, v_next = lax.ppermute(k, "pipe", forward), lax.ppermute(v, "pipe", forward)
        got = plan.regroup(attend(plan, (asked[t],), k, v, bias, send))
        placed, squares = place(plan, got, places, (returned,) if last else (), (squares,))
        blocks.append(placed)
        if not last:
            k, v = k_next, v_next
    if plan.tensor == 2:
        sums = [squares, lax.ppermute(squares, "tensor", [(0, 1), (1, 0)])]
    else:
        sums = [lax.psum(squares, "tensor")]
    return norm(plan, (*blocks, returned), sums, gain)[None]


def solution(mesh):
    return jax.shard_map(
        functools.partial(body, mesh),
        mesh=mesh,
        in_specs=(
            P("pipe", "dp", "tensor"),
            P("dp", "tensor", "pipe", None),
            P("dp", "tensor", "pipe", None),
            P("dp", None),
            P(),
            P("tensor"),
        ),
        out_specs=P("pipe", "dp", "tensor"),
        check_vma=False,
    )
```

```python
import functools

import jax
import jax.numpy as jnp
from jax import lax
from jax.experimental import pallas as pl
from jax.experimental.pallas import tpu as pltpu
from jax.sharding import PartitionSpec as P

HEADS = 64
HEAD_DIM = 128

masked_fill = -1e30
norm_eps = 1e-06
log2_e = 1.4426950408889634

VMEM = pl.BlockSpec(memory_space=pltpu.VMEM)
SMEM = pl.BlockSpec(memory_space=pltpu.SMEM)
ANY = pl.BlockSpec(memory_space=pl.ANY)
COST = pl.CostEstimate(flops=1, bytes_accessed=1, transcendentals=0)
PARAMS = pltpu.CompilerParams(vmem_limit_bytes=32 * 1024 * 1024)


def iota(shape, dim):
    return lax.broadcasted_iota(jnp.int32, shape, dim)


def pick(index, table):
    value = jnp.int32(table[0])
    for i, entry in enumerate(table[1:], 1):
        value = jnp.where(index == i, jnp.int32(entry), value)
    return value


def one_hot(condition):
    return condition.astype(jnp.float32).astype(jnp.bfloat16)


class Plan:
    def __init__(self, mesh, seq, local_width):
        self.pipe, self.groups, self.tensor = (mesh.shape[a] for a in ("pipe", "dp", "tensor"))
        self.seq, self.block = seq, local_width // self.pipe
        self.cap = 5 * seq // (4 * self.groups)
        self.pairwise = self.groups == 4 and self.cap % 8 == 0
        self.parts = self.groups if self.pairwise else 1
        self.rows = self.groups * self.cap // self.parts
        self.steps = [0, 3, 1, 2] if self.pairwise else list(range(self.groups))
        n = self.pipe
        order = [0] + list(range(1, n, 2)) + [i for i in reversed(range(2, n)) if i % 2 == 0]
        self.ring = [(order[i], order[(i + 1) % n]) for i in range(n)]
        where = {d: i for i, d in enumerate(order)}
        self.behind = [[order[(where[p] - t) % n] for p in range(n)] for t in range(n)]

    def partner(self, own, i):
        step = jnp.int32(self.steps[i])
        return jnp.bitwise_xor(own, step) if self.pairwise else step

    def regroup(self, parts):
        if not self.pairwise:
            return [lax.all_to_all(parts[0], "dp", split_axis=0, concat_axis=0, tiled=True)]
        got = [parts[0]]
        for step, part in zip(self.steps[1:], parts[1:], strict=True):
            got.append(lax.ppermute(part, "dp", [(g, g ^ step) for g in range(self.groups)]))
        return got


def split_kernel(plan, query, *refs):
    outs, sems = refs[:-1], refs[-1]
    place = lax.axis_index("pipe")
    copies = []
    for t, out in enumerate(outs):
        begin = pl.multiple_of(pick(place, plan.behind[t]) * plan.block, plan.block)
        copies.append(
            pltpu.make_async_copy(query.at[:, pl.ds(begin, plan.block)], out, sems.at[t])
        )
        copies[-1].start()
    for copy in copies:
        copy.wait()


def split(plan, query):
    shape = jax.ShapeDtypeStruct((plan.seq, plan.block), query.dtype)
    return pl.pallas_call(
        functools.partial(split_kernel, plan),
        out_shape=[shape] * (plan.pipe - 1),
        in_specs=[ANY],
        out_specs=[VMEM] * (plan.pipe - 1),
        scratch_shapes=[pltpu.SemaphoreType.DMA((plan.pipe - 1,))],
        compiler_params=PARAMS,
        cost_estimate=COST,
        name="split",
    )(query)


def tables_kernel(plan, docs, counts, bias, send, *places):
    seq, cap, groups = plan.seq, plan.cap, plan.groups
    own = lax.axis_index("dp")
    rows, cols = iota((seq, seq), 0), iota((seq, seq), 1)
    row_doc = jnp.zeros((seq, seq), jnp.int32)
    col_doc = jnp.zeros((seq, seq), jnp.int32)
    end = jnp.int32(0)
    for k in range(docs.shape[1]):
        end = end + docs[0, k]
        row_doc = row_doc + (rows >= end).astype(jnp.int32)
        col_doc = col_doc + (cols >= end).astype(jnp.int32)
    bias[...] = jnp.where((row_doc == col_doc) & (rows <= cols), 0.0, masked_fill)
    rows, cols = iota((groups * cap, seq), 0), iota((groups * cap, seq), 1)
    target = jnp.full((groups * cap, seq), -1, jnp.int32)
    for i in range(groups):
        to = plan.partner(own, i)
        begin = jnp.int32(0)
        for j in range(groups):
            begin = begin + jnp.where(j < to, counts[own, j], 0)
        inside = (rows >= i * cap) & (rows < i * cap + counts[own, to])
        target = jnp.where(inside, rows - i * cap + begin, target)
    send[...] = one_hot(cols == target)
    per = groups // plan.parts
    for part, out in enumerate(places):
        rows, cols = iota(out.shape, 0), iota(out.shape, 1)
        target = jnp.full(out.shape, -1, jnp.int32)
        for slot in range(per):
            source = plan.partner(own, part * per + slot)
            begin = jnp.int32(0)
            for j in range(groups):
                begin = begin + jnp.where(j < source, counts[j, own], 0)
            inside = (cols >= slot * cap) & (cols < slot * cap + counts[source, own])
            target = jnp.where(inside, cols - slot * cap + begin, target)
        out[...] = one_hot(rows == target)


def tables(plan, docs, counts):
    shapes = [
        jax.ShapeDtypeStruct((plan.seq, plan.seq), jnp.float32),
        jax.ShapeDtypeStruct((plan.groups * plan.cap, plan.seq), jnp.bfloat16),
    ] + [jax.ShapeDtypeStruct((plan.seq, plan.rows), jnp.bfloat16)] * plan.parts
    bias, send, *places = pl.pallas_call(
        functools.partial(tables_kernel, plan),
        out_shape=shapes,
        in_specs=[SMEM] * 2,
        out_specs=[VMEM] * len(shapes),
        compiler_params=PARAMS,
        cost_estimate=COST,
        name="tables",
    )(docs, counts)
    return bias, send, places


def attend_kernel(plan, jobs, *refs):
    count = len(jobs)
    operands, (bias, send) = refs[: 3 * count], refs[3 * count : 3 * count + 2]
    outs, attn = refs[-1 - plan.parts : -1], refs[-1]
    scale = log2_e / HEAD_DIM**0.5
    base = 0
    for n, (q_from, k_from, v_from, width) in enumerate(jobs):
        q_ref, k_ref, v_ref = operands[3 * n : 3 * n + 3]
        heads = range(0, width, HEAD_DIM)
        scores = [
            lax.dot_general(
                k_ref[:, k_from + h : k_from + h + HEAD_DIM],
                q_ref[:, q_from + h : q_from + h + HEAD_DIM],
                (((1,), (1,)), ((), ())),
                preferred_element_type=jnp.float32,
            )
            for h in heads
        ]
        weights, totals = [], []
        for score in scores:
            score = score * scale + bias[...]
            weight = jnp.exp2(score - jnp.max(score, axis=0, keepdims=True))
            totals.append(jnp.sum(weight, axis=0, keepdims=True))
            weights.append(weight.astype(jnp.bfloat16))
        for h, weight, total in zip(heads, weights, totals, strict=True):
            accum = lax.dot_general(
                v_ref[:, v_from + h : v_from + h + HEAD_DIM],
                weight,
                (((0,), (0,)), ((), ())),
                preferred_element_type=jnp.float32,
            )
            rows = slice(base + h, base + h + HEAD_DIM)
            attn[rows, :] = (accum * (1.0 / total)).astype(jnp.bfloat16)
        base += width
    picked = lax.dot_general(
        send[...], attn[...], (((1,), (1,)), ((), ())), preferred_element_type=jnp.float32
    )
    for part, out in enumerate(outs):
        out[...] = picked[part * plan.rows : (part + 1) * plan.rows].astype(jnp.bfloat16)


def attend(plan, jobs, bias, send, after=None):
    operands = [ref for job in jobs for ref in job[:3]]
    spans = tuple(job[3:] for job in jobs)
    width = sum(span[-1] for span in spans)
    order = () if after is None else (after,)
    return pl.pallas_call(
        functools.partial(attend_kernel, plan, spans),
        out_shape=[jax.ShapeDtypeStruct((plan.rows, width), jnp.bfloat16)] * plan.parts,
        in_specs=[VMEM] * (len(operands) + 2) + [ANY] * len(order),
        out_specs=[VMEM] * plan.parts,
        scratch_shapes=[pltpu.VMEM((width, plan.seq), jnp.bfloat16)],
        compiler_params=PARAMS,
        cost_estimate=COST,
        name="attend",
    )(*operands, bias, send, *order)


def pack_kernel(k_ref, v_ref, first, second):
    half = k_ref.shape[1] // 2
    first[:, :half] = k_ref[:, :half]
    first[:, half:] = v_ref[:, :half]
    second[:, :half] = k_ref[:, half:]
    second[:, half:] = v_ref[:, half:]


def pack(k, v):
    return pl.pallas_call(
        pack_kernel,
        out_shape=[jax.ShapeDtypeStruct(k.shape, k.dtype)] * 2,
        in_specs=[VMEM] * 2,
        out_specs=[VMEM] * 2,
        compiler_params=PARAMS,
        cost_estimate=COST,
        name="pack",
    )(k, v)


def squares_of(ref):
    total = None
    for c in range(0, ref.shape[1], HEAD_DIM):
        wide = ref[:, c : c + HEAD_DIM].astype(jnp.float32)
        total = wide * wide if total is None else total + wide * wide
    return total


def place_kernel(plan, widths, summed, extra, sums, *refs):
    parts = plan.parts
    got, matrices, refs = refs[:parts], refs[parts : 2 * parts], refs[2 * parts :]
    blocks, earlier = refs[:extra], refs[extra : extra + sums]
    outs = refs[extra + sums :]
    totals = [squares_of(ref) for ref in blocks] + [ref[...] for ref in earlier]
    base = 0
    for n, (width, out) in enumerate(zip(widths, outs, strict=False)):
        placed = None
        for matrix, ref in zip(matrices, got, strict=True):
            more = jnp.dot(
                matrix[...], ref[:, base : base + width], preferred_element_type=jnp.float32
            )
            placed = more if placed is None else placed + more
        out[...] = placed.astype(jnp.bfloat16)
        if n < summed:
            for c in range(0, width, HEAD_DIM):
                totals.append(placed[:, c : c + HEAD_DIM] * placed[:, c : c + HEAD_DIM])
        base += width
    if summed:
        total = totals[0]
        for more in totals[1:]:
            total = total + more
        outs[-1][...] = total


def place(plan, got, matrices, widths, summed=1, blocks=(), sums=()):
    shapes = [jax.ShapeDtypeStruct((plan.seq, width), jnp.bfloat16) for width in widths]
    if summed:
        shapes.append(jax.ShapeDtypeStruct((plan.seq, HEAD_DIM), jnp.float32))
    args = (*got, *matrices, *blocks, *sums)
    return pl.pallas_call(
        functools.partial(place_kernel, plan, widths, summed, len(blocks), len(sums)),
        out_shape=shapes,
        in_specs=[VMEM] * len(args),
        out_specs=[VMEM] * len(shapes),
        compiler_params=PARAMS,
        cost_estimate=COST,
        name="place",
    )(*args)


def norm_kernel(plan, spots, sums, *refs):
    count = len(spots)
    pieces, refs = refs[:count], refs[count:]
    squares, (gain, out, held, sems) = refs[:sums], refs[sums:]
    width = HEADS * HEAD_DIM
    lanes = squares[0][...]
    for ref in squares[1:]:
        lanes = lanes + ref[...]
    mean = jnp.sum(lanes, axis=1, keepdims=True) / width
    factor = jnp.broadcast_to(lax.rsqrt(mean + norm_eps), lanes.shape)
    device = lax.axis_index("pipe")
    copies = []
    for i, ((t, offset), ref) in enumerate(zip(spots, pieces, strict=True)):
        begin = pick(device, plan.behind[t]) * plan.block + offset
        size = ref.shape[1]
        for c in range(0, size, HEAD_DIM):
            at = pl.ds(pl.multiple_of(begin + c, HEAD_DIM), HEAD_DIM)
            wide = ref[:, c : c + HEAD_DIM].astype(jnp.float32)
            spot = slice(t * plan.block + offset + c, t * plan.block + offset + c + HEAD_DIM)
            held[:, spot] = (wide * factor * gain[:, at]).astype(jnp.bfloat16)
        spot = pl.ds(t * plan.block + offset, size)
        at = pl.ds(pl.multiple_of(begin, HEAD_DIM), size)
        copies.append(pltpu.make_async_copy(held.at[:, spot], out.at[:, at], sems.at[i]))
        copies[-1].start()
    for copy in copies:
        copy.wait()


def norm(plan, pieces, squares, gain):
    arrays, spots = [piece[0] for piece in pieces], tuple(piece[1:] for piece in pieces)
    return pl.pallas_call(
        functools.partial(norm_kernel, plan, spots, len(squares)),
        out_shape=jax.ShapeDtypeStruct((plan.seq, plan.pipe * plan.block), jnp.bfloat16),
        in_specs=[VMEM] * (len(arrays) + len(squares) + 1),
        out_specs=ANY,
        scratch_shapes=[
            pltpu.VMEM((plan.seq, plan.pipe * plan.block), jnp.bfloat16),
            pltpu.SemaphoreType.DMA((len(arrays),)),
        ],
        compiler_params=PARAMS,
        cost_estimate=COST,
        name="norm",
    )(*arrays, *squares, gain)


def body(mesh, queries, cache_keys, cache_values, doc_lengths, row_counts, out_gain):
    query = queries[0]
    seq, local_width = query.shape
    plan = Plan(mesh, seq, local_width)
    n, block, half = plan.pipe, plan.block, plan.block // 2
    forward, backward = plan.ring, [(b, a) for a, b in plan.ring]
    keys, values = cache_keys.reshape(seq, block), cache_values.reshape(seq, block)
    gain = out_gain.astype(jnp.float32).reshape(1, local_width)

    begin = pick(lax.axis_index("pipe"), plan.behind[n - 1]) * block
    ahead = lax.dynamic_slice_in_dim(query, begin, block, 1)
    ahead, values_out = lax.optimization_barrier((ahead, values))
    pairs = [(keys, values)]
    k, v = lax.ppermute(keys, "pipe", forward), lax.ppermute(values_out, "pipe", forward)
    lent = lax.ppermute(ahead, "pipe", forward)
    for _ in range(n - 3):
        pairs.append((k, v))
        k, v = lax.ppermute(k, "pipe", forward), lax.ppermute(v, "pipe", forward)
    pairs.append((k, v))

    asked = split(plan, query)
    bias, send, places = tables(plan, doc_lengths, row_counts)
    run = functools.partial(attend, plan, bias=bias, send=send)
    jobs = [(asked[t], *pairs[t], 0, 0, 0, block) for t in range(n - 1)]
    got = [plan.regroup(run([jobs[0], (lent, keys, values, 0, 0, 0, block)]))]
    got += [plan.regroup(run([job])) for job in jobs[1:]]
    mine, borrowed, total = place(plan, got[0], places, (block, block), summed=1)
    borrowed, _ = lax.optimization_barrier((borrowed, pairs[-1][0]))
    returned = lax.ppermute(borrowed, "pipe", backward)

    pieces = [(mine, 0, 0), (returned, n - 1, 0)]
    for t, parts in enumerate(got[1:], 1):
        last = t == n - 2
        placed, total = place(
            plan, parts, places, (block,), blocks=(returned,) if last else (), sums=(total,)
        )
        pieces.append((placed, t, 0))
    if plan.tensor == 2:
        sums = (total, lax.ppermute(total, "tensor", [(0, 1), (1, 0)]))
    else:
        sums = (lax.psum(total, "tensor"),)
    return norm(plan, pieces, sums, gain)[None]


def solution(mesh):
    return jax.shard_map(
        functools.partial(body, mesh),
        mesh=mesh,
        in_specs=(
            P("pipe", "dp", "tensor"),
            P("dp", "tensor", "pipe", None),
            P("dp", "tensor", "pipe", None),
            P("dp", None),
            P(),
            P("tensor"),
        ),
        out_specs=P("pipe", "dp", "tensor"),
        check_vma=False,
    )
```

```python
import functools

import jax
import jax.numpy as jnp
from jax import lax
from jax.experimental import pallas as pl
from jax.experimental.pallas import tpu as pltpu
from jax.sharding import PartitionSpec as P

HEADS = 64
HEAD_DIM = 128

masked_fill = -1e30
norm_eps = 1e-06
log2_e = 1.4426950408889634

VMEM = pl.BlockSpec(memory_space=pltpu.VMEM)
SMEM = pl.BlockSpec(memory_space=pltpu.SMEM)
ANY = pl.BlockSpec(memory_space=pl.ANY)
COST = pl.CostEstimate(flops=1, bytes_accessed=1, transcendentals=0)
PARAMS = pltpu.CompilerParams(vmem_limit_bytes=32 * 1024 * 1024)


def iota(shape, dim):
    return lax.broadcasted_iota(jnp.int32, shape, dim)


def pick(index, table):
    value = jnp.int32(table[0])
    for i, entry in enumerate(table[1:], 1):
        value = jnp.where(index == i, jnp.int32(entry), value)
    return value


def one_hot(condition):
    return condition.astype(jnp.float32).astype(jnp.bfloat16)


class Plan:
    def __init__(self, mesh, seq, local_width):
        self.pipe, self.groups, self.tensor = (mesh.shape[a] for a in ("pipe", "dp", "tensor"))
        self.seq, self.block = seq, local_width // self.pipe
        self.cap = 5 * seq // (4 * self.groups)
        self.pairwise = self.groups == 4 and self.cap % 8 == 0
        self.parts = self.groups if self.pairwise else 1
        self.rows = self.groups * self.cap // self.parts
        self.steps = [0, 3, 1, 2] if self.pairwise else list(range(self.groups))
        n = self.pipe
        order = [0] + list(range(1, n, 2)) + [i for i in reversed(range(2, n)) if i % 2 == 0]
        self.ring = [(order[i], order[(i + 1) % n]) for i in range(n)]
        where = {d: i for i, d in enumerate(order)}
        self.behind = [[order[(where[p] - t) % n] for p in range(n)] for t in range(n)]

    def partner(self, own, i):
        step = jnp.int32(self.steps[i])
        return jnp.bitwise_xor(own, step) if self.pairwise else step

    def regroup(self, parts):
        if not self.pairwise:
            return [lax.all_to_all(parts[0], "dp", split_axis=0, concat_axis=0, tiled=True)]
        got = [parts[0]]
        for step, part in zip(self.steps[1:], parts[1:], strict=True):
            got.append(lax.ppermute(part, "dp", [(g, g ^ step) for g in range(self.groups)]))
        return got


def split_kernel(plan, query, *refs):
    outs, sems = refs[:-1], refs[-1]
    place = lax.axis_index("pipe")
    copies = []
    for t, out in enumerate(outs):
        begin = pl.multiple_of(pick(place, plan.behind[t]) * plan.block, plan.block)
        copies.append(
            pltpu.make_async_copy(query.at[:, pl.ds(begin, plan.block)], out, sems.at[t])
        )
        copies[-1].start()
    for copy in copies:
        copy.wait()


def split(plan, query):
    shape = jax.ShapeDtypeStruct((plan.seq, plan.block), query.dtype)
    return pl.pallas_call(
        functools.partial(split_kernel, plan),
        out_shape=[shape] * (plan.pipe - 1),
        in_specs=[ANY],
        out_specs=[VMEM] * (plan.pipe - 1),
        scratch_shapes=[pltpu.SemaphoreType.DMA((plan.pipe - 1,))],
        compiler_params=PARAMS,
        cost_estimate=COST,
        name="split",
    )(query)


def tables_kernel(plan, docs, counts, bias, send, *places):
    seq, cap, groups = plan.seq, plan.cap, plan.groups
    own = lax.axis_index("dp")
    rows, cols = iota((seq, seq), 0), iota((seq, seq), 1)
    row_doc = jnp.zeros((seq, seq), jnp.int32)
    col_doc = jnp.zeros((seq, seq), jnp.int32)
    end = jnp.int32(0)
    for k in range(docs.shape[1]):
        end = end + docs[0, k]
        row_doc = row_doc + (rows >= end).astype(jnp.int32)
        col_doc = col_doc + (cols >= end).astype(jnp.int32)
    bias[...] = jnp.where((row_doc == col_doc) & (rows <= cols), 0.0, masked_fill)
    rows, cols = iota((groups * cap, seq), 0), iota((groups * cap, seq), 1)
    target = jnp.full((groups * cap, seq), -1, jnp.int32)
    for i in range(groups):
        to = plan.partner(own, i)
        begin = jnp.int32(0)
        for j in range(groups):
            begin = begin + jnp.where(j < to, counts[own, j], 0)
        inside = (rows >= i * cap) & (rows < i * cap + counts[own, to])
        target = jnp.where(inside, rows - i * cap + begin, target)
    send[...] = one_hot(cols == target)
    per = groups // plan.parts
    for part, out in enumerate(places):
        rows, cols = iota(out.shape, 0), iota(out.shape, 1)
        target = jnp.full(out.shape, -1, jnp.int32)
        for slot in range(per):
            source = plan.partner(own, part * per + slot)
            begin = jnp.int32(0)
            for j in range(groups):
                begin = begin + jnp.where(j < source, counts[j, own], 0)
            inside = (cols >= slot * cap) & (cols < slot * cap + counts[source, own])
            target = jnp.where(inside, cols - slot * cap + begin, target)
        out[...] = one_hot(rows == target)


def tables(plan, docs, counts):
    shapes = [
        jax.ShapeDtypeStruct((plan.seq, plan.seq), jnp.float32),
        jax.ShapeDtypeStruct((plan.groups * plan.cap, plan.seq), jnp.bfloat16),
    ] + [jax.ShapeDtypeStruct((plan.seq, plan.rows), jnp.bfloat16)] * plan.parts
    bias, send, *places = pl.pallas_call(
        functools.partial(tables_kernel, plan),
        out_shape=shapes,
        in_specs=[SMEM] * 2,
        out_specs=[VMEM] * len(shapes),
        compiler_params=PARAMS,
        cost_estimate=COST,
        name="tables",
    )(docs, counts)
    return bias, send, places


def attend_kernel(plan, jobs, *refs):
    count = len(jobs)
    operands, (bias, send) = refs[: 3 * count], refs[3 * count : 3 * count + 2]
    outs, attn = refs[-1 - plan.parts : -1], refs[-1]
    scale = log2_e / HEAD_DIM**0.5
    base = 0
    for n, (q_from, k_from, v_from, width) in enumerate(jobs):
        q_ref, k_ref, v_ref = operands[3 * n : 3 * n + 3]
        heads = range(0, width, HEAD_DIM)
        scores = [
            lax.dot_general(
                k_ref[:, k_from + h : k_from + h + HEAD_DIM],
                q_ref[:, q_from + h : q_from + h + HEAD_DIM],
                (((1,), (1,)), ((), ())),
                preferred_element_type=jnp.float32,
            )
            for h in heads
        ]
        weights, totals = [], []
        for score in scores:
            score = score * scale + bias[...]
            weight = jnp.exp2(score - jnp.max(score, axis=0, keepdims=True))
            totals.append(jnp.sum(weight, axis=0, keepdims=True))
            weights.append(weight.astype(jnp.bfloat16))
        for h, weight, total in zip(heads, weights, totals, strict=True):
            accum = lax.dot_general(
                v_ref[:, v_from + h : v_from + h + HEAD_DIM],
                weight,
                (((0,), (0,)), ((), ())),
                preferred_element_type=jnp.float32,
            )
            rows = slice(base + h, base + h + HEAD_DIM)
            attn[rows, :] = (accum * (1.0 / total)).astype(jnp.bfloat16)
        base += width
    picked = lax.dot_general(
        send[...], attn[...], (((1,), (1,)), ((), ())), preferred_element_type=jnp.float32
    )
    for part, out in enumerate(outs):
        out[...] = picked[part * plan.rows : (part + 1) * plan.rows].astype(jnp.bfloat16)


def attend(plan, jobs, bias, send, after=None):
    operands = [ref for job in jobs for ref in job[:3]]
    spans = tuple(job[3:] for job in jobs)
    width = sum(span[-1] for span in spans)
    order = () if after is None else (after,)
    return pl.pallas_call(
        functools.partial(attend_kernel, plan, spans),
        out_shape=[jax.ShapeDtypeStruct((plan.rows, width), jnp.bfloat16)] * plan.parts,
        in_specs=[VMEM] * (len(operands) + 2) + [ANY] * len(order),
        out_specs=[VMEM] * plan.parts,
        scratch_shapes=[pltpu.VMEM((width, plan.seq), jnp.bfloat16)],
        compiler_params=PARAMS,
        cost_estimate=COST,
        name="attend",
    )(*operands, bias, send, *order)


def pack_kernel(k_ref, v_ref, first, second):
    half = k_ref.shape[1] // 2
    first[:, :half] = k_ref[:, :half]
    first[:, half:] = v_ref[:, :half]
    second[:, :half] = k_ref[:, half:]
    second[:, half:] = v_ref[:, half:]


def pack(k, v):
    return pl.pallas_call(
        pack_kernel,
        out_shape=[jax.ShapeDtypeStruct(k.shape, k.dtype)] * 2,
        in_specs=[VMEM] * 2,
        out_specs=[VMEM] * 2,
        compiler_params=PARAMS,
        cost_estimate=COST,
        name="pack",
    )(k, v)


def squares_of(ref):
    total = None
    for c in range(0, ref.shape[1], HEAD_DIM):
        wide = ref[:, c : c + HEAD_DIM].astype(jnp.float32)
        total = wide * wide if total is None else total + wide * wide
    return total


def place_kernel(plan, widths, summed, extra, sums, *refs):
    parts = plan.parts
    got, matrices, refs = refs[:parts], refs[parts : 2 * parts], refs[2 * parts :]
    blocks, earlier = refs[:extra], refs[extra : extra + sums]
    outs = refs[extra + sums :]
    totals = [squares_of(ref) for ref in blocks] + [ref[...] for ref in earlier]
    base = 0
    for n, (width, out) in enumerate(zip(widths, outs, strict=False)):
        placed = None
        for matrix, ref in zip(matrices, got, strict=True):
            more = jnp.dot(
                matrix[...], ref[:, base : base + width], preferred_element_type=jnp.float32
            )
            placed = more if placed is None else placed + more
        out[...] = placed.astype(jnp.bfloat16)
        if n < summed:
            for c in range(0, width, HEAD_DIM):
                totals.append(placed[:, c : c + HEAD_DIM] * placed[:, c : c + HEAD_DIM])
        base += width
    if summed:
        total = totals[0]
        for more in totals[1:]:
            total = total + more
        outs[-1][...] = total


def place(plan, got, matrices, widths, summed=1, blocks=(), sums=()):
    shapes = [jax.ShapeDtypeStruct((plan.seq, width), jnp.bfloat16) for width in widths]
    if summed:
        shapes.append(jax.ShapeDtypeStruct((plan.seq, HEAD_DIM), jnp.float32))
    args = (*got, *matrices, *blocks, *sums)
    return pl.pallas_call(
        functools.partial(place_kernel, plan, widths, summed, len(blocks), len(sums)),
        out_shape=shapes,
        in_specs=[VMEM] * len(args),
        out_specs=[VMEM] * len(shapes),
        compiler_params=PARAMS,
        cost_estimate=COST,
        name="place",
    )(*args)


def norm_kernel(plan, spots, sums, *refs):
    count = len(spots)
    pieces, refs = refs[:count], refs[count:]
    squares, (gain, out, held, sems) = refs[:sums], refs[sums:]
    width = HEADS * HEAD_DIM
    lanes = squares[0][...]
    for ref in squares[1:]:
        lanes = lanes + ref[...]
    mean = jnp.sum(lanes, axis=1, keepdims=True) / width
    factor = jnp.broadcast_to(lax.rsqrt(mean + norm_eps), lanes.shape)
    device = lax.axis_index("pipe")
    copies = []
    for i, ((t, offset), ref) in enumerate(zip(spots, pieces, strict=True)):
        begin = pick(device, plan.behind[t]) * plan.block + offset
        size = ref.shape[1]
        for c in range(0, size, HEAD_DIM):
            at = pl.ds(pl.multiple_of(begin + c, HEAD_DIM), HEAD_DIM)
            wide = ref[:, c : c + HEAD_DIM].astype(jnp.float32)
            spot = slice(t * plan.block + offset + c, t * plan.block + offset + c + HEAD_DIM)
            held[:, spot] = (wide * factor * gain[:, at]).astype(jnp.bfloat16)
        spot = pl.ds(t * plan.block + offset, size)
        at = pl.ds(pl.multiple_of(begin, HEAD_DIM), size)
        copies.append(pltpu.make_async_copy(held.at[:, spot], out.at[:, at], sems.at[i]))
        copies[-1].start()
    for copy in copies:
        copy.wait()


def norm(plan, pieces, squares, gain):
    arrays, spots = [piece[0] for piece in pieces], tuple(piece[1:] for piece in pieces)
    return pl.pallas_call(
        functools.partial(norm_kernel, plan, spots, len(squares)),
        out_shape=jax.ShapeDtypeStruct((plan.seq, plan.pipe * plan.block), jnp.bfloat16),
        in_specs=[VMEM] * (len(arrays) + len(squares) + 1),
        out_specs=ANY,
        scratch_shapes=[
            pltpu.VMEM((plan.seq, plan.pipe * plan.block), jnp.bfloat16),
            pltpu.SemaphoreType.DMA((len(arrays),)),
        ],
        compiler_params=PARAMS,
        cost_estimate=COST,
        name="norm",
    )(*arrays, *squares, gain)


def body(mesh, queries, cache_keys, cache_values, doc_lengths, row_counts, out_gain):
    query = queries[0]
    seq, local_width = query.shape
    plan = Plan(mesh, seq, local_width)
    n, block, half = plan.pipe, plan.block, plan.block // 2
    forward, backward = plan.ring, [(b, a) for a, b in plan.ring]
    keys, values = cache_keys.reshape(seq, block), cache_values.reshape(seq, block)
    gain = out_gain.astype(jnp.float32).reshape(1, local_width)

    begin = pick(lax.axis_index("pipe"), plan.behind[n - 1]) * block
    ahead = lax.dynamic_slice_in_dim(query, begin, block, 1)
    lent = lax.ppermute(ahead, "pipe", forward)
    pairs = [(keys, values)]
    for _ in range(n - 2):
        pairs.append(tuple(lax.ppermute(x, "pipe", forward) for x in pairs[-1]))

    asked = split(plan, query)
    bias, send, places = tables(plan, doc_lengths, row_counts)
    run = functools.partial(attend, plan, bias=bias, send=send)
    jobs = [(asked[t], *pairs[t], 0, 0, 0, block) for t in range(n - 1)]
    got = [plan.regroup(run([jobs[0], (lent, keys, values, 0, 0, 0, block)]))]
    got += [plan.regroup(run([job])) for job in jobs[1:]]
    mine, borrowed, total = place(plan, got[0], places, (block, block), summed=1)
    pieces = [(mine, 0, 0)]
    for t, parts in enumerate(got[1:-1], 1):
        placed, total = place(plan, parts, places, (block,), sums=(total,))
        pieces.append((placed, t, 0))
    borrowed, total, *_ = lax.optimization_barrier((borrowed, total, *pairs[-1]))
    returned = lax.ppermute(borrowed, "pipe", backward)
    placed, total = place(plan, got[-1], places, (block,), blocks=(returned,), sums=(total,))
    pieces += [(placed, n - 2, 0), (returned, n - 1, 0)]
    if plan.tensor == 2:
        sums = (total, lax.ppermute(total, "tensor", [(0, 1), (1, 0)]))
    else:
        sums = (lax.psum(total, "tensor"),)
    return norm(plan, pieces, sums, gain)[None]


def solution(mesh):
    return jax.shard_map(
        functools.partial(body, mesh),
        mesh=mesh,
        in_specs=(
            P("pipe", "dp", "tensor"),
            P("dp", "tensor", "pipe", None),
            P("dp", "tensor", "pipe", None),
            P("dp", None),
            P(),
            P("tensor"),
        ),
        out_specs=P("pipe", "dp", "tensor"),
        check_vma=False,
    )
```

```python
import functools

import jax
import jax.numpy as jnp
from jax import lax
from jax.experimental import pallas as pl
from jax.experimental.pallas import tpu as pltpu
from jax.sharding import PartitionSpec as P

HEADS = 64
HEAD_DIM = 128

masked_fill = -1e30
norm_eps = 1e-06
log2_e = 1.4426950408889634

VMEM = pl.BlockSpec(memory_space=pltpu.VMEM)
SMEM = pl.BlockSpec(memory_space=pltpu.SMEM)
ANY = pl.BlockSpec(memory_space=pl.ANY)
COST = pl.CostEstimate(flops=1, bytes_accessed=1, transcendentals=0)
PARAMS = pltpu.CompilerParams(vmem_limit_bytes=32 * 1024 * 1024)


def iota(shape, dim):
    return lax.broadcasted_iota(jnp.int32, shape, dim)


def pick(index, table):
    value = jnp.int32(table[0])
    for i, entry in enumerate(table[1:], 1):
        value = jnp.where(index == i, jnp.int32(entry), value)
    return value


def one_hot(condition):
    return condition.astype(jnp.float32).astype(jnp.bfloat16)


class Plan:
    def __init__(self, mesh, seq, local_width):
        self.pipe, self.groups, self.tensor = (mesh.shape[a] for a in ("pipe", "dp", "tensor"))
        self.seq, self.block = seq, local_width // self.pipe
        self.cap = 5 * seq // (4 * self.groups)
        self.pairwise = self.groups == 4 and self.cap % 8 == 0
        self.parts = self.groups if self.pairwise else 1
        self.rows = self.groups * self.cap // self.parts
        self.steps = [0, 3, 1, 2] if self.pairwise else list(range(self.groups))
        n = self.pipe
        order = [0] + list(range(1, n, 2)) + [i for i in reversed(range(2, n)) if i % 2 == 0]
        self.ring = [(order[i], order[(i + 1) % n]) for i in range(n)]
        where = {d: i for i, d in enumerate(order)}
        self.behind = [[order[(where[p] - t) % n] for p in range(n)] for t in range(n)]

    def partner(self, own, i):
        step = jnp.int32(self.steps[i])
        return jnp.bitwise_xor(own, step) if self.pairwise else step

    def regroup(self, parts):
        if not self.pairwise:
            return [lax.all_to_all(parts[0], "dp", split_axis=0, concat_axis=0, tiled=True)]
        got = [parts[0]]
        for step, part in zip(self.steps[1:], parts[1:], strict=True):
            got.append(lax.ppermute(part, "dp", [(g, g ^ step) for g in range(self.groups)]))
        return got


def split_kernel(plan, query, *refs):
    outs, sems = refs[:-1], refs[-1]
    place = lax.axis_index("pipe")
    copies = []
    for t, out in enumerate(outs):
        begin = pl.multiple_of(pick(place, plan.behind[t]) * plan.block, plan.block)
        copies.append(
            pltpu.make_async_copy(query.at[:, pl.ds(begin, plan.block)], out, sems.at[t])
        )
        copies[-1].start()
    for copy in copies:
        copy.wait()


def split(plan, query):
    shape = jax.ShapeDtypeStruct((plan.seq, plan.block), query.dtype)
    return pl.pallas_call(
        functools.partial(split_kernel, plan),
        out_shape=[shape] * (plan.pipe - 1),
        in_specs=[ANY],
        out_specs=[VMEM] * (plan.pipe - 1),
        scratch_shapes=[pltpu.SemaphoreType.DMA((plan.pipe - 1,))],
        compiler_params=PARAMS,
        cost_estimate=COST,
        name="split",
    )(query)


def tables_kernel(plan, docs, counts, bias, send, *places):
    seq, cap, groups = plan.seq, plan.cap, plan.groups
    own = lax.axis_index("dp")
    rows, cols = iota((seq, seq), 0), iota((seq, seq), 1)
    row_doc = jnp.zeros((seq, seq), jnp.int32)
    col_doc = jnp.zeros((seq, seq), jnp.int32)
    end = jnp.int32(0)
    for k in range(docs.shape[1]):
        end = end + docs[0, k]
        row_doc = row_doc + (rows >= end).astype(jnp.int32)
        col_doc = col_doc + (cols >= end).astype(jnp.int32)
    bias[...] = jnp.where((row_doc == col_doc) & (rows <= cols), 0.0, masked_fill)
    rows, cols = iota((groups * cap, seq), 0), iota((groups * cap, seq), 1)
    target = jnp.full((groups * cap, seq), -1, jnp.int32)
    for i in range(groups):
        to = plan.partner(own, i)
        begin = jnp.int32(0)
        for j in range(groups):
            begin = begin + jnp.where(j < to, counts[own, j], 0)
        inside = (rows >= i * cap) & (rows < i * cap + counts[own, to])
        target = jnp.where(inside, rows - i * cap + begin, target)
    send[...] = one_hot(cols == target)
    per = groups // plan.parts
    for part, out in enumerate(places):
        rows, cols = iota(out.shape, 0), iota(out.shape, 1)
        target = jnp.full(out.shape, -1, jnp.int32)
        for slot in range(per):
            source = plan.partner(own, part * per + slot)
            begin = jnp.int32(0)
            for j in range(groups):
                begin = begin + jnp.where(j < source, counts[j, own], 0)
            inside = (cols >= slot * cap) & (cols < slot * cap + counts[source, own])
            target = jnp.where(inside, cols - slot * cap + begin, target)
        out[...] = one_hot(rows == target)


def tables(plan, docs, counts):
    shapes = [
        jax.ShapeDtypeStruct((plan.seq, plan.seq), jnp.float32),
        jax.ShapeDtypeStruct((plan.groups * plan.cap, plan.seq), jnp.bfloat16),
    ] + [jax.ShapeDtypeStruct((plan.seq, plan.rows), jnp.bfloat16)] * plan.parts
    bias, send, *places = pl.pallas_call(
        functools.partial(tables_kernel, plan),
        out_shape=shapes,
        in_specs=[SMEM] * 2,
        out_specs=[VMEM] * len(shapes),
        compiler_params=PARAMS,
        cost_estimate=COST,
        name="tables",
    )(docs, counts)
    return bias, send, places


def attend_kernel(plan, jobs, *refs):
    count = len(jobs)
    operands, (bias, send) = refs[: 3 * count], refs[3 * count : 3 * count + 2]
    outs, attn = refs[-1 - plan.parts : -1], refs[-1]
    scale = log2_e / HEAD_DIM**0.5
    base = 0
    for n, (q_from, k_from, v_from, width) in enumerate(jobs):
        q_ref, k_ref, v_ref = operands[3 * n : 3 * n + 3]
        heads = range(0, width, HEAD_DIM)
        scores = [
            lax.dot_general(
                k_ref[:, k_from + h : k_from + h + HEAD_DIM],
                q_ref[:, q_from + h : q_from + h + HEAD_DIM],
                (((1,), (1,)), ((), ())),
                preferred_element_type=jnp.float32,
            )
            for h in heads
        ]
        weights, totals = [], []
        for score in scores:
            score = score * scale + bias[...]
            weight = jnp.exp2(score - jnp.max(score, axis=0, keepdims=True))
            totals.append(jnp.sum(weight, axis=0, keepdims=True))
            weights.append(weight.astype(jnp.bfloat16))
        for h, weight, total in zip(heads, weights, totals, strict=True):
            accum = lax.dot_general(
                v_ref[:, v_from + h : v_from + h + HEAD_DIM],
                weight,
                (((0,), (0,)), ((), ())),
                preferred_element_type=jnp.float32,
            )
            rows = slice(base + h, base + h + HEAD_DIM)
            attn[rows, :] = (accum * (1.0 / total)).astype(jnp.bfloat16)
        base += width
    picked = lax.dot_general(
        send[...], attn[...], (((1,), (1,)), ((), ())), preferred_element_type=jnp.float32
    )
    for part, out in enumerate(outs):
        out[...] = picked[part * plan.rows : (part + 1) * plan.rows].astype(jnp.bfloat16)


def attend(plan, jobs, bias, send, after=None):
    operands = [ref for job in jobs for ref in job[:3]]
    spans = tuple(job[3:] for job in jobs)
    width = sum(span[-1] for span in spans)
    order = () if after is None else (after,)
    return pl.pallas_call(
        functools.partial(attend_kernel, plan, spans),
        out_shape=[jax.ShapeDtypeStruct((plan.rows, width), jnp.bfloat16)] * plan.parts,
        in_specs=[VMEM] * (len(operands) + 2) + [ANY] * len(order),
        out_specs=[VMEM] * plan.parts,
        scratch_shapes=[pltpu.VMEM((width, plan.seq), jnp.bfloat16)],
        compiler_params=PARAMS,
        cost_estimate=COST,
        name="attend",
    )(*operands, bias, send, *order)


def pack_kernel(k_ref, v_ref, first, second):
    half = k_ref.shape[1] // 2
    first[:, :half] = k_ref[:, :half]
    first[:, half:] = v_ref[:, :half]
    second[:, :half] = k_ref[:, half:]
    second[:, half:] = v_ref[:, half:]


def pack(k, v):
    return pl.pallas_call(
        pack_kernel,
        out_shape=[jax.ShapeDtypeStruct(k.shape, k.dtype)] * 2,
        in_specs=[VMEM] * 2,
        out_specs=[VMEM] * 2,
        compiler_params=PARAMS,
        cost_estimate=COST,
        name="pack",
    )(k, v)


def squares_of(ref):
    total = None
    for c in range(0, ref.shape[1], HEAD_DIM):
        wide = ref[:, c : c + HEAD_DIM].astype(jnp.float32)
        total = wide * wide if total is None else total + wide * wide
    return total


def place_kernel(plan, widths, summed, extra, sums, *refs):
    parts = plan.parts
    got, matrices, refs = refs[:parts], refs[parts : 2 * parts], refs[2 * parts :]
    blocks, earlier = refs[:extra], refs[extra : extra + sums]
    outs = refs[extra + sums :]
    totals = [squares_of(ref) for ref in blocks] + [ref[...] for ref in earlier]
    base = 0
    for n, (width, out) in enumerate(zip(widths, outs, strict=False)):
        placed = None
        for matrix, ref in zip(matrices, got, strict=True):
            more = jnp.dot(
                matrix[...], ref[:, base : base + width], preferred_element_type=jnp.float32
            )
            placed = more if placed is None else placed + more
        out[...] = placed.astype(jnp.bfloat16)
        if n < summed:
            for c in range(0, width, HEAD_DIM):
                totals.append(placed[:, c : c + HEAD_DIM] * placed[:, c : c + HEAD_DIM])
        base += width
    if summed:
        total = totals[0]
        for more in totals[1:]:
            total = total + more
        outs[-1][...] = total


def place(plan, got, matrices, widths, summed=1, blocks=(), sums=()):
    shapes = [jax.ShapeDtypeStruct((plan.seq, width), jnp.bfloat16) for width in widths]
    if summed:
        shapes.append(jax.ShapeDtypeStruct((plan.seq, HEAD_DIM), jnp.float32))
    args = (*got, *matrices, *blocks, *sums)
    return pl.pallas_call(
        functools.partial(place_kernel, plan, widths, summed, len(blocks), len(sums)),
        out_shape=shapes,
        in_specs=[VMEM] * len(args),
        out_specs=[VMEM] * len(shapes),
        compiler_params=PARAMS,
        cost_estimate=COST,
        name="place",
    )(*args)


def norm_kernel(plan, spots, sums, *refs):
    count = len(spots)
    pieces, refs = refs[:count], refs[count:]
    squares, (gain, out, held, sems) = refs[:sums], refs[sums:]
    width = HEADS * HEAD_DIM
    lanes = squares[0][...]
    for ref in squares[1:]:
        lanes = lanes + ref[...]
    mean = jnp.sum(lanes, axis=1, keepdims=True) / width
    factor = jnp.broadcast_to(lax.rsqrt(mean + norm_eps), lanes.shape)
    device = lax.axis_index("pipe")
    copies = []
    for i, ((t, offset), ref) in enumerate(zip(spots, pieces, strict=True)):
        begin = pick(device, plan.behind[t]) * plan.block + offset
        size = ref.shape[1]
        for c in range(0, size, HEAD_DIM):
            at = pl.ds(pl.multiple_of(begin + c, HEAD_DIM), HEAD_DIM)
            wide = ref[:, c : c + HEAD_DIM].astype(jnp.float32)
            spot = slice(t * plan.block + offset + c, t * plan.block + offset + c + HEAD_DIM)
            held[:, spot] = (wide * factor * gain[:, at]).astype(jnp.bfloat16)
        spot = pl.ds(t * plan.block + offset, size)
        at = pl.ds(pl.multiple_of(begin, HEAD_DIM), size)
        copies.append(pltpu.make_async_copy(held.at[:, spot], out.at[:, at], sems.at[i]))
        copies[-1].start()
    for copy in copies:
        copy.wait()


def norm(plan, pieces, squares, gain):
    arrays, spots = [piece[0] for piece in pieces], tuple(piece[1:] for piece in pieces)
    return pl.pallas_call(
        functools.partial(norm_kernel, plan, spots, len(squares)),
        out_shape=jax.ShapeDtypeStruct((plan.seq, plan.pipe * plan.block), jnp.bfloat16),
        in_specs=[VMEM] * (len(arrays) + len(squares) + 1),
        out_specs=ANY,
        scratch_shapes=[
            pltpu.VMEM((plan.seq, plan.pipe * plan.block), jnp.bfloat16),
            pltpu.SemaphoreType.DMA((len(arrays),)),
        ],
        compiler_params=PARAMS,
        cost_estimate=COST,
        name="norm",
    )(*arrays, *squares, gain)


def body(mesh, queries, cache_keys, cache_values, doc_lengths, row_counts, out_gain):
    query = queries[0]
    seq, local_width = query.shape
    plan = Plan(mesh, seq, local_width)
    n, block, half = plan.pipe, plan.block, plan.block // 2
    forward, backward = plan.ring, [(b, a) for a, b in plan.ring]
    keys, values = cache_keys.reshape(seq, block), cache_values.reshape(seq, block)
    gain = out_gain.astype(jnp.float32).reshape(1, local_width)

    begin = pick(lax.axis_index("pipe"), plan.behind[n - 1]) * block
    ahead = lax.dynamic_slice_in_dim(query, begin, block, 1)
    lent = lax.ppermute(ahead, "pipe", forward)
    pairs = [(keys, values)]
    for _ in range(n - 2):
        pairs.append(tuple(lax.ppermute(x, "pipe", forward) for x in pairs[-1]))

    asked = split(plan, query)
    bias, send, places = tables(plan, doc_lengths, row_counts)
    run = functools.partial(attend, plan, bias=bias, send=send)
    jobs = [(asked[t], *pairs[t], 0, 0, 0, block) for t in range(n - 1)]
    pieces, sums = [], ()
    for t in range(n - 2):
        got = plan.regroup(run([jobs[t]]))
        placed, total = place(plan, got, places, (block,), sums=sums)
        pieces.append((placed, t, 0))
        sums = (total,)
    borrowed = plan.regroup(run([(lent, keys, values, 0, 0, 0, block)], after=total))
    (borrowed,) = place(plan, borrowed, places, (block,), summed=0)
    borrowed, total, *_ = lax.optimization_barrier((borrowed, total, *pairs[-1]))
    returned = lax.ppermute(borrowed, "pipe", backward)
    got = plan.regroup(run([jobs[n - 2]]))
    placed, total = place(plan, got, places, (block,), blocks=(returned,), sums=(total,))
    pieces += [(placed, n - 2, 0), (returned, n - 1, 0)]
    if plan.tensor == 2:
        sums = (total, lax.ppermute(total, "tensor", [(0, 1), (1, 0)]))
    else:
        sums = (lax.psum(total, "tensor"),)
    return norm(plan, pieces, sums, gain)[None]


def solution(mesh):
    return jax.shard_map(
        functools.partial(body, mesh),
        mesh=mesh,
        in_specs=(
            P("pipe", "dp", "tensor"),
            P("dp", "tensor", "pipe", None),
            P("dp", "tensor", "pipe", None),
            P("dp", None),
            P(),
            P("tensor"),
        ),
        out_specs=P("pipe", "dp", "tensor"),
        check_vma=False,
    )
```

```python
import functools

import jax
import jax.numpy as jnp
from jax import lax
from jax.experimental import pallas as pl
from jax.experimental.pallas import tpu as pltpu
from jax.sharding import PartitionSpec as P

HEADS = 64
HEAD_DIM = 128

masked_fill = -1e30
norm_eps = 1e-06
log2_e = 1.4426950408889634

VMEM = pl.BlockSpec(memory_space=pltpu.VMEM)
SMEM = pl.BlockSpec(memory_space=pltpu.SMEM)
ANY = pl.BlockSpec(memory_space=pl.ANY)
COST = pl.CostEstimate(flops=1, bytes_accessed=1, transcendentals=0)
PARAMS = pltpu.CompilerParams(vmem_limit_bytes=32 * 1024 * 1024)


def iota(shape, dim):
    return lax.broadcasted_iota(jnp.int32, shape, dim)


def pick(index, table):
    value = jnp.int32(table[0])
    for i, entry in enumerate(table[1:], 1):
        value = jnp.where(index == i, jnp.int32(entry), value)
    return value


def one_hot(condition):
    return condition.astype(jnp.float32).astype(jnp.bfloat16)


class Plan:
    def __init__(self, mesh, seq, local_width):
        self.pipe, self.groups, self.tensor = (mesh.shape[a] for a in ("pipe", "dp", "tensor"))
        self.seq, self.block = seq, local_width // self.pipe
        self.cap = 5 * seq // (4 * self.groups)
        self.pairwise = self.groups == 4 and self.cap % 8 == 0
        self.parts = self.groups if self.pairwise else 1
        self.rows = self.groups * self.cap // self.parts
        self.steps = [0, 3, 1, 2] if self.pairwise else list(range(self.groups))
        n = self.pipe
        order = [0] + list(range(1, n, 2)) + [i for i in reversed(range(2, n)) if i % 2 == 0]
        self.ring = [(order[i], order[(i + 1) % n]) for i in range(n)]
        where = {d: i for i, d in enumerate(order)}
        self.behind = [[order[(where[p] - t) % n] for p in range(n)] for t in range(n)]

    def partner(self, own, i):
        step = jnp.int32(self.steps[i])
        return jnp.bitwise_xor(own, step) if self.pairwise else step

    def regroup(self, parts):
        if not self.pairwise:
            return [lax.all_to_all(parts[0], "dp", split_axis=0, concat_axis=0, tiled=True)]
        got = [parts[0]]
        for step, part in zip(self.steps[1:], parts[1:], strict=True):
            got.append(lax.ppermute(part, "dp", [(g, g ^ step) for g in range(self.groups)]))
        return got


def split_kernel(plan, query, *refs):
    outs, sems = refs[:-1], refs[-1]
    place = lax.axis_index("pipe")
    copies = []
    for t, out in enumerate(outs):
        begin = pl.multiple_of(pick(place, plan.behind[t]) * plan.block, plan.block)
        copies.append(
            pltpu.make_async_copy(query.at[:, pl.ds(begin, plan.block)], out, sems.at[t])
        )
        copies[-1].start()
    for copy in copies:
        copy.wait()


def split(plan, query):
    shape = jax.ShapeDtypeStruct((plan.seq, plan.block), query.dtype)
    return pl.pallas_call(
        functools.partial(split_kernel, plan),
        out_shape=[shape] * (plan.pipe - 1),
        in_specs=[ANY],
        out_specs=[VMEM] * (plan.pipe - 1),
        scratch_shapes=[pltpu.SemaphoreType.DMA((plan.pipe - 1,))],
        compiler_params=PARAMS,
        cost_estimate=COST,
        name="split",
    )(query)


def tables_kernel(plan, docs, counts, bias, send, *places):
    seq, cap, groups = plan.seq, plan.cap, plan.groups
    own = lax.axis_index("dp")
    rows, cols = iota((seq, seq), 0), iota((seq, seq), 1)
    row_doc = jnp.zeros((seq, seq), jnp.int32)
    col_doc = jnp.zeros((seq, seq), jnp.int32)
    end = jnp.int32(0)
    for k in range(docs.shape[1]):
        end = end + docs[0, k]
        row_doc = row_doc + (rows >= end).astype(jnp.int32)
        col_doc = col_doc + (cols >= end).astype(jnp.int32)
    bias[...] = jnp.where((row_doc == col_doc) & (rows <= cols), 0.0, masked_fill)
    rows, cols = iota((groups * cap, seq), 0), iota((groups * cap, seq), 1)
    target = jnp.full((groups * cap, seq), -1, jnp.int32)
    for i in range(groups):
        to = plan.partner(own, i)
        begin = jnp.int32(0)
        for j in range(groups):
            begin = begin + jnp.where(j < to, counts[own, j], 0)
        inside = (rows >= i * cap) & (rows < i * cap + counts[own, to])
        target = jnp.where(inside, rows - i * cap + begin, target)
    send[...] = one_hot(cols == target)
    per = groups // plan.parts
    for part, out in enumerate(places):
        rows, cols = iota(out.shape, 0), iota(out.shape, 1)
        target = jnp.full(out.shape, -1, jnp.int32)
        for slot in range(per):
            source = plan.partner(own, part * per + slot)
            begin = jnp.int32(0)
            for j in range(groups):
                begin = begin + jnp.where(j < source, counts[j, own], 0)
            inside = (cols >= slot * cap) & (cols < slot * cap + counts[source, own])
            target = jnp.where(inside, cols - slot * cap + begin, target)
        out[...] = one_hot(rows == target)


def tables(plan, docs, counts):
    shapes = [
        jax.ShapeDtypeStruct((plan.seq, plan.seq), jnp.float32),
        jax.ShapeDtypeStruct((plan.groups * plan.cap, plan.seq), jnp.bfloat16),
    ] + [jax.ShapeDtypeStruct((plan.seq, plan.rows), jnp.bfloat16)] * plan.parts
    bias, send, *places = pl.pallas_call(
        functools.partial(tables_kernel, plan),
        out_shape=shapes,
        in_specs=[SMEM] * 2,
        out_specs=[VMEM] * len(shapes),
        compiler_params=PARAMS,
        cost_estimate=COST,
        name="tables",
    )(docs, counts)
    return bias, send, places


def attend_kernel(plan, jobs, *refs):
    count = len(jobs)
    operands, (bias, send) = refs[: 3 * count], refs[3 * count : 3 * count + 2]
    outs, attn = refs[-1 - plan.parts : -1], refs[-1]
    scale = log2_e / HEAD_DIM**0.5
    base = 0
    for n, (q_from, k_from, v_from, width) in enumerate(jobs):
        q_ref, k_ref, v_ref = operands[3 * n : 3 * n + 3]
        heads = range(0, width, HEAD_DIM)
        scores = [
            lax.dot_general(
                k_ref[:, k_from + h : k_from + h + HEAD_DIM],
                q_ref[:, q_from + h : q_from + h + HEAD_DIM],
                (((1,), (1,)), ((), ())),
                preferred_element_type=jnp.float32,
            )
            for h in heads
        ]
        weights, totals = [], []
        for score in scores:
            score = score * scale + bias[...]
            weight = jnp.exp2(score - jnp.max(score, axis=0, keepdims=True))
            totals.append(jnp.sum(weight, axis=0, keepdims=True))
            weights.append(weight.astype(jnp.bfloat16))
        for h, weight, total in zip(heads, weights, totals, strict=True):
            accum = lax.dot_general(
                v_ref[:, v_from + h : v_from + h + HEAD_DIM],
                weight,
                (((0,), (0,)), ((), ())),
                preferred_element_type=jnp.float32,
            )
            rows = slice(base + h, base + h + HEAD_DIM)
            attn[rows, :] = (accum * (1.0 / total)).astype(jnp.bfloat16)
        base += width
    picked = lax.dot_general(
        send[...], attn[...], (((1,), (1,)), ((), ())), preferred_element_type=jnp.float32
    )
    for part, out in enumerate(outs):
        out[...] = picked[part * plan.rows : (part + 1) * plan.rows].astype(jnp.bfloat16)


def attend(plan, jobs, bias, send, after=None):
    operands = [ref for job in jobs for ref in job[:3]]
    spans = tuple(job[3:] for job in jobs)
    width = sum(span[-1] for span in spans)
    order = () if after is None else (after,)
    return pl.pallas_call(
        functools.partial(attend_kernel, plan, spans),
        out_shape=[jax.ShapeDtypeStruct((plan.rows, width), jnp.bfloat16)] * plan.parts,
        in_specs=[VMEM] * (len(operands) + 2) + [ANY] * len(order),
        out_specs=[VMEM] * plan.parts,
        scratch_shapes=[pltpu.VMEM((width, plan.seq), jnp.bfloat16)],
        compiler_params=PARAMS,
        cost_estimate=COST,
        name="attend",
    )(*operands, bias, send, *order)


def pack_kernel(k_ref, v_ref, first, second):
    half = k_ref.shape[1] // 2
    first[:, :half] = k_ref[:, :half]
    first[:, half:] = v_ref[:, :half]
    second[:, :half] = k_ref[:, half:]
    second[:, half:] = v_ref[:, half:]


def pack(k, v):
    return pl.pallas_call(
        pack_kernel,
        out_shape=[jax.ShapeDtypeStruct(k.shape, k.dtype)] * 2,
        in_specs=[VMEM] * 2,
        out_specs=[VMEM] * 2,
        compiler_params=PARAMS,
        cost_estimate=COST,
        name="pack",
    )(k, v)


def squares_of(ref):
    total = None
    for c in range(0, ref.shape[1], HEAD_DIM):
        wide = ref[:, c : c + HEAD_DIM].astype(jnp.float32)
        total = wide * wide if total is None else total + wide * wide
    return total


def place_kernel(plan, widths, summed, extra, sums, *refs):
    parts = plan.parts
    got, matrices, refs = refs[:parts], refs[parts : 2 * parts], refs[2 * parts :]
    blocks, earlier = refs[:extra], refs[extra : extra + sums]
    outs = refs[extra + sums :]
    totals = [squares_of(ref) for ref in blocks] + [ref[...] for ref in earlier]
    base = 0
    for n, (width, out) in enumerate(zip(widths, outs, strict=False)):
        placed = None
        for matrix, ref in zip(matrices, got, strict=True):
            more = jnp.dot(
                matrix[...], ref[:, base : base + width], preferred_element_type=jnp.float32
            )
            placed = more if placed is None else placed + more
        out[...] = placed.astype(jnp.bfloat16)
        if n < summed:
            for c in range(0, width, HEAD_DIM):
                totals.append(placed[:, c : c + HEAD_DIM] * placed[:, c : c + HEAD_DIM])
        base += width
    if summed:
        total = totals[0]
        for more in totals[1:]:
            total = total + more
        outs[-1][...] = total


def place(plan, got, matrices, widths, summed=1, blocks=(), sums=()):
    shapes = [jax.ShapeDtypeStruct((plan.seq, width), jnp.bfloat16) for width in widths]
    if summed:
        shapes.append(jax.ShapeDtypeStruct((plan.seq, HEAD_DIM), jnp.float32))
    args = (*got, *matrices, *blocks, *sums)
    return pl.pallas_call(
        functools.partial(place_kernel, plan, widths, summed, len(blocks), len(sums)),
        out_shape=shapes,
        in_specs=[VMEM] * len(args),
        out_specs=[VMEM] * len(shapes),
        compiler_params=PARAMS,
        cost_estimate=COST,
        name="place",
    )(*args)


def norm_kernel(plan, spots, sums, *refs):
    count = len(spots)
    pieces, refs = refs[:count], refs[count:]
    squares, (gain, out, held, sems) = refs[:sums], refs[sums:]
    width = HEADS * HEAD_DIM
    lanes = squares[0][...]
    for ref in squares[1:]:
        lanes = lanes + ref[...]
    mean = jnp.sum(lanes, axis=1, keepdims=True) / width
    factor = jnp.broadcast_to(lax.rsqrt(mean + norm_eps), lanes.shape)
    device = lax.axis_index("pipe")
    copies = []
    for i, ((t, offset), ref) in enumerate(zip(spots, pieces, strict=True)):
        begin = pick(device, plan.behind[t]) * plan.block + offset
        size = ref.shape[1]
        for c in range(0, size, HEAD_DIM):
            at = pl.ds(pl.multiple_of(begin + c, HEAD_DIM), HEAD_DIM)
            wide = ref[:, c : c + HEAD_DIM].astype(jnp.float32)
            spot = slice(t * plan.block + offset + c, t * plan.block + offset + c + HEAD_DIM)
            held[:, spot] = (wide * factor * gain[:, at]).astype(jnp.bfloat16)
        spot = pl.ds(t * plan.block + offset, size)
        at = pl.ds(pl.multiple_of(begin, HEAD_DIM), size)
        copies.append(pltpu.make_async_copy(held.at[:, spot], out.at[:, at], sems.at[i]))
        copies[-1].start()
    for copy in copies:
        copy.wait()


def norm(plan, pieces, squares, gain):
    arrays, spots = [piece[0] for piece in pieces], tuple(piece[1:] for piece in pieces)
    return pl.pallas_call(
        functools.partial(norm_kernel, plan, spots, len(squares)),
        out_shape=jax.ShapeDtypeStruct((plan.seq, plan.pipe * plan.block), jnp.bfloat16),
        in_specs=[VMEM] * (len(arrays) + len(squares) + 1),
        out_specs=ANY,
        scratch_shapes=[
            pltpu.VMEM((plan.seq, plan.pipe * plan.block), jnp.bfloat16),
            pltpu.SemaphoreType.DMA((len(arrays),)),
        ],
        compiler_params=PARAMS,
        cost_estimate=COST,
        name="norm",
    )(*arrays, *squares, gain)


def body(mesh, queries, cache_keys, cache_values, doc_lengths, row_counts, out_gain):
    query = queries[0]
    seq, local_width = query.shape
    plan = Plan(mesh, seq, local_width)
    n, block, half = plan.pipe, plan.block, plan.block // 2
    forward, backward = plan.ring, [(b, a) for a, b in plan.ring]
    keys, values = cache_keys.reshape(seq, block), cache_values.reshape(seq, block)
    gain = out_gain.astype(jnp.float32).reshape(1, local_width)

    begin = pick(lax.axis_index("pipe"), plan.behind[n - 1]) * block
    ahead = lax.dynamic_slice_in_dim(query, begin, block, 1)
    asked = split(plan, query)
    bias, send, places = tables(plan, doc_lengths, row_counts)
    run = functools.partial(attend, plan, bias=bias, send=send)
    lent = lax.ppermute(ahead, "pipe", forward)
    sent = run([(asked[0], keys, values, 0, 0, 0, block), (lent, keys, values, 0, 0, 0, block)])
    arrived = plan.regroup(sent)
    pairs = [(keys, values)]
    k, v = lax.ppermute(keys, "pipe", forward), lax.ppermute(values, "pipe", forward)
    for _ in range(n - 3):
        pairs.append((k, v))
        k, *_ = lax.optimization_barrier((k, *arrived))
        k, v = lax.ppermute(k, "pipe", forward), lax.ppermute(v, "pipe", forward)
    pairs.append((k, v))
    jobs = [(asked[t], *pairs[t], 0, 0, 0, block) for t in range(n - 1)]

    mine, borrowed, total = place(plan, arrived, places, (block, block), summed=1)
    pieces = [(mine, 0, 0)]
    for t in range(1, n - 2):
        got = plan.regroup(run([jobs[t]]))
        placed, total = place(plan, got, places, (block,), sums=(total,))
        pieces.append((placed, t, 0))
    borrowed, total, *_ = lax.optimization_barrier((borrowed, total, *pairs[-1]))
    returned = lax.ppermute(borrowed, "pipe", backward)
    got = plan.regroup(run([jobs[n - 2]]))
    placed, total = place(plan, got, places, (block,), blocks=(returned,), sums=(total,))
    pieces += [(placed, n - 2, 0), (returned, n - 1, 0)]
    if plan.tensor == 2:
        sums = (total, lax.ppermute(total, "tensor", [(0, 1), (1, 0)]))
    else:
        sums = (lax.psum(total, "tensor"),)
    return norm(plan, pieces, sums, gain)[None]


def solution(mesh):
    return jax.shard_map(
        functools.partial(body, mesh),
        mesh=mesh,
        in_specs=(
            P("pipe", "dp", "tensor"),
            P("dp", "tensor", "pipe", None),
            P("dp", "tensor", "pipe", None),
            P("dp", None),
            P(),
            P("tensor"),
        ),
        out_specs=P("pipe", "dp", "tensor"),
        check_vma=False,
    )
```

```python
import functools

import jax
import jax.numpy as jnp
from jax import lax
from jax.experimental import pallas as pl
from jax.experimental.pallas import tpu as pltpu
from jax.sharding import PartitionSpec as P

HEADS = 64
HEAD_DIM = 128

masked_fill = -1e30
norm_eps = 1e-06
log2_e = 1.4426950408889634

VMEM = pl.BlockSpec(memory_space=pltpu.VMEM)
SMEM = pl.BlockSpec(memory_space=pltpu.SMEM)
ANY = pl.BlockSpec(memory_space=pl.ANY)
COST = pl.CostEstimate(flops=1, bytes_accessed=1, transcendentals=0)
PARAMS = pltpu.CompilerParams(vmem_limit_bytes=32 * 1024 * 1024)


def iota(shape, dim):
    return lax.broadcasted_iota(jnp.int32, shape, dim)


def pick(index, table):
    value = jnp.int32(table[0])
    for i, entry in enumerate(table[1:], 1):
        value = jnp.where(index == i, jnp.int32(entry), value)
    return value


def one_hot(condition):
    return condition.astype(jnp.float32).astype(jnp.bfloat16)


class Plan:
    def __init__(self, mesh, seq, local_width):
        self.pipe, self.groups, self.tensor = (mesh.shape[a] for a in ("pipe", "dp", "tensor"))
        self.seq, self.block = seq, local_width // self.pipe
        self.cap = 5 * seq // (4 * self.groups)
        self.pairwise = self.groups == 4 and self.cap % 8 == 0
        self.parts = self.groups if self.pairwise else 1
        self.rows = self.groups * self.cap // self.parts
        self.steps = [0, 3, 1, 2] if self.pairwise else list(range(self.groups))
        n = self.pipe
        order = [0] + list(range(1, n, 2)) + [i for i in reversed(range(2, n)) if i % 2 == 0]
        self.ring = [(order[i], order[(i + 1) % n]) for i in range(n)]
        where = {d: i for i, d in enumerate(order)}
        self.behind = [[order[(where[p] - t) % n] for p in range(n)] for t in range(n)]

    def partner(self, own, i):
        step = jnp.int32(self.steps[i])
        return jnp.bitwise_xor(own, step) if self.pairwise else step

    def regroup(self, parts):
        if not self.pairwise:
            return [lax.all_to_all(parts[0], "dp", split_axis=0, concat_axis=0, tiled=True)]
        got = [parts[0]]
        for step, part in zip(self.steps[1:], parts[1:], strict=True):
            got.append(lax.ppermute(part, "dp", [(g, g ^ step) for g in range(self.groups)]))
        return got


def split_kernel(plan, query, *refs):
    outs, sems = refs[:-1], refs[-1]
    place = lax.axis_index("pipe")
    copies = []
    for t, out in enumerate(outs):
        begin = pl.multiple_of(pick(place, plan.behind[t]) * plan.block, plan.block)
        copies.append(
            pltpu.make_async_copy(query.at[:, pl.ds(begin, plan.block)], out, sems.at[t])
        )
        copies[-1].start()
    for copy in copies:
        copy.wait()


def split(plan, query):
    shape = jax.ShapeDtypeStruct((plan.seq, plan.block), query.dtype)
    return pl.pallas_call(
        functools.partial(split_kernel, plan),
        out_shape=[shape] * (plan.pipe - 1),
        in_specs=[ANY],
        out_specs=[VMEM] * (plan.pipe - 1),
        scratch_shapes=[pltpu.SemaphoreType.DMA((plan.pipe - 1,))],
        compiler_params=PARAMS,
        cost_estimate=COST,
        name="split",
    )(query)


def tables_kernel(plan, docs, counts, bias, send, *places):
    seq, cap, groups = plan.seq, plan.cap, plan.groups
    own = lax.axis_index("dp")
    rows, cols = iota((seq, seq), 0), iota((seq, seq), 1)
    row_doc = jnp.zeros((seq, seq), jnp.int32)
    col_doc = jnp.zeros((seq, seq), jnp.int32)
    end = jnp.int32(0)
    for k in range(docs.shape[1]):
        end = end + docs[0, k]
        row_doc = row_doc + (rows >= end).astype(jnp.int32)
        col_doc = col_doc + (cols >= end).astype(jnp.int32)
    bias[...] = jnp.where((row_doc == col_doc) & (rows <= cols), 0.0, masked_fill)
    rows, cols = iota((groups * cap, seq), 0), iota((groups * cap, seq), 1)
    target = jnp.full((groups * cap, seq), -1, jnp.int32)
    for i in range(groups):
        to = plan.partner(own, i)
        begin = jnp.int32(0)
        for j in range(groups):
            begin = begin + jnp.where(j < to, counts[own, j], 0)
        inside = (rows >= i * cap) & (rows < i * cap + counts[own, to])
        target = jnp.where(inside, rows - i * cap + begin, target)
    send[...] = one_hot(cols == target)
    per = groups // plan.parts
    for part, out in enumerate(places):
        rows, cols = iota(out.shape, 0), iota(out.shape, 1)
        target = jnp.full(out.shape, -1, jnp.int32)
        for slot in range(per):
            source = plan.partner(own, part * per + slot)
            begin = jnp.int32(0)
            for j in range(groups):
                begin = begin + jnp.where(j < source, counts[j, own], 0)
            inside = (cols >= slot * cap) & (cols < slot * cap + counts[source, own])
            target = jnp.where(inside, cols - slot * cap + begin, target)
        out[...] = one_hot(rows == target)


def tables(plan, docs, counts):
    shapes = [
        jax.ShapeDtypeStruct((plan.seq, plan.seq), jnp.float32),
        jax.ShapeDtypeStruct((plan.groups * plan.cap, plan.seq), jnp.bfloat16),
    ] + [jax.ShapeDtypeStruct((plan.seq, plan.rows), jnp.bfloat16)] * plan.parts
    bias, send, *places = pl.pallas_call(
        functools.partial(tables_kernel, plan),
        out_shape=shapes,
        in_specs=[SMEM] * 2,
        out_specs=[VMEM] * len(shapes),
        compiler_params=PARAMS,
        cost_estimate=COST,
        name="tables",
    )(docs, counts)
    return bias, send, places


def softmax(score, bias):
    score = score * (log2_e / HEAD_DIM**0.5) + bias
    weight = jnp.exp2(score - jnp.max(score, axis=0, keepdims=True))
    return weight.astype(jnp.bfloat16), 1.0 / jnp.sum(weight, axis=0, keepdims=True)


def head_columns(plan):
    return [slice(c, c + HEAD_DIM) for c in range(0, plan.block, HEAD_DIM)]


def all_weights(plan, q_ref, k_ref, bias):
    scores = [
        lax.dot_general(
            k_ref[:, cols], q_ref[:, cols], (((1,), (1,)), ((), ())), preferred_element_type=jnp.float32
        )
        for cols in head_columns(plan)
    ]
    return [softmax(score, bias[...]) for score in scores]


def weighted(v_ref, cols, weight, inverse):
    accum = lax.dot_general(
        v_ref[:, cols], weight, (((0,), (0,)), ((), ())), preferred_element_type=jnp.float32
    )
    return (accum * inverse).astype(jnp.bfloat16)


def pick_rows(plan, send, attn, outs):
    picked = lax.dot_general(
        send[...], attn[...], (((1,), (1,)), ((), ())), preferred_element_type=jnp.float32
    )
    for part, out in enumerate(outs):
        out[...] = picked[part * plan.rows : (part + 1) * plan.rows].astype(jnp.bfloat16)


def heads_kernel(plan, q_ref, k_ref, v_ref, bias, _, attn):
    weights = all_weights(plan, q_ref, k_ref, bias)
    for cols, (weight, inverse) in zip(head_columns(plan), weights, strict=True):
        attn[cols, :] = weighted(v_ref, cols, weight, inverse)


def heads(plan, query, k, v, bias, after):
    return pl.pallas_call(
        functools.partial(heads_kernel, plan),
        out_shape=jax.ShapeDtypeStruct((plan.block, plan.seq), jnp.bfloat16),
        in_specs=[VMEM] * 4 + [ANY],
        out_specs=VMEM,
        compiler_params=PARAMS,
        cost_estimate=COST,
        name="heads",
    )(query, k, v, bias, after)


def attend_kernel(plan, bases, q_ref, k_ref, v_ref, bias, send, *refs):
    outs, attn = refs[-1 - plan.parts : -1], refs[-1]
    for i, base in enumerate(refs[:bases]):
        attn[i * plan.block : (i + 1) * plan.block, :] = base[...]
    weights = all_weights(plan, q_ref, k_ref, bias)
    for cols, (weight, inverse) in zip(head_columns(plan), weights, strict=True):
        rows = slice(bases * plan.block + cols.start, bases * plan.block + cols.stop)
        attn[rows, :] = weighted(v_ref, cols, weight, inverse)
    pick_rows(plan, send, attn, outs)


def attend(plan, query, k, v, bias, send, bases=(), after=()):
    width = (len(bases) + 1) * plan.block
    return pl.pallas_call(
        functools.partial(attend_kernel, plan, len(bases)),
        out_shape=[jax.ShapeDtypeStruct((plan.rows, width), jnp.bfloat16)] * plan.parts,
        in_specs=[VMEM] * (5 + len(bases)) + [ANY] * len(after),
        out_specs=[VMEM] * plan.parts,
        scratch_shapes=[pltpu.VMEM((width, plan.seq), jnp.bfloat16)],
        compiler_params=PARAMS,
        cost_estimate=COST,
        name="attend",
    )(query, k, v, bias, send, *bases, *after)


def weigh_kernel(plan, q_ref, k_ref, bias, *refs):
    weights, inverses = refs[-2:]
    found = all_weights(plan, q_ref, k_ref, bias)
    for h, (cols, (weight, inverse)) in enumerate(zip(head_columns(plan), found, strict=True)):
        weights[cols, :] = weight
        inverses[h : h + 1, :] = inverse


def weigh(plan, query, k, bias, after=()):
    count = plan.block // HEAD_DIM
    return pl.pallas_call(
        functools.partial(weigh_kernel, plan),
        out_shape=[
            jax.ShapeDtypeStruct((plan.block, plan.seq), jnp.bfloat16),
            jax.ShapeDtypeStruct((count, plan.seq), jnp.float32),
        ],
        in_specs=[VMEM] * 3 + [ANY] * len(after),
        out_specs=[VMEM] * 2,
        compiler_params=PARAMS,
        cost_estimate=COST,
        name="weigh",
    )(query, k, bias, *after)


def finish_kernel(plan, weights, inverses, v_ref, send, *refs):
    outs, attn = refs[:-1], refs[-1]
    for h, cols in enumerate(head_columns(plan)):
        attn[cols, :] = weighted(v_ref, cols, weights[cols, :], inverses[h : h + 1, :])
    pick_rows(plan, send, attn, outs)


def finish(plan, weights, inverses, v, send):
    return pl.pallas_call(
        functools.partial(finish_kernel, plan),
        out_shape=[jax.ShapeDtypeStruct((plan.rows, plan.block), jnp.bfloat16)] * plan.parts,
        in_specs=[VMEM] * 4,
        out_specs=[VMEM] * plan.parts,
        scratch_shapes=[pltpu.VMEM((plan.block, plan.seq), jnp.bfloat16)],
        compiler_params=PARAMS,
        cost_estimate=COST,
        name="finish",
    )(weights, inverses, v, send)


def squares_of(ref):
    total = None
    for c in range(0, ref.shape[1], HEAD_DIM):
        wide = ref[:, c : c + HEAD_DIM].astype(jnp.float32)
        total = wide * wide if total is None else total + wide * wide
    return total


def place_kernel(plan, widths, summed, extra, sums, *refs):
    parts = plan.parts
    got, matrices, refs = refs[:parts], refs[parts : 2 * parts], refs[2 * parts :]
    blocks, earlier = refs[:extra], refs[extra : extra + sums]
    outs = refs[extra + sums :]
    totals = [squares_of(ref) for ref in blocks] + [ref[...] for ref in earlier]
    base = 0
    for n, (width, out) in enumerate(zip(widths, outs, strict=False)):
        placed = None
        for matrix, ref in zip(matrices, got, strict=True):
            more = jnp.dot(
                matrix[...], ref[:, base : base + width], preferred_element_type=jnp.float32
            )
            placed = more if placed is None else placed + more
        out[...] = placed.astype(jnp.bfloat16)
        if n < summed:
            for c in range(0, width, HEAD_DIM):
                totals.append(placed[:, c : c + HEAD_DIM] * placed[:, c : c + HEAD_DIM])
        base += width
    if summed:
        total = totals[0]
        for more in totals[1:]:
            total = total + more
        outs[-1][...] = total


def place(plan, got, matrices, widths, summed=1, blocks=(), sums=()):
    shapes = [jax.ShapeDtypeStruct((plan.seq, width), jnp.bfloat16) for width in widths]
    if summed:
        shapes.append(jax.ShapeDtypeStruct((plan.seq, HEAD_DIM), jnp.float32))
    args = (*got, *matrices, *blocks, *sums)
    return pl.pallas_call(
        functools.partial(place_kernel, plan, widths, summed, len(blocks), len(sums)),
        out_shape=shapes,
        in_specs=[VMEM] * len(args),
        out_specs=[VMEM] * len(shapes),
        compiler_params=PARAMS,
        cost_estimate=COST,
        name="place",
    )(*args)


def norm_kernel(plan, spots, sums, *refs):
    count = len(spots)
    pieces, refs = refs[:count], refs[count:]
    squares, (gain, out, held, sems) = refs[:sums], refs[sums:]
    width = HEADS * HEAD_DIM
    lanes = squares[0][...]
    for ref in squares[1:]:
        lanes = lanes + ref[...]
    mean = jnp.sum(lanes, axis=1, keepdims=True) / width
    factor = jnp.broadcast_to(lax.rsqrt(mean + norm_eps), lanes.shape)
    device = lax.axis_index("pipe")
    copies = []
    for i, ((t, offset), ref) in enumerate(zip(spots, pieces, strict=True)):
        begin = pick(device, plan.behind[t]) * plan.block + offset
        size = ref.shape[1]
        for c in range(0, size, HEAD_DIM):
            at = pl.ds(pl.multiple_of(begin + c, HEAD_DIM), HEAD_DIM)
            wide = ref[:, c : c + HEAD_DIM].astype(jnp.float32)
            spot = slice(t * plan.block + offset + c, t * plan.block + offset + c + HEAD_DIM)
            held[:, spot] = (wide * factor * gain[:, at]).astype(jnp.bfloat16)
        spot = pl.ds(t * plan.block + offset, size)
        at = pl.ds(pl.multiple_of(begin, HEAD_DIM), size)
        copies.append(pltpu.make_async_copy(held.at[:, spot], out.at[:, at], sems.at[i]))
        copies[-1].start()
    for copy in copies:
        copy.wait()


def norm(plan, pieces, squares, gain):
    arrays, spots = [piece[0] for piece in pieces], tuple(piece[1:] for piece in pieces)
    return pl.pallas_call(
        functools.partial(norm_kernel, plan, spots, len(squares)),
        out_shape=jax.ShapeDtypeStruct((plan.seq, plan.pipe * plan.block), jnp.bfloat16),
        in_specs=[VMEM] * (len(arrays) + len(squares) + 1),
        out_specs=ANY,
        scratch_shapes=[
            pltpu.VMEM((plan.seq, plan.pipe * plan.block), jnp.bfloat16),
            pltpu.SemaphoreType.DMA((len(arrays),)),
        ],
        compiler_params=PARAMS,
        cost_estimate=COST,
        name="norm",
    )(*arrays, *squares, gain)


def body(mesh, queries, cache_keys, cache_values, doc_lengths, row_counts, out_gain):
    query = queries[0]
    seq, local_width = query.shape
    plan = Plan(mesh, seq, local_width)
    n, block, half = plan.pipe, plan.block, plan.block // 2
    forward, backward = plan.ring, [(b, a) for a, b in plan.ring]
    keys, values = cache_keys.reshape(seq, block), cache_values.reshape(seq, block)
    gain = out_gain.astype(jnp.float32).reshape(1, local_width)

    begin = pick(lax.axis_index("pipe"), plan.behind[n - 1]) * block
    ahead = lax.dynamic_slice_in_dim(query, begin, block, 1)
    asked = split(plan, query)
    bias, send, places = tables(plan, doc_lengths, row_counts)
    k, v = lax.ppermute(keys, "pipe", forward), lax.ppermute(values, "pipe", forward)
    lent = lax.ppermute(ahead, "pipe", forward)
    own = heads(plan, asked[0], keys, values, bias, after=bias)
    arrived = plan.regroup(attend(plan, lent, keys, values, bias, send, bases=(own,)))
    mine, borrowed, total = place(plan, arrived, places, (block, block), summed=1)
    pieces = [(mine, 0, 0)]
    for t in range(1, n - 2):
        sent = attend(plan, asked[t], k, v, bias, send)
        got = plan.regroup(sent)
        placed, total = place(plan, got, places, (block,), sums=(total,))
        pieces.append((placed, t, 0))
        if t == 1:
            v, *_ = lax.optimization_barrier((v, *arrived))
        k, v = lax.ppermute(k, "pipe", forward), lax.ppermute(v, "pipe", forward)
    weights = weigh(plan, asked[n - 2], k, bias, after=())
    borrowed, *_ = lax.optimization_barrier((borrowed, *weights, v, *got))
    returned = lax.ppermute(borrowed, "pipe", backward)
    got = plan.regroup(finish(plan, *weights, v, send))
    placed, total = place(plan, got, places, (block,), blocks=(returned,), sums=(total,))
    pieces += [(placed, n - 2, 0), (returned, n - 1, 0)]
    if plan.tensor == 2:
        sums = (total, lax.ppermute(total, "tensor", [(0, 1), (1, 0)]))
    else:
        sums = (lax.psum(total, "tensor"),)
    return norm(plan, pieces, sums, gain)[None]


def solution(mesh):
    return jax.shard_map(
        functools.partial(body, mesh),
        mesh=mesh,
        in_specs=(
            P("pipe", "dp", "tensor"),
            P("dp", "tensor", "pipe", None),
            P("dp", "tensor", "pipe", None),
            P("dp", None),
            P(),
            P("tensor"),
        ),
        out_specs=P("pipe", "dp", "tensor"),
        check_vma=False,
    )
```

```python
import functools

import jax
import jax.numpy as jnp
from jax import lax
from jax.experimental import pallas as pl
from jax.experimental.pallas import tpu as pltpu
from jax.sharding import PartitionSpec as P

HEADS = 64
HEAD_DIM = 128

masked_fill = -1e30
norm_eps = 1e-06
log2_e = 1.4426950408889634

VMEM = pl.BlockSpec(memory_space=pltpu.VMEM)
SMEM = pl.BlockSpec(memory_space=pltpu.SMEM)
ANY = pl.BlockSpec(memory_space=pl.ANY)
COST = pl.CostEstimate(flops=1, bytes_accessed=1, transcendentals=0)
PARAMS = pltpu.CompilerParams(vmem_limit_bytes=32 * 1024 * 1024)


def iota(shape, dim):
    return lax.broadcasted_iota(jnp.int32, shape, dim)


def pick(index, table):
    value = jnp.int32(table[0])
    for i, entry in enumerate(table[1:], 1):
        value = jnp.where(index == i, jnp.int32(entry), value)
    return value


def one_hot(condition):
    return condition.astype(jnp.float32).astype(jnp.bfloat16)


class Plan:
    def __init__(self, mesh, seq, local_width):
        self.pipe, self.groups, self.tensor = (mesh.shape[a] for a in ("pipe", "dp", "tensor"))
        self.seq, self.block = seq, local_width // self.pipe
        self.cap = 5 * seq // (4 * self.groups)
        self.pairwise = self.groups == 4 and self.cap % 8 == 0
        self.parts = self.groups if self.pairwise else 1
        self.rows = self.groups * self.cap // self.parts
        self.steps = [0, 3, 1, 2] if self.pairwise else list(range(self.groups))
        n = self.pipe
        order = [0] + list(range(1, n, 2)) + [i for i in reversed(range(2, n)) if i % 2 == 0]
        self.ring = [(order[i], order[(i + 1) % n]) for i in range(n)]
        where = {d: i for i, d in enumerate(order)}
        self.behind = [[order[(where[p] - t) % n] for p in range(n)] for t in range(n)]

    def partner(self, own, i):
        step = jnp.int32(self.steps[i])
        return jnp.bitwise_xor(own, step) if self.pairwise else step

    def regroup(self, parts):
        if not self.pairwise:
            return [lax.all_to_all(parts[0], "dp", split_axis=0, concat_axis=0, tiled=True)]
        got = [parts[0]]
        for step, part in zip(self.steps[1:], parts[1:], strict=True):
            got.append(lax.ppermute(part, "dp", [(g, g ^ step) for g in range(self.groups)]))
        return got


def split_kernel(plan, query, *refs):
    outs, sems = refs[:-1], refs[-1]
    place = lax.axis_index("pipe")
    copies = []
    for t, out in enumerate(outs):
        begin = pl.multiple_of(pick(place, plan.behind[t]) * plan.block, plan.block)
        copies.append(
            pltpu.make_async_copy(query.at[:, pl.ds(begin, plan.block)], out, sems.at[t])
        )
        copies[-1].start()
    for copy in copies:
        copy.wait()


def split(plan, query):
    shape = jax.ShapeDtypeStruct((plan.seq, plan.block), query.dtype)
    return pl.pallas_call(
        functools.partial(split_kernel, plan),
        out_shape=[shape] * (plan.pipe - 1),
        in_specs=[ANY],
        out_specs=[VMEM] * (plan.pipe - 1),
        scratch_shapes=[pltpu.SemaphoreType.DMA((plan.pipe - 1,))],
        compiler_params=PARAMS,
        cost_estimate=COST,
        name="split",
    )(query)


def tables_kernel(plan, docs, counts, bias, send, *places):
    seq, cap, groups = plan.seq, plan.cap, plan.groups
    own = lax.axis_index("dp")
    rows, cols = iota((seq, seq), 0), iota((seq, seq), 1)
    row_doc = jnp.zeros((seq, seq), jnp.int32)
    col_doc = jnp.zeros((seq, seq), jnp.int32)
    end = jnp.int32(0)
    for k in range(docs.shape[1]):
        end = end + docs[0, k]
        row_doc = row_doc + (rows >= end).astype(jnp.int32)
        col_doc = col_doc + (cols >= end).astype(jnp.int32)
    bias[...] = jnp.where((row_doc == col_doc) & (rows <= cols), 0.0, masked_fill)
    rows, cols = iota((groups * cap, seq), 0), iota((groups * cap, seq), 1)
    target = jnp.full((groups * cap, seq), -1, jnp.int32)
    for i in range(groups):
        to = plan.partner(own, i)
        begin = jnp.int32(0)
        for j in range(groups):
            begin = begin + jnp.where(j < to, counts[own, j], 0)
        inside = (rows >= i * cap) & (rows < i * cap + counts[own, to])
        target = jnp.where(inside, rows - i * cap + begin, target)
    send[...] = one_hot(cols == target)
    per = groups // plan.parts
    for part, out in enumerate(places):
        rows, cols = iota(out.shape, 0), iota(out.shape, 1)
        target = jnp.full(out.shape, -1, jnp.int32)
        for slot in range(per):
            source = plan.partner(own, part * per + slot)
            begin = jnp.int32(0)
            for j in range(groups):
                begin = begin + jnp.where(j < source, counts[j, own], 0)
            inside = (cols >= slot * cap) & (cols < slot * cap + counts[source, own])
            target = jnp.where(inside, cols - slot * cap + begin, target)
        out[...] = one_hot(rows == target)


def tables(plan, docs, counts):
    shapes = [
        jax.ShapeDtypeStruct((plan.seq, plan.seq), jnp.float32),
        jax.ShapeDtypeStruct((plan.groups * plan.cap, plan.seq), jnp.bfloat16),
    ] + [jax.ShapeDtypeStruct((plan.seq, plan.rows), jnp.bfloat16)] * plan.parts
    bias, send, *places = pl.pallas_call(
        functools.partial(tables_kernel, plan),
        out_shape=shapes,
        in_specs=[SMEM] * 2,
        out_specs=[VMEM] * len(shapes),
        compiler_params=PARAMS,
        cost_estimate=COST,
        name="tables",
    )(docs, counts)
    return bias, send, places


def softmax(score, bias):
    score = score * (log2_e / HEAD_DIM**0.5) + bias
    weight = jnp.exp2(score - jnp.max(score, axis=0, keepdims=True))
    return weight.astype(jnp.bfloat16), 1.0 / jnp.sum(weight, axis=0, keepdims=True)


def head_columns(plan):
    return [slice(c, c + HEAD_DIM) for c in range(0, plan.block, HEAD_DIM)]


def all_weights(plan, q_ref, k_ref, bias):
    scores = [
        lax.dot_general(
            k_ref[:, cols], q_ref[:, cols], (((1,), (1,)), ((), ())), preferred_element_type=jnp.float32
        )
        for cols in head_columns(plan)
    ]
    return [softmax(score, bias[...]) for score in scores]


def weighted(v_ref, cols, weight, inverse):
    accum = lax.dot_general(
        v_ref[:, cols], weight, (((0,), (0,)), ((), ())), preferred_element_type=jnp.float32
    )
    return (accum * inverse).astype(jnp.bfloat16)


def pick_rows(plan, send, attn, outs):
    picked = lax.dot_general(
        send[...], attn[...], (((1,), (1,)), ((), ())), preferred_element_type=jnp.float32
    )
    for part, out in enumerate(outs):
        out[...] = picked[part * plan.rows : (part + 1) * plan.rows].astype(jnp.bfloat16)


def heads_kernel(plan, q_ref, k_ref, v_ref, bias, _, attn):
    weights = all_weights(plan, q_ref, k_ref, bias)
    for cols, (weight, inverse) in zip(head_columns(plan), weights, strict=True):
        attn[cols, :] = weighted(v_ref, cols, weight, inverse)


def heads(plan, query, k, v, bias, after):
    return pl.pallas_call(
        functools.partial(heads_kernel, plan),
        out_shape=jax.ShapeDtypeStruct((plan.block, plan.seq), jnp.bfloat16),
        in_specs=[VMEM] * 4 + [ANY],
        out_specs=VMEM,
        compiler_params=PARAMS,
        cost_estimate=COST,
        name="heads",
    )(query, k, v, bias, after)


def attend_kernel(plan, bases, q_ref, k_ref, v_ref, bias, send, *refs):
    outs, attn = refs[-1 - plan.parts : -1], refs[-1]
    for i, base in enumerate(refs[:bases]):
        attn[i * plan.block : (i + 1) * plan.block, :] = base[...]
    weights = all_weights(plan, q_ref, k_ref, bias)
    for cols, (weight, inverse) in zip(head_columns(plan), weights, strict=True):
        rows = slice(bases * plan.block + cols.start, bases * plan.block + cols.stop)
        attn[rows, :] = weighted(v_ref, cols, weight, inverse)
    pick_rows(plan, send, attn, outs)


def attend(plan, query, k, v, bias, send, bases=(), after=()):
    width = (len(bases) + 1) * plan.block
    return pl.pallas_call(
        functools.partial(attend_kernel, plan, len(bases)),
        out_shape=[jax.ShapeDtypeStruct((plan.rows, width), jnp.bfloat16)] * plan.parts,
        in_specs=[VMEM] * (5 + len(bases)) + [ANY] * len(after),
        out_specs=[VMEM] * plan.parts,
        scratch_shapes=[pltpu.VMEM((width, plan.seq), jnp.bfloat16)],
        compiler_params=PARAMS,
        cost_estimate=COST,
        name="attend",
    )(query, k, v, bias, send, *bases, *after)


def weigh_kernel(plan, q_ref, k_ref, bias, *refs):
    weights, inverses = refs[-2:]
    found = all_weights(plan, q_ref, k_ref, bias)
    for h, (cols, (weight, inverse)) in enumerate(zip(head_columns(plan), found, strict=True)):
        weights[cols, :] = weight
        inverses[h : h + 1, :] = inverse


def weigh(plan, query, k, bias, after=()):
    count = plan.block // HEAD_DIM
    return pl.pallas_call(
        functools.partial(weigh_kernel, plan),
        out_shape=[
            jax.ShapeDtypeStruct((plan.block, plan.seq), jnp.bfloat16),
            jax.ShapeDtypeStruct((count, plan.seq), jnp.float32),
        ],
        in_specs=[VMEM] * 3 + [ANY] * len(after),
        out_specs=[VMEM] * 2,
        compiler_params=PARAMS,
        cost_estimate=COST,
        name="weigh",
    )(query, k, bias, *after)


def finish_kernel(plan, weights, inverses, v_ref, send, *refs):
    outs, attn = refs[-1 - plan.parts : -1], refs[-1]
    for h, cols in enumerate(head_columns(plan)):
        attn[cols, :] = weighted(v_ref, cols, weights[cols, :], inverses[h : h + 1, :])
    pick_rows(plan, send, attn, outs)


def finish(plan, weights, inverses, v, send, after=()):
    return pl.pallas_call(
        functools.partial(finish_kernel, plan),
        out_shape=[jax.ShapeDtypeStruct((plan.rows, plan.block), jnp.bfloat16)] * plan.parts,
        in_specs=[VMEM] * 4 + [ANY] * len(after),
        out_specs=[VMEM] * plan.parts,
        scratch_shapes=[pltpu.VMEM((plan.block, plan.seq), jnp.bfloat16)],
        compiler_params=PARAMS,
        cost_estimate=COST,
        name="finish",
    )(weights, inverses, v, send, *after)


def squares_of(ref):
    total = None
    for c in range(0, ref.shape[1], HEAD_DIM):
        wide = ref[:, c : c + HEAD_DIM].astype(jnp.float32)
        total = wide * wide if total is None else total + wide * wide
    return total


def place_kernel(plan, widths, summed, extra, sums, *refs):
    parts = plan.parts
    got, matrices, refs = refs[:parts], refs[parts : 2 * parts], refs[2 * parts :]
    blocks, earlier = refs[:extra], refs[extra : extra + sums]
    outs = refs[extra + sums :]
    totals = [squares_of(ref) for ref in blocks] + [ref[...] for ref in earlier]
    base = 0
    for n, (width, out) in enumerate(zip(widths, outs, strict=False)):
        placed = None
        for matrix, ref in zip(matrices, got, strict=True):
            more = jnp.dot(
                matrix[...], ref[:, base : base + width], preferred_element_type=jnp.float32
            )
            placed = more if placed is None else placed + more
        out[...] = placed.astype(jnp.bfloat16)
        if n < summed:
            for c in range(0, width, HEAD_DIM):
                totals.append(placed[:, c : c + HEAD_DIM] * placed[:, c : c + HEAD_DIM])
        base += width
    if summed:
        total = totals[0]
        for more in totals[1:]:
            total = total + more
        outs[-1][...] = total


def place(plan, got, matrices, widths, summed=1, blocks=(), sums=()):
    shapes = [jax.ShapeDtypeStruct((plan.seq, width), jnp.bfloat16) for width in widths]
    if summed:
        shapes.append(jax.ShapeDtypeStruct((plan.seq, HEAD_DIM), jnp.float32))
    args = (*got, *matrices, *blocks, *sums)
    return pl.pallas_call(
        functools.partial(place_kernel, plan, widths, summed, len(blocks), len(sums)),
        out_shape=shapes,
        in_specs=[VMEM] * len(args),
        out_specs=[VMEM] * len(shapes),
        compiler_params=PARAMS,
        cost_estimate=COST,
        name="place",
    )(*args)


def norm_kernel(plan, spots, sums, *refs):
    count = len(spots)
    pieces, refs = refs[:count], refs[count:]
    squares, (gain, out, held, sems) = refs[:sums], refs[sums:]
    width = HEADS * HEAD_DIM
    lanes = squares[0][...]
    for ref in squares[1:]:
        lanes = lanes + ref[...]
    mean = jnp.sum(lanes, axis=1, keepdims=True) / width
    factor = jnp.broadcast_to(lax.rsqrt(mean + norm_eps), lanes.shape)
    device = lax.axis_index("pipe")
    copies = []
    for i, ((t, offset), ref) in enumerate(zip(spots, pieces, strict=True)):
        begin = pick(device, plan.behind[t]) * plan.block + offset
        size = ref.shape[1]
        for c in range(0, size, HEAD_DIM):
            at = pl.ds(pl.multiple_of(begin + c, HEAD_DIM), HEAD_DIM)
            wide = ref[:, c : c + HEAD_DIM].astype(jnp.float32)
            spot = slice(t * plan.block + offset + c, t * plan.block + offset + c + HEAD_DIM)
            held[:, spot] = (wide * factor * gain[:, at]).astype(jnp.bfloat16)
        spot = pl.ds(t * plan.block + offset, size)
        at = pl.ds(pl.multiple_of(begin, HEAD_DIM), size)
        copies.append(pltpu.make_async_copy(held.at[:, spot], out.at[:, at], sems.at[i]))
        copies[-1].start()
    for copy in copies:
        copy.wait()


def norm(plan, pieces, squares, gain):
    arrays, spots = [piece[0] for piece in pieces], tuple(piece[1:] for piece in pieces)
    return pl.pallas_call(
        functools.partial(norm_kernel, plan, spots, len(squares)),
        out_shape=jax.ShapeDtypeStruct((plan.seq, plan.pipe * plan.block), jnp.bfloat16),
        in_specs=[VMEM] * (len(arrays) + len(squares) + 1),
        out_specs=ANY,
        scratch_shapes=[
            pltpu.VMEM((plan.seq, plan.pipe * plan.block), jnp.bfloat16),
            pltpu.SemaphoreType.DMA((len(arrays),)),
        ],
        compiler_params=PARAMS,
        cost_estimate=COST,
        name="norm",
    )(*arrays, *squares, gain)


def body(mesh, queries, cache_keys, cache_values, doc_lengths, row_counts, out_gain):
    query = queries[0]
    seq, local_width = query.shape
    plan = Plan(mesh, seq, local_width)
    n, block, half = plan.pipe, plan.block, plan.block // 2
    forward, backward = plan.ring, [(b, a) for a, b in plan.ring]
    keys, values = cache_keys.reshape(seq, block), cache_values.reshape(seq, block)
    gain = out_gain.astype(jnp.float32).reshape(1, local_width)

    begin = pick(lax.axis_index("pipe"), plan.behind[n - 1]) * block
    ahead = lax.dynamic_slice_in_dim(query, begin, block, 1)
    asked = split(plan, query)
    bias, send, places = tables(plan, doc_lengths, row_counts)
    k, v = lax.ppermute(keys, "pipe", forward), lax.ppermute(values, "pipe", forward)
    lent = lax.ppermute(ahead, "pipe", forward)
    own = heads(plan, asked[0], keys, values, bias, after=bias)
    arrived = plan.regroup(attend(plan, lent, keys, values, bias, send, bases=(own,)))
    mine, borrowed, total = place(plan, arrived, places, (block, block), summed=1)
    pieces = [(mine, 0, 0)]
    for t in range(1, n - 2):
        sent = attend(plan, asked[t], k, v, bias, send, after=arrived[1:2] or arrived)
        got = plan.regroup(sent)
        placed, total = place(plan, got, places, (block,), sums=(total,))
        pieces.append((placed, t, 0))
        if t == 1:
            pass
        k, v = lax.ppermute(k, "pipe", forward), lax.ppermute(v, "pipe", forward)
    weights = weigh(plan, asked[n - 2], k, bias, after=(borrowed,))
    if plan.tensor == 2:
        met = lax.ppermute(weights[1], "tensor", [(0, 1), (1, 0)])
    else:
        met = weights[1]
    borrowed, *_ = lax.optimization_barrier((borrowed, met, *got))
    returned = lax.ppermute(borrowed, "pipe", backward)
    got = plan.regroup(finish(plan, *weights, v, send, after=(met,)))
    placed, total = place(plan, got, places, (block,), blocks=(returned,), sums=(total,))
    pieces += [(placed, n - 2, 0), (returned, n - 1, 0)]
    if plan.tensor == 2:
        sums = (total, lax.ppermute(total, "tensor", [(0, 1), (1, 0)]))
    else:
        sums = (lax.psum(total, "tensor"),)
    return norm(plan, pieces, sums, gain)[None]


def solution(mesh):
    return jax.shard_map(
        functools.partial(body, mesh),
        mesh=mesh,
        in_specs=(
            P("pipe", "dp", "tensor"),
            P("dp", "tensor", "pipe", None),
            P("dp", "tensor", "pipe", None),
            P("dp", None),
            P(),
            P("tensor"),
        ),
        out_specs=P("pipe", "dp", "tensor"),
        check_vma=False,
    )
```

```python
import functools

import jax
import jax.numpy as jnp
from jax import lax
from jax.experimental import pallas as pl
from jax.experimental.pallas import tpu as pltpu
from jax.sharding import PartitionSpec as P

HEADS = 64
HEAD_DIM = 128

masked_fill = -1e30
norm_eps = 1e-06
log2_e = 1.4426950408889634

VMEM = pl.BlockSpec(memory_space=pltpu.VMEM)
SMEM = pl.BlockSpec(memory_space=pltpu.SMEM)
ANY = pl.BlockSpec(memory_space=pl.ANY)
COST = pl.CostEstimate(flops=1, bytes_accessed=1, transcendentals=0)
PARAMS = pltpu.CompilerParams(vmem_limit_bytes=32 * 1024 * 1024)


def iota(shape, dim):
    return lax.broadcasted_iota(jnp.int32, shape, dim)


def pick(index, table):
    value = jnp.int32(table[0])
    for i, entry in enumerate(table[1:], 1):
        value = jnp.where(index == i, jnp.int32(entry), value)
    return value


def one_hot(condition):
    return condition.astype(jnp.float32).astype(jnp.bfloat16)


class Plan:
    def __init__(self, mesh, seq, local_width):
        self.pipe, self.groups, self.tensor = (mesh.shape[a] for a in ("pipe", "dp", "tensor"))
        self.seq, self.block = seq, local_width // self.pipe
        self.cap = 5 * seq // (4 * self.groups)
        self.pairwise = self.groups == 4 and self.cap % 8 == 0
        self.parts = self.groups if self.pairwise else 1
        self.rows = self.groups * self.cap // self.parts
        self.steps = [0, 3, 1, 2] if self.pairwise else list(range(self.groups))
        n = self.pipe
        order = [0] + list(range(1, n, 2)) + [i for i in reversed(range(2, n)) if i % 2 == 0]
        self.ring = [(order[i], order[(i + 1) % n]) for i in range(n)]
        where = {d: i for i, d in enumerate(order)}
        self.behind = [[order[(where[p] - t) % n] for p in range(n)] for t in range(n)]

    def partner(self, own, i):
        step = jnp.int32(self.steps[i])
        return jnp.bitwise_xor(own, step) if self.pairwise else step

    def regroup(self, parts):
        if not self.pairwise:
            return [lax.all_to_all(parts[0], "dp", split_axis=0, concat_axis=0, tiled=True)]
        got = [parts[0]]
        for step, part in zip(self.steps[1:], parts[1:], strict=True):
            got.append(lax.ppermute(part, "dp", [(g, g ^ step) for g in range(self.groups)]))
        return got


def split_kernel(plan, query, *refs):
    outs, sems = refs[:-1], refs[-1]
    place = lax.axis_index("pipe")
    copies = []
    for t, out in enumerate(outs):
        begin = pl.multiple_of(pick(place, plan.behind[t]) * plan.block, plan.block)
        copies.append(
            pltpu.make_async_copy(query.at[:, pl.ds(begin, plan.block)], out, sems.at[t])
        )
        copies[-1].start()
    for copy in copies:
        copy.wait()


def split(plan, query):
    shape = jax.ShapeDtypeStruct((plan.seq, plan.block), query.dtype)
    return pl.pallas_call(
        functools.partial(split_kernel, plan),
        out_shape=[shape] * (plan.pipe - 1),
        in_specs=[ANY],
        out_specs=[VMEM] * (plan.pipe - 1),
        scratch_shapes=[pltpu.SemaphoreType.DMA((plan.pipe - 1,))],
        compiler_params=PARAMS,
        cost_estimate=COST,
        name="split",
    )(query)


def tables_kernel(plan, docs, counts, bias, send, *places):
    seq, cap, groups = plan.seq, plan.cap, plan.groups
    own = lax.axis_index("dp")
    rows, cols = iota((seq, seq), 0), iota((seq, seq), 1)
    row_doc = jnp.zeros((seq, seq), jnp.int32)
    col_doc = jnp.zeros((seq, seq), jnp.int32)
    end = jnp.int32(0)
    for k in range(docs.shape[1]):
        end = end + docs[0, k]
        row_doc = row_doc + (rows >= end).astype(jnp.int32)
        col_doc = col_doc + (cols >= end).astype(jnp.int32)
    bias[...] = jnp.where((row_doc == col_doc) & (rows <= cols), 0.0, masked_fill)
    rows, cols = iota((groups * cap, seq), 0), iota((groups * cap, seq), 1)
    target = jnp.full((groups * cap, seq), -1, jnp.int32)
    for i in range(groups):
        to = plan.partner(own, i)
        begin = jnp.int32(0)
        for j in range(groups):
            begin = begin + jnp.where(j < to, counts[own, j], 0)
        inside = (rows >= i * cap) & (rows < i * cap + counts[own, to])
        target = jnp.where(inside, rows - i * cap + begin, target)
    send[...] = one_hot(cols == target)
    per = groups // plan.parts
    for part, out in enumerate(places):
        rows, cols = iota(out.shape, 0), iota(out.shape, 1)
        target = jnp.full(out.shape, -1, jnp.int32)
        for slot in range(per):
            source = plan.partner(own, part * per + slot)
            begin = jnp.int32(0)
            for j in range(groups):
                begin = begin + jnp.where(j < source, counts[j, own], 0)
            inside = (cols >= slot * cap) & (cols < slot * cap + counts[source, own])
            target = jnp.where(inside, cols - slot * cap + begin, target)
        out[...] = one_hot(rows == target)


def tables(plan, docs, counts):
    shapes = [
        jax.ShapeDtypeStruct((plan.seq, plan.seq), jnp.float32),
        jax.ShapeDtypeStruct((plan.groups * plan.cap, plan.seq), jnp.bfloat16),
    ] + [jax.ShapeDtypeStruct((plan.seq, plan.rows), jnp.bfloat16)] * plan.parts
    bias, send, *places = pl.pallas_call(
        functools.partial(tables_kernel, plan),
        out_shape=shapes,
        in_specs=[SMEM] * 2,
        out_specs=[VMEM] * len(shapes),
        compiler_params=PARAMS,
        cost_estimate=COST,
        name="tables",
    )(docs, counts)
    return bias, send, places


def softmax(score, bias):
    score = score * (log2_e / HEAD_DIM**0.5) + bias
    weight = jnp.exp2(score - jnp.max(score, axis=0, keepdims=True))
    return weight.astype(jnp.bfloat16), 1.0 / jnp.sum(weight, axis=0, keepdims=True)


def head_columns(plan):
    return [slice(c, c + HEAD_DIM) for c in range(0, plan.block, HEAD_DIM)]


def all_weights(plan, q_ref, k_ref, bias):
    scores = [
        lax.dot_general(
            k_ref[:, cols], q_ref[:, cols], (((1,), (1,)), ((), ())), preferred_element_type=jnp.float32
        )
        for cols in head_columns(plan)
    ]
    return [softmax(score, bias[...]) for score in scores]


def weighted(v_ref, cols, weight, inverse):
    accum = lax.dot_general(
        v_ref[:, cols], weight, (((0,), (0,)), ((), ())), preferred_element_type=jnp.float32
    )
    return (accum * inverse).astype(jnp.bfloat16)


def pick_rows(plan, send, attn, outs):
    picked = lax.dot_general(
        send[...], attn[...], (((1,), (1,)), ((), ())), preferred_element_type=jnp.float32
    )
    for part, out in enumerate(outs):
        out[...] = picked[part * plan.rows : (part + 1) * plan.rows].astype(jnp.bfloat16)


def heads_kernel(plan, q_ref, k_ref, v_ref, bias, attn):
    weights = all_weights(plan, q_ref, k_ref, bias)
    for cols, (weight, inverse) in zip(head_columns(plan), weights, strict=True):
        attn[cols, :] = weighted(v_ref, cols, weight, inverse)


def heads(plan, query, k, v, bias):
    return pl.pallas_call(
        functools.partial(heads_kernel, plan),
        out_shape=jax.ShapeDtypeStruct((plan.block, plan.seq), jnp.bfloat16),
        in_specs=[VMEM] * 4,
        out_specs=VMEM,
        compiler_params=PARAMS,
        cost_estimate=COST,
        name="heads",
    )(query, k, v, bias)


def attend_kernel(plan, bases, q_ref, k_ref, v_ref, bias, send, *refs):
    outs, attn = refs[-1 - plan.parts : -1], refs[-1]
    for i, base in enumerate(refs[:bases]):
        attn[i * plan.block : (i + 1) * plan.block, :] = base[...]
    weights = all_weights(plan, q_ref, k_ref, bias)
    for cols, (weight, inverse) in zip(head_columns(plan), weights, strict=True):
        rows = slice(bases * plan.block + cols.start, bases * plan.block + cols.stop)
        attn[rows, :] = weighted(v_ref, cols, weight, inverse)
    pick_rows(plan, send, attn, outs)


def attend(plan, query, k, v, bias, send, bases=()):
    width = (len(bases) + 1) * plan.block
    return pl.pallas_call(
        functools.partial(attend_kernel, plan, len(bases)),
        out_shape=[jax.ShapeDtypeStruct((plan.rows, width), jnp.bfloat16)] * plan.parts,
        in_specs=[VMEM] * (5 + len(bases)),
        out_specs=[VMEM] * plan.parts,
        scratch_shapes=[pltpu.VMEM((width, plan.seq), jnp.bfloat16)],
        compiler_params=PARAMS,
        cost_estimate=COST,
        name="attend",
    )(query, k, v, bias, send, *bases)


def weigh_kernel(plan, q_ref, k_ref, bias, _, weights, inverses):
    found = all_weights(plan, q_ref, k_ref, bias)
    for h, (cols, (weight, inverse)) in enumerate(zip(head_columns(plan), found, strict=True)):
        weights[cols, :] = weight
        inverses[h : h + 1, :] = inverse


def weigh(plan, query, k, bias, after):
    count = plan.block // HEAD_DIM
    return pl.pallas_call(
        functools.partial(weigh_kernel, plan),
        out_shape=[
            jax.ShapeDtypeStruct((plan.block, plan.seq), jnp.bfloat16),
            jax.ShapeDtypeStruct((count, plan.seq), jnp.float32),
        ],
        in_specs=[VMEM] * 3 + [ANY],
        out_specs=[VMEM] * 2,
        compiler_params=PARAMS,
        cost_estimate=COST,
        name="weigh",
    )(query, k, bias, after)


def finish_kernel(plan, weights, inverses, v_ref, send, _, *refs):
    outs, attn = refs[:-1], refs[-1]
    for h, cols in enumerate(head_columns(plan)):
        attn[cols, :] = weighted(v_ref, cols, weights[cols, :], inverses[h : h + 1, :])
    pick_rows(plan, send, attn, outs)


def finish(plan, weights, inverses, v, send, after):
    return pl.pallas_call(
        functools.partial(finish_kernel, plan),
        out_shape=[jax.ShapeDtypeStruct((plan.rows, plan.block), jnp.bfloat16)] * plan.parts,
        in_specs=[VMEM] * 4 + [ANY],
        out_specs=[VMEM] * plan.parts,
        scratch_shapes=[pltpu.VMEM((plan.block, plan.seq), jnp.bfloat16)],
        compiler_params=PARAMS,
        cost_estimate=COST,
        name="finish",
    )(weights, inverses, v, send, after)


def squares_of(ref):
    total = None
    for c in range(0, ref.shape[1], HEAD_DIM):
        wide = ref[:, c : c + HEAD_DIM].astype(jnp.float32)
        total = wide * wide if total is None else total + wide * wide
    return total


def place_kernel(plan, widths, summed, extra, sums, *refs):
    parts = plan.parts
    got, matrices, refs = refs[:parts], refs[parts : 2 * parts], refs[2 * parts :]
    blocks, earlier = refs[:extra], refs[extra : extra + sums]
    outs = refs[extra + sums :]
    totals = [squares_of(ref) for ref in blocks] + [ref[...] for ref in earlier]
    base = 0
    for n, (width, out) in enumerate(zip(widths, outs, strict=False)):
        placed = None
        for matrix, ref in zip(matrices, got, strict=True):
            more = jnp.dot(
                matrix[...], ref[:, base : base + width], preferred_element_type=jnp.float32
            )
            placed = more if placed is None else placed + more
        out[...] = placed.astype(jnp.bfloat16)
        if n < summed:
            for c in range(0, width, HEAD_DIM):
                totals.append(placed[:, c : c + HEAD_DIM] * placed[:, c : c + HEAD_DIM])
        base += width
    if summed:
        total = totals[0]
        for more in totals[1:]:
            total = total + more
        outs[-1][...] = total


def place(plan, got, matrices, widths, summed=1, blocks=(), sums=()):
    shapes = [jax.ShapeDtypeStruct((plan.seq, width), jnp.bfloat16) for width in widths]
    if summed:
        shapes.append(jax.ShapeDtypeStruct((plan.seq, HEAD_DIM), jnp.float32))
    args = (*got, *matrices, *blocks, *sums)
    return pl.pallas_call(
        functools.partial(place_kernel, plan, widths, summed, len(blocks), len(sums)),
        out_shape=shapes,
        in_specs=[VMEM] * len(args),
        out_specs=[VMEM] * len(shapes),
        compiler_params=PARAMS,
        cost_estimate=COST,
        name="place",
    )(*args)


def norm_kernel(plan, spots, sums, *refs):
    count = len(spots)
    pieces, refs = refs[:count], refs[count:]
    squares, (gain, out, held, sems) = refs[:sums], refs[sums:]
    width = HEADS * HEAD_DIM
    lanes = squares[0][...]
    for ref in squares[1:]:
        lanes = lanes + ref[...]
    mean = jnp.sum(lanes, axis=1, keepdims=True) / width
    factor = jnp.broadcast_to(lax.rsqrt(mean + norm_eps), lanes.shape)
    device = lax.axis_index("pipe")
    copies = []
    for i, ((t, offset), ref) in enumerate(zip(spots, pieces, strict=True)):
        begin = pick(device, plan.behind[t]) * plan.block + offset
        size = ref.shape[1]
        for c in range(0, size, HEAD_DIM):
            at = pl.ds(pl.multiple_of(begin + c, HEAD_DIM), HEAD_DIM)
            wide = ref[:, c : c + HEAD_DIM].astype(jnp.float32)
            spot = slice(t * plan.block + offset + c, t * plan.block + offset + c + HEAD_DIM)
            held[:, spot] = (wide * factor * gain[:, at]).astype(jnp.bfloat16)
        spot = pl.ds(t * plan.block + offset, size)
        at = pl.ds(pl.multiple_of(begin, HEAD_DIM), size)
        copies.append(pltpu.make_async_copy(held.at[:, spot], out.at[:, at], sems.at[i]))
        copies[-1].start()
    for copy in copies:
        copy.wait()


def norm(plan, pieces, squares, gain):
    arrays, spots = [piece[0] for piece in pieces], tuple(piece[1:] for piece in pieces)
    return pl.pallas_call(
        functools.partial(norm_kernel, plan, spots, len(squares)),
        out_shape=jax.ShapeDtypeStruct((plan.seq, plan.pipe * plan.block), jnp.bfloat16),
        in_specs=[VMEM] * (len(arrays) + len(squares) + 1),
        out_specs=ANY,
        scratch_shapes=[
            pltpu.VMEM((plan.seq, plan.pipe * plan.block), jnp.bfloat16),
            pltpu.SemaphoreType.DMA((len(arrays),)),
        ],
        compiler_params=PARAMS,
        cost_estimate=COST,
        name="norm",
    )(*arrays, *squares, gain)


def body(mesh, queries, cache_keys, cache_values, doc_lengths, row_counts, out_gain):
    query = queries[0]
    seq, local_width = query.shape
    plan = Plan(mesh, seq, local_width)
    n, block = plan.pipe, plan.block
    forward, backward = plan.ring, [(b, a) for a, b in plan.ring]
    keys, values = cache_keys.reshape(seq, block), cache_values.reshape(seq, block)
    gain = out_gain.astype(jnp.float32).reshape(1, local_width)

    begin = pick(lax.axis_index("pipe"), plan.behind[n - 1]) * block
    ahead = lax.dynamic_slice_in_dim(query, begin, block, 1)
    asked = split(plan, query)
    bias, send, places = tables(plan, doc_lengths, row_counts)
    k, v = lax.ppermute(keys, "pipe", forward), lax.ppermute(values, "pipe", forward)
    lent = lax.ppermute(ahead, "pipe", forward)
    own = heads(plan, asked[0], keys, values, bias)
    arrived = plan.regroup(attend(plan, lent, keys, values, bias, send, bases=(own,)))
    mine, borrowed, total = place(plan, arrived, places, (block, block), summed=1)
    pieces = [(mine, 0, 0)]
    for t in range(1, n - 2):
        sent = attend(plan, asked[t], k, v, bias, send)
        *sent, _ = lax.optimization_barrier((*sent, arrived[1 % len(arrived)]))
        got = plan.regroup(sent)
        placed, total = place(plan, got, places, (block,), sums=(total,))
        pieces.append((placed, t, 0))
        k, v = lax.ppermute(k, "pipe", forward), lax.ppermute(v, "pipe", forward)
    weights, inverses = weigh(plan, asked[n - 2], k, bias, borrowed)
    met = inverses
    if plan.tensor == 2:
        met = lax.ppermute(inverses, "tensor", [(0, 1), (1, 0)])
    borrowed, *_ = lax.optimization_barrier((borrowed, met, *got))
    returned = lax.ppermute(borrowed, "pipe", backward)
    got = plan.regroup(finish(plan, weights, inverses, v, send, met))
    placed, total = place(plan, got, places, (block,), blocks=(returned,), sums=(total,))
    pieces += [(placed, n - 2, 0), (returned, n - 1, 0)]
    if plan.tensor == 2:
        sums = (total, lax.ppermute(total, "tensor", [(0, 1), (1, 0)]))
    else:
        sums = (lax.psum(total, "tensor"),)
    return norm(plan, pieces, sums, gain)[None]


def solution(mesh):
    return jax.shard_map(
        functools.partial(body, mesh),
        mesh=mesh,
        in_specs=(
            P("pipe", "dp", "tensor"),
            P("dp", "tensor", "pipe", None),
            P("dp", "tensor", "pipe", None),
            P("dp", None),
            P(),
            P("tensor"),
        ),
        out_specs=P("pipe", "dp", "tensor"),
        check_vma=False,
    )
```

```python
import functools

import jax
import jax.numpy as jnp
from jax import lax
from jax.experimental import pallas as pl
from jax.experimental.pallas import tpu as pltpu
from jax.sharding import PartitionSpec as P

HEADS = 64
HEAD_DIM = 128

masked_fill = -1e30
norm_eps = 1e-06
log2_e = 1.4426950408889634

VMEM = pl.BlockSpec(memory_space=pltpu.VMEM)
SMEM = pl.BlockSpec(memory_space=pltpu.SMEM)
ANY = pl.BlockSpec(memory_space=pl.ANY)
COST = pl.CostEstimate(flops=1, bytes_accessed=1, transcendentals=0)
PARAMS = pltpu.CompilerParams(vmem_limit_bytes=32 * 1024 * 1024)


def iota(shape, dim):
    return lax.broadcasted_iota(jnp.int32, shape, dim)


def pick(index, table):
    value = jnp.int32(table[0])
    for i, entry in enumerate(table[1:], 1):
        value = jnp.where(index == i, jnp.int32(entry), value)
    return value


def one_hot(condition):
    return condition.astype(jnp.float32).astype(jnp.bfloat16)


class Plan:
    def __init__(self, mesh, seq, local_width):
        self.pipe, self.groups, self.tensor = (mesh.shape[a] for a in ("pipe", "dp", "tensor"))
        self.seq, self.block = seq, local_width // self.pipe
        self.cap = 5 * seq // (4 * self.groups)
        self.pairwise = self.groups == 4 and self.cap % 8 == 0
        self.parts = self.groups if self.pairwise else 1
        self.rows = self.groups * self.cap // self.parts
        self.steps = [0, 3, 1, 2] if self.pairwise else list(range(self.groups))
        n = self.pipe
        order = [0] + list(range(1, n, 2)) + [i for i in reversed(range(2, n)) if i % 2 == 0]
        self.ring = [(order[i], order[(i + 1) % n]) for i in range(n)]
        where = {d: i for i, d in enumerate(order)}
        self.behind = [[order[(where[p] - t) % n] for p in range(n)] for t in range(n)]

    def partner(self, own, i):
        step = jnp.int32(self.steps[i])
        return jnp.bitwise_xor(own, step) if self.pairwise else step

    def regroup(self, parts):
        if not self.pairwise:
            return [lax.all_to_all(parts[0], "dp", split_axis=0, concat_axis=0, tiled=True)]
        got = [parts[0]]
        for step, part in zip(self.steps[1:], parts[1:], strict=True):
            got.append(lax.ppermute(part, "dp", [(g, g ^ step) for g in range(self.groups)]))
        return got


def split_kernel(plan, query, *refs):
    outs, sems = refs[:-1], refs[-1]
    place = lax.axis_index("pipe")
    copies = []
    for t, out in enumerate(outs):
        begin = pl.multiple_of(pick(place, plan.behind[t]) * plan.block, plan.block)
        copies.append(
            pltpu.make_async_copy(query.at[:, pl.ds(begin, plan.block)], out, sems.at[t])
        )
        copies[-1].start()
    for copy in copies:
        copy.wait()


def split(plan, query):
    shape = jax.ShapeDtypeStruct((plan.seq, plan.block), query.dtype)
    return pl.pallas_call(
        functools.partial(split_kernel, plan),
        out_shape=[shape] * (plan.pipe - 1),
        in_specs=[ANY],
        out_specs=[VMEM] * (plan.pipe - 1),
        scratch_shapes=[pltpu.SemaphoreType.DMA((plan.pipe - 1,))],
        compiler_params=PARAMS,
        cost_estimate=COST,
        name="split",
    )(query)


def tables_kernel(plan, docs, counts, bias, send, *places):
    seq, cap, groups = plan.seq, plan.cap, plan.groups
    own = lax.axis_index("dp")
    rows, cols = iota((seq, seq), 0), iota((seq, seq), 1)
    row_doc = jnp.zeros((seq, seq), jnp.int32)
    col_doc = jnp.zeros((seq, seq), jnp.int32)
    end = jnp.int32(0)
    for k in range(docs.shape[1]):
        end = end + docs[0, k]
        row_doc = row_doc + (rows >= end).astype(jnp.int32)
        col_doc = col_doc + (cols >= end).astype(jnp.int32)
    bias[...] = jnp.where((row_doc == col_doc) & (rows <= cols), 0.0, masked_fill)
    rows, cols = iota((groups * cap, seq), 0), iota((groups * cap, seq), 1)
    target = jnp.full((groups * cap, seq), -1, jnp.int32)
    for i in range(groups):
        to = plan.partner(own, i)
        begin = jnp.int32(0)
        for j in range(groups):
            begin = begin + jnp.where(j < to, counts[own, j], 0)
        inside = (rows >= i * cap) & (rows < i * cap + counts[own, to])
        target = jnp.where(inside, rows - i * cap + begin, target)
    send[...] = one_hot(cols == target)
    per = groups // plan.parts
    for part, out in enumerate(places):
        rows, cols = iota(out.shape, 0), iota(out.shape, 1)
        target = jnp.full(out.shape, -1, jnp.int32)
        for slot in range(per):
            source = plan.partner(own, part * per + slot)
            begin = jnp.int32(0)
            for j in range(groups):
                begin = begin + jnp.where(j < source, counts[j, own], 0)
            inside = (cols >= slot * cap) & (cols < slot * cap + counts[source, own])
            target = jnp.where(inside, cols - slot * cap + begin, target)
        out[...] = one_hot(rows == target)


def tables(plan, docs, counts):
    shapes = [
        jax.ShapeDtypeStruct((plan.seq, plan.seq), jnp.float32),
        jax.ShapeDtypeStruct((plan.groups * plan.cap, plan.seq), jnp.bfloat16),
    ] + [jax.ShapeDtypeStruct((plan.seq, plan.rows), jnp.bfloat16)] * plan.parts
    bias, send, *places = pl.pallas_call(
        functools.partial(tables_kernel, plan),
        out_shape=shapes,
        in_specs=[SMEM] * 2,
        out_specs=[VMEM] * len(shapes),
        compiler_params=PARAMS,
        cost_estimate=COST,
        name="tables",
    )(docs, counts)
    return bias, send, places


def softmax(score, bias):
    score = score * (log2_e / HEAD_DIM**0.5) + bias
    weight = jnp.exp2(score - jnp.max(score, axis=0, keepdims=True))
    return weight.astype(jnp.bfloat16), 1.0 / jnp.sum(weight, axis=0, keepdims=True)


def head_columns(plan):
    return [slice(c, c + HEAD_DIM) for c in range(0, plan.block, HEAD_DIM)]


def all_weights(plan, q_ref, k_ref, bias):
    scores = [
        lax.dot_general(
            k_ref[:, cols], q_ref[:, cols], (((1,), (1,)), ((), ())), preferred_element_type=jnp.float32
        )
        for cols in head_columns(plan)
    ]
    return [softmax(score, bias[...]) for score in scores]


def weighted(v_ref, cols, weight, inverse):
    accum = lax.dot_general(
        v_ref[:, cols], weight, (((0,), (0,)), ((), ())), preferred_element_type=jnp.float32
    )
    return (accum * inverse).astype(jnp.bfloat16)


def pick_rows(plan, send, attn, outs):
    picked = lax.dot_general(
        send[...], attn[...], (((1,), (1,)), ((), ())), preferred_element_type=jnp.float32
    )
    for part, out in enumerate(outs):
        out[...] = picked[part * plan.rows : (part + 1) * plan.rows].astype(jnp.bfloat16)


def heads_kernel(plan, q_ref, k_ref, v_ref, bias, attn):
    weights = all_weights(plan, q_ref, k_ref, bias)
    for cols, (weight, inverse) in zip(head_columns(plan), weights, strict=True):
        attn[cols, :] = weighted(v_ref, cols, weight, inverse)


def heads(plan, query, k, v, bias):
    return pl.pallas_call(
        functools.partial(heads_kernel, plan),
        out_shape=jax.ShapeDtypeStruct((plan.block, plan.seq), jnp.bfloat16),
        in_specs=[VMEM] * 4,
        out_specs=VMEM,
        compiler_params=PARAMS,
        cost_estimate=COST,
        name="heads",
    )(query, k, v, bias)


def attend_kernel(plan, bases, q_ref, k_ref, v_ref, bias, send, *refs):
    outs, attn = refs[-1 - plan.parts : -1], refs[-1]
    for i, base in enumerate(refs[:bases]):
        attn[i * plan.block : (i + 1) * plan.block, :] = base[...]
    weights = all_weights(plan, q_ref, k_ref, bias)
    for cols, (weight, inverse) in zip(head_columns(plan), weights, strict=True):
        rows = slice(bases * plan.block + cols.start, bases * plan.block + cols.stop)
        attn[rows, :] = weighted(v_ref, cols, weight, inverse)
    pick_rows(plan, send, attn, outs)


def attend(plan, query, k, v, bias, send, bases=()):
    width = (len(bases) + 1) * plan.block
    return pl.pallas_call(
        functools.partial(attend_kernel, plan, len(bases)),
        out_shape=[jax.ShapeDtypeStruct((plan.rows, width), jnp.bfloat16)] * plan.parts,
        in_specs=[VMEM] * (5 + len(bases)),
        out_specs=[VMEM] * plan.parts,
        scratch_shapes=[pltpu.VMEM((width, plan.seq), jnp.bfloat16)],
        compiler_params=PARAMS,
        cost_estimate=COST,
        name="attend",
    )(query, k, v, bias, send, *bases)


def weigh_kernel(plan, q_ref, k_ref, bias, _, weights, spread, inverses):
    found = all_weights(plan, q_ref, k_ref, bias)
    for h, (cols, (weight, inverse)) in enumerate(zip(head_columns(plan), found, strict=True)):
        weights[:, cols] = weight.T
        spread[:, cols] = jnp.broadcast_to(inverse, (HEAD_DIM, plan.seq)).T
        inverses[h : h + 1, :] = inverse


def weigh(plan, query, k, bias, after):
    count = plan.block // HEAD_DIM
    return pl.pallas_call(
        functools.partial(weigh_kernel, plan),
        out_shape=[
            jax.ShapeDtypeStruct((plan.seq, plan.block), jnp.bfloat16),
            jax.ShapeDtypeStruct((plan.seq, plan.block), jnp.float32),
            jax.ShapeDtypeStruct((count, plan.seq), jnp.float32),
        ],
        in_specs=[VMEM] * 3 + [ANY],
        out_specs=[VMEM] * 3,
        compiler_params=PARAMS,
        cost_estimate=COST,
        name="weigh",
    )(query, k, bias, after)


def finish_kernel(plan, weights, spread, v_ref, send, _, *refs):
    outs, attn = refs[:-1], refs[-1]
    for cols in head_columns(plan):
        accum = jnp.dot(weights[:, cols], v_ref[:, cols], preferred_element_type=jnp.float32)
        attn[:, cols] = (accum * spread[:, cols]).astype(jnp.bfloat16)
    picked = jnp.dot(send[...], attn[...], preferred_element_type=jnp.float32)
    for part, out in enumerate(outs):
        out[...] = picked[part * plan.rows : (part + 1) * plan.rows].astype(jnp.bfloat16)


def finish(plan, weights, spread, v, send, after):
    return pl.pallas_call(
        functools.partial(finish_kernel, plan),
        out_shape=[jax.ShapeDtypeStruct((plan.rows, plan.block), jnp.bfloat16)] * plan.parts,
        in_specs=[VMEM] * 4 + [ANY],
        out_specs=[VMEM] * plan.parts,
        scratch_shapes=[pltpu.VMEM((plan.seq, plan.block), jnp.bfloat16)],
        compiler_params=PARAMS,
        cost_estimate=COST,
        name="finish",
    )(weights, spread, v, send, after)


def squares_of(ref):
    total = None
    for c in range(0, ref.shape[1], HEAD_DIM):
        wide = ref[:, c : c + HEAD_DIM].astype(jnp.float32)
        total = wide * wide if total is None else total + wide * wide
    return total


def place_kernel(plan, widths, summed, extra, sums, *refs):
    parts = plan.parts
    got, matrices, refs = refs[:parts], refs[parts : 2 * parts], refs[2 * parts :]
    blocks, earlier = refs[:extra], refs[extra : extra + sums]
    outs = refs[extra + sums :]
    totals = [squares_of(ref) for ref in blocks] + [ref[...] for ref in earlier]
    base = 0
    for n, (width, out) in enumerate(zip(widths, outs, strict=False)):
        placed = None
        for matrix, ref in zip(matrices, got, strict=True):
            more = jnp.dot(
                matrix[...], ref[:, base : base + width], preferred_element_type=jnp.float32
            )
            placed = more if placed is None else placed + more
        out[...] = placed.astype(jnp.bfloat16)
        if n < summed:
            for c in range(0, width, HEAD_DIM):
                totals.append(placed[:, c : c + HEAD_DIM] * placed[:, c : c + HEAD_DIM])
        base += width
    if summed:
        total = totals[0]
        for more in totals[1:]:
            total = total + more
        outs[-1][...] = total


def place(plan, got, matrices, widths, summed=1, blocks=(), sums=()):
    shapes = [jax.ShapeDtypeStruct((plan.seq, width), jnp.bfloat16) for width in widths]
    if summed:
        shapes.append(jax.ShapeDtypeStruct((plan.seq, HEAD_DIM), jnp.float32))
    args = (*got, *matrices, *blocks, *sums)
    return pl.pallas_call(
        functools.partial(place_kernel, plan, widths, summed, len(blocks), len(sums)),
        out_shape=shapes,
        in_specs=[VMEM] * len(args),
        out_specs=[VMEM] * len(shapes),
        compiler_params=PARAMS,
        cost_estimate=COST,
        name="place",
    )(*args)


def norm_kernel(plan, spots, sums, *refs):
    count = len(spots)
    pieces, refs = refs[:count], refs[count:]
    squares, (gain, out, held, sems) = refs[:sums], refs[sums:]
    width = HEADS * HEAD_DIM
    lanes = squares[0][...]
    for ref in squares[1:]:
        lanes = lanes + ref[...]
    mean = jnp.sum(lanes, axis=1, keepdims=True) / width
    factor = jnp.broadcast_to(lax.rsqrt(mean + norm_eps), lanes.shape)
    device = lax.axis_index("pipe")
    copies = []
    for i, ((t, offset), ref) in enumerate(zip(spots, pieces, strict=True)):
        begin = pick(device, plan.behind[t]) * plan.block + offset
        size = ref.shape[1]
        for c in range(0, size, HEAD_DIM):
            at = pl.ds(pl.multiple_of(begin + c, HEAD_DIM), HEAD_DIM)
            wide = ref[:, c : c + HEAD_DIM].astype(jnp.float32)
            spot = slice(t * plan.block + offset + c, t * plan.block + offset + c + HEAD_DIM)
            held[:, spot] = (wide * factor * gain[:, at]).astype(jnp.bfloat16)
        spot = pl.ds(t * plan.block + offset, size)
        at = pl.ds(pl.multiple_of(begin, HEAD_DIM), size)
        copies.append(pltpu.make_async_copy(held.at[:, spot], out.at[:, at], sems.at[i]))
        copies[-1].start()
    for copy in copies:
        copy.wait()


def norm(plan, pieces, squares, gain):
    arrays, spots = [piece[0] for piece in pieces], tuple(piece[1:] for piece in pieces)
    return pl.pallas_call(
        functools.partial(norm_kernel, plan, spots, len(squares)),
        out_shape=jax.ShapeDtypeStruct((plan.seq, plan.pipe * plan.block), jnp.bfloat16),
        in_specs=[VMEM] * (len(arrays) + len(squares) + 1),
        out_specs=ANY,
        scratch_shapes=[
            pltpu.VMEM((plan.seq, plan.pipe * plan.block), jnp.bfloat16),
            pltpu.SemaphoreType.DMA((len(arrays),)),
        ],
        compiler_params=PARAMS,
        cost_estimate=COST,
        name="norm",
    )(*arrays, *squares, gain)


def body(mesh, queries, cache_keys, cache_values, doc_lengths, row_counts, out_gain):
    query = queries[0]
    seq, local_width = query.shape
    plan = Plan(mesh, seq, local_width)
    n, block = plan.pipe, plan.block
    forward, backward = plan.ring, [(b, a) for a, b in plan.ring]
    keys, values = cache_keys.reshape(seq, block), cache_values.reshape(seq, block)
    gain = out_gain.astype(jnp.float32).reshape(1, local_width)

    begin = pick(lax.axis_index("pipe"), plan.behind[n - 1]) * block
    ahead = lax.dynamic_slice_in_dim(query, begin, block, 1)
    asked = split(plan, query)
    bias, send, places = tables(plan, doc_lengths, row_counts)
    k, v = lax.ppermute(keys, "pipe", forward), lax.ppermute(values, "pipe", forward)
    lent = lax.ppermute(ahead, "pipe", forward)
    own = heads(plan, asked[0], keys, values, bias)
    arrived = plan.regroup(attend(plan, lent, keys, values, bias, send, bases=(own,)))
    mine, borrowed, total = place(plan, arrived, places, (block, block), summed=1)
    pieces = [(mine, 0, 0)]
    for t in range(1, n - 2):
        sent = attend(plan, asked[t], k, v, bias, send)
        *sent, _ = lax.optimization_barrier((*sent, arrived[1 % len(arrived)]))
        got = plan.regroup(sent)
        placed, total = place(plan, got, places, (block,), sums=(total,))
        pieces.append((placed, t, 0))
        k, v = lax.ppermute(k, "pipe", forward), lax.ppermute(v, "pipe", forward)
    weights, spread, inverses = weigh(plan, asked[n - 2], k, bias, borrowed)
    met = inverses
    if plan.tensor == 2:
        met = lax.ppermute(inverses, "tensor", [(0, 1), (1, 0)])
    borrowed, *_ = lax.optimization_barrier((borrowed, met, *got))
    returned = lax.ppermute(borrowed, "pipe", backward)
    got = plan.regroup(finish(plan, weights, spread, v, send, met))
    placed, total = place(plan, got, places, (block,), blocks=(returned,), sums=(total,))
    pieces += [(placed, n - 2, 0), (returned, n - 1, 0)]
    if plan.tensor == 2:
        sums = (total, lax.ppermute(total, "tensor", [(0, 1), (1, 0)]))
    else:
        sums = (lax.psum(total, "tensor"),)
    return norm(plan, pieces, sums, gain)[None]


def solution(mesh):
    return jax.shard_map(
        functools.partial(body, mesh),
        mesh=mesh,
        in_specs=(
            P("pipe", "dp", "tensor"),
            P("dp", "tensor", "pipe", None),
            P("dp", "tensor", "pipe", None),
            P("dp", None),
            P(),
            P("tensor"),
        ),
        out_specs=P("pipe", "dp", "tensor"),
        check_vma=False,
    )
```

```python
import functools

import jax
import jax.numpy as jnp
from jax import lax
from jax.experimental import pallas as pl
from jax.experimental.pallas import tpu as pltpu
from jax.sharding import PartitionSpec as P

HEADS = 64
HEAD_DIM = 128

masked_fill = -1e30
norm_eps = 1e-06
log2_e = 1.4426950408889634

VMEM = pl.BlockSpec(memory_space=pltpu.VMEM)
SMEM = pl.BlockSpec(memory_space=pltpu.SMEM)
ANY = pl.BlockSpec(memory_space=pl.ANY)
COST = pl.CostEstimate(flops=1, bytes_accessed=1, transcendentals=0)
PARAMS = pltpu.CompilerParams(vmem_limit_bytes=32 * 1024 * 1024)


def iota(shape, dim):
    return lax.broadcasted_iota(jnp.int32, shape, dim)


def pick(index, table):
    value = jnp.int32(table[0])
    for i, entry in enumerate(table[1:], 1):
        value = jnp.where(index == i, jnp.int32(entry), value)
    return value


def one_hot(condition):
    return condition.astype(jnp.float32).astype(jnp.bfloat16)


class Plan:
    def __init__(self, mesh, seq, local_width):
        self.pipe, self.groups, self.tensor = (mesh.shape[a] for a in ("pipe", "dp", "tensor"))
        self.seq, self.block = seq, local_width // self.pipe
        self.cap = 5 * seq // (4 * self.groups)
        self.pairwise = self.groups == 4 and self.cap % 8 == 0
        self.parts = self.groups if self.pairwise else 1
        self.rows = self.groups * self.cap // self.parts
        self.steps = [0, 3, 1, 2] if self.pairwise else list(range(self.groups))
        n = self.pipe
        order = [0] + list(range(1, n, 2)) + [i for i in reversed(range(2, n)) if i % 2 == 0]
        self.ring = [(order[i], order[(i + 1) % n]) for i in range(n)]
        where = {d: i for i, d in enumerate(order)}
        self.behind = [[order[(where[p] - t) % n] for p in range(n)] for t in range(n)]

    def partner(self, own, i):
        step = jnp.int32(self.steps[i])
        return jnp.bitwise_xor(own, step) if self.pairwise else step

    def regroup(self, parts):
        if not self.pairwise:
            return [lax.all_to_all(parts[0], "dp", split_axis=0, concat_axis=0, tiled=True)]
        got = [parts[0]]
        for step, part in zip(self.steps[1:], parts[1:], strict=True):
            got.append(lax.ppermute(part, "dp", [(g, g ^ step) for g in range(self.groups)]))
        return got


def split_kernel(plan, query, *refs):
    outs, sems = refs[:-1], refs[-1]
    place = lax.axis_index("pipe")
    copies = []
    for t, out in enumerate(outs):
        begin = pl.multiple_of(pick(place, plan.behind[t]) * plan.block, plan.block)
        copies.append(
            pltpu.make_async_copy(query.at[:, pl.ds(begin, plan.block)], out, sems.at[t])
        )
        copies[-1].start()
    for copy in copies:
        copy.wait()


def split(plan, query):
    shape = jax.ShapeDtypeStruct((plan.seq, plan.block), query.dtype)
    return pl.pallas_call(
        functools.partial(split_kernel, plan),
        out_shape=[shape] * (plan.pipe - 1),
        in_specs=[ANY],
        out_specs=[VMEM] * (plan.pipe - 1),
        scratch_shapes=[pltpu.SemaphoreType.DMA((plan.pipe - 1,))],
        compiler_params=PARAMS,
        cost_estimate=COST,
        name="split",
    )(query)


def tables_kernel(plan, docs, counts, bias, send, *places):
    seq, cap, groups = plan.seq, plan.cap, plan.groups
    own = lax.axis_index("dp")
    rows, cols = iota((seq, seq), 0), iota((seq, seq), 1)
    row_doc = jnp.zeros((seq, seq), jnp.int32)
    col_doc = jnp.zeros((seq, seq), jnp.int32)
    end = jnp.int32(0)
    for k in range(docs.shape[1]):
        end = end + docs[0, k]
        row_doc = row_doc + (rows >= end).astype(jnp.int32)
        col_doc = col_doc + (cols >= end).astype(jnp.int32)
    bias[...] = jnp.where((row_doc == col_doc) & (rows <= cols), 0.0, masked_fill)
    rows, cols = iota((groups * cap, seq), 0), iota((groups * cap, seq), 1)
    target = jnp.full((groups * cap, seq), -1, jnp.int32)
    for i in range(groups):
        to = plan.partner(own, i)
        begin = jnp.int32(0)
        for j in range(groups):
            begin = begin + jnp.where(j < to, counts[own, j], 0)
        inside = (rows >= i * cap) & (rows < i * cap + counts[own, to])
        target = jnp.where(inside, rows - i * cap + begin, target)
    send[...] = one_hot(cols == target)
    per = groups // plan.parts
    for part, out in enumerate(places):
        rows, cols = iota(out.shape, 0), iota(out.shape, 1)
        target = jnp.full(out.shape, -1, jnp.int32)
        for slot in range(per):
            source = plan.partner(own, part * per + slot)
            begin = jnp.int32(0)
            for j in range(groups):
                begin = begin + jnp.where(j < source, counts[j, own], 0)
            inside = (cols >= slot * cap) & (cols < slot * cap + counts[source, own])
            target = jnp.where(inside, cols - slot * cap + begin, target)
        out[...] = one_hot(rows == target)


def tables(plan, docs, counts):
    shapes = [
        jax.ShapeDtypeStruct((plan.seq, plan.seq), jnp.float32),
        jax.ShapeDtypeStruct((plan.groups * plan.cap, plan.seq), jnp.bfloat16),
    ] + [jax.ShapeDtypeStruct((plan.seq, plan.rows), jnp.bfloat16)] * plan.parts
    bias, send, *places = pl.pallas_call(
        functools.partial(tables_kernel, plan),
        out_shape=shapes,
        in_specs=[SMEM] * 2,
        out_specs=[VMEM] * len(shapes),
        compiler_params=PARAMS,
        cost_estimate=COST,
        name="tables",
    )(docs, counts)
    return bias, send, places


def softmax(score, bias):
    score = score * (log2_e / HEAD_DIM**0.5) + bias
    weight = jnp.exp2(score - jnp.max(score, axis=0, keepdims=True))
    return weight.astype(jnp.bfloat16), 1.0 / jnp.sum(weight, axis=0, keepdims=True)


def head_columns(plan):
    return [slice(c, c + HEAD_DIM) for c in range(0, plan.block, HEAD_DIM)]


def all_weights(plan, q_ref, k_ref, bias):
    scores = [
        lax.dot_general(
            k_ref[:, cols], q_ref[:, cols], (((1,), (1,)), ((), ())), preferred_element_type=jnp.float32
        )
        for cols in head_columns(plan)
    ]
    return [softmax(score, bias[...]) for score in scores]


def weighted(v_ref, cols, weight, inverse):
    accum = lax.dot_general(
        v_ref[:, cols], weight, (((0,), (0,)), ((), ())), preferred_element_type=jnp.float32
    )
    return (accum * inverse).astype(jnp.bfloat16)


def pick_rows(plan, send, attn, outs):
    picked = lax.dot_general(
        send[...], attn[...], (((1,), (1,)), ((), ())), preferred_element_type=jnp.float32
    )
    for part, out in enumerate(outs):
        out[...] = picked[part * plan.rows : (part + 1) * plan.rows].astype(jnp.bfloat16)


def heads_kernel(plan, q_ref, k_ref, v_ref, bias, attn):
    weights = all_weights(plan, q_ref, k_ref, bias)
    for cols, (weight, inverse) in zip(head_columns(plan), weights, strict=True):
        attn[cols, :] = weighted(v_ref, cols, weight, inverse)


def heads(plan, query, k, v, bias):
    return pl.pallas_call(
        functools.partial(heads_kernel, plan),
        out_shape=jax.ShapeDtypeStruct((plan.block, plan.seq), jnp.bfloat16),
        in_specs=[VMEM] * 4,
        out_specs=VMEM,
        compiler_params=PARAMS,
        cost_estimate=COST,
        name="heads",
    )(query, k, v, bias)


def attend_kernel(plan, bases, q_ref, k_ref, v_ref, bias, send, *refs):
    outs, attn = refs[-1 - plan.parts : -1], refs[-1]
    for i, base in enumerate(refs[:bases]):
        attn[i * plan.block : (i + 1) * plan.block, :] = base[...]
    weights = all_weights(plan, q_ref, k_ref, bias)
    for cols, (weight, inverse) in zip(head_columns(plan), weights, strict=True):
        rows = slice(bases * plan.block + cols.start, bases * plan.block + cols.stop)
        attn[rows, :] = weighted(v_ref, cols, weight, inverse)
    pick_rows(plan, send, attn, outs)


def attend(plan, query, k, v, bias, send, bases=()):
    width = (len(bases) + 1) * plan.block
    return pl.pallas_call(
        functools.partial(attend_kernel, plan, len(bases)),
        out_shape=[jax.ShapeDtypeStruct((plan.rows, width), jnp.bfloat16)] * plan.parts,
        in_specs=[VMEM] * (5 + len(bases)),
        out_specs=[VMEM] * plan.parts,
        scratch_shapes=[pltpu.VMEM((width, plan.seq), jnp.bfloat16)],
        compiler_params=PARAMS,
        cost_estimate=COST,
        name="attend",
    )(query, k, v, bias, send, *bases)


def weigh_kernel(plan, q_ref, k_ref, bias, _, weights, spread, inverses):
    found = all_weights(plan, q_ref, k_ref, bias)
    for h, (cols, (weight, inverse)) in enumerate(zip(head_columns(plan), found, strict=True)):
        weights[:, cols] = weight.T
        spread[:, cols] = jnp.broadcast_to(inverse, (HEAD_DIM, plan.seq)).T
        inverses[h : h + 1, :] = inverse


def weigh(plan, query, k, bias, after):
    count = plan.block // HEAD_DIM
    return pl.pallas_call(
        functools.partial(weigh_kernel, plan),
        out_shape=[
            jax.ShapeDtypeStruct((plan.seq, plan.block), jnp.bfloat16),
            jax.ShapeDtypeStruct((plan.seq, plan.block), jnp.float32),
            jax.ShapeDtypeStruct((count, plan.seq), jnp.float32),
        ],
        in_specs=[VMEM] * 3 + [ANY],
        out_specs=[VMEM] * 3,
        compiler_params=PARAMS,
        cost_estimate=COST,
        name="weigh",
    )(query, k, bias, after)


def finish_kernel(plan, weights, spread, v_ref, send, _, *refs):
    outs, attn = refs[:-1], refs[-1]
    for cols in head_columns(plan):
        accum = jnp.dot(weights[:, cols], v_ref[:, cols], preferred_element_type=jnp.float32)
        attn[:, cols] = (accum * spread[:, cols]).astype(jnp.bfloat16)
    picked = jnp.dot(send[...], attn[...], preferred_element_type=jnp.float32)
    for part, out in enumerate(outs):
        out[...] = picked[part * plan.rows : (part + 1) * plan.rows].astype(jnp.bfloat16)


def finish(plan, weights, spread, v, send, after):
    return pl.pallas_call(
        functools.partial(finish_kernel, plan),
        out_shape=[jax.ShapeDtypeStruct((plan.rows, plan.block), jnp.bfloat16)] * plan.parts,
        in_specs=[VMEM] * 4 + [ANY],
        out_specs=[VMEM] * plan.parts,
        scratch_shapes=[pltpu.VMEM((plan.seq, plan.block), jnp.bfloat16)],
        compiler_params=PARAMS,
        cost_estimate=COST,
        name="finish",
    )(weights, spread, v, send, after)


def squares_of(ref):
    total = None
    for c in range(0, ref.shape[1], HEAD_DIM):
        wide = ref[:, c : c + HEAD_DIM].astype(jnp.float32)
        total = wide * wide if total is None else total + wide * wide
    return total


def place_kernel(plan, widths, summed, extra, sums, *refs):
    parts = plan.parts
    got, matrices, refs = refs[:parts], refs[parts : 2 * parts], refs[2 * parts :]
    blocks, earlier = refs[:extra], refs[extra : extra + sums]
    outs = refs[extra + sums :]
    totals = [squares_of(ref) for ref in blocks] + [ref[...] for ref in earlier]
    base = 0
    for n, (width, out) in enumerate(zip(widths, outs, strict=False)):
        placed = None
        for matrix, ref in zip(matrices, got, strict=True):
            more = jnp.dot(
                matrix[...], ref[:, base : base + width], preferred_element_type=jnp.float32
            )
            placed = more if placed is None else placed + more
        out[...] = placed.astype(jnp.bfloat16)
        if n < summed:
            for c in range(0, width, HEAD_DIM):
                totals.append(placed[:, c : c + HEAD_DIM] * placed[:, c : c + HEAD_DIM])
        base += width
    if summed:
        total = totals[0]
        for more in totals[1:]:
            total = total + more
        outs[-1][...] = total


def place(plan, got, matrices, widths, summed=1, blocks=(), sums=()):
    shapes = [jax.ShapeDtypeStruct((plan.seq, width), jnp.bfloat16) for width in widths]
    if summed:
        shapes.append(jax.ShapeDtypeStruct((plan.seq, HEAD_DIM), jnp.float32))
    args = (*got, *matrices, *blocks, *sums)
    return pl.pallas_call(
        functools.partial(place_kernel, plan, widths, summed, len(blocks), len(sums)),
        out_shape=shapes,
        in_specs=[VMEM] * len(args),
        out_specs=[VMEM] * len(shapes),
        compiler_params=PARAMS,
        cost_estimate=COST,
        name="place",
    )(*args)


def norm_kernel(plan, spots, sums, *refs):
    count = len(spots)
    pieces, refs = refs[:count], refs[count:]
    squares, (gain, out, held, sems) = refs[:sums], refs[sums:]
    width = HEADS * HEAD_DIM
    lanes = squares[0][...]
    for ref in squares[1:]:
        lanes = lanes + ref[...]
    mean = jnp.sum(lanes, axis=1, keepdims=True) / width
    factor = jnp.broadcast_to(lax.rsqrt(mean + norm_eps), lanes.shape)
    device = lax.axis_index("pipe")
    copies = []
    for i, ((t, offset), ref) in enumerate(zip(spots, pieces, strict=True)):
        begin = pick(device, plan.behind[t]) * plan.block + offset
        size = ref.shape[1]
        for c in range(0, size, HEAD_DIM):
            at = pl.ds(pl.multiple_of(begin + c, HEAD_DIM), HEAD_DIM)
            wide = ref[:, c : c + HEAD_DIM].astype(jnp.float32)
            spot = slice(t * plan.block + offset + c, t * plan.block + offset + c + HEAD_DIM)
            held[:, spot] = (wide * factor * gain[:, at]).astype(jnp.bfloat16)
        spot = pl.ds(t * plan.block + offset, size)
        at = pl.ds(pl.multiple_of(begin, HEAD_DIM), size)
        copies.append(pltpu.make_async_copy(held.at[:, spot], out.at[:, at], sems.at[i]))
        copies[-1].start()
    for copy in copies:
        copy.wait()


def norm(plan, pieces, squares, gain):
    arrays, spots = [piece[0] for piece in pieces], tuple(piece[1:] for piece in pieces)
    return pl.pallas_call(
        functools.partial(norm_kernel, plan, spots, len(squares)),
        out_shape=jax.ShapeDtypeStruct((plan.seq, plan.pipe * plan.block), jnp.bfloat16),
        in_specs=[VMEM] * (len(arrays) + len(squares) + 1),
        out_specs=ANY,
        scratch_shapes=[
            pltpu.VMEM((plan.seq, plan.pipe * plan.block), jnp.bfloat16),
            pltpu.SemaphoreType.DMA((len(arrays),)),
        ],
        compiler_params=PARAMS,
        cost_estimate=COST,
        name="norm",
    )(*arrays, *squares, gain)


def body(mesh, queries, cache_keys, cache_values, doc_lengths, row_counts, out_gain):
    query = queries[0]
    seq, local_width = query.shape
    plan = Plan(mesh, seq, local_width)
    n, block = plan.pipe, plan.block
    forward, backward = plan.ring, [(b, a) for a, b in plan.ring]
    keys, values = cache_keys.reshape(seq, block), cache_values.reshape(seq, block)
    gain = out_gain.astype(jnp.float32).reshape(1, local_width)

    begin = pick(lax.axis_index("pipe"), plan.behind[n - 1]) * block
    ahead = lax.dynamic_slice_in_dim(query, begin, block, 1)
    asked = split(plan, query)
    bias, send, places = tables(plan, doc_lengths, row_counts)
    k, v = lax.ppermute(keys, "pipe", forward), lax.ppermute(values, "pipe", forward)
    lent = lax.ppermute(ahead, "pipe", forward)
    own = heads(plan, asked[0], keys, values, bias)
    arrived = plan.regroup(attend(plan, lent, keys, values, bias, send, bases=(own,)))
    mine, borrowed, total = place(plan, arrived, places, (block, block), summed=1)
    pieces = [(mine, 0, 0)]
    for t in range(1, n - 2):
        sent = attend(plan, asked[t], k, v, bias, send)
        v_out, _ = lax.optimization_barrier((v, sent[0]))
        *sent, _ = lax.optimization_barrier((*sent, arrived[1 % len(arrived)]))
        got = plan.regroup(sent)
        placed, total = place(plan, got, places, (block,), sums=(total,))
        pieces.append((placed, t, 0))
        k, v = lax.ppermute(k, "pipe", forward), lax.ppermute(v_out, "pipe", forward)
    weights, spread, inverses = weigh(plan, asked[n - 2], k, bias, borrowed)
    met = inverses
    if plan.tensor == 2:
        met = lax.ppermute(inverses, "tensor", [(0, 1), (1, 0)])
    borrowed, *_ = lax.optimization_barrier((borrowed, met, *got))
    returned = lax.ppermute(borrowed, "pipe", backward)
    got = plan.regroup(finish(plan, weights, spread, v, send, met))
    placed, total = place(plan, got, places, (block,), blocks=(returned,), sums=(total,))
    pieces += [(placed, n - 2, 0), (returned, n - 1, 0)]
    if plan.tensor == 2:
        sums = (total, lax.ppermute(total, "tensor", [(0, 1), (1, 0)]))
    else:
        sums = (lax.psum(total, "tensor"),)
    return norm(plan, pieces, sums, gain)[None]


def solution(mesh):
    return jax.shard_map(
        functools.partial(body, mesh),
        mesh=mesh,
        in_specs=(
            P("pipe", "dp", "tensor"),
            P("dp", "tensor", "pipe", None),
            P("dp", "tensor", "pipe", None),
            P("dp", None),
            P(),
            P("tensor"),
        ),
        out_specs=P("pipe", "dp", "tensor"),
        check_vma=False,
    )
```

```python
import functools

import jax
import jax.numpy as jnp
from jax import lax
from jax.experimental import pallas as pl
from jax.experimental.pallas import tpu as pltpu
from jax.sharding import PartitionSpec as P

HEADS = 64
HEAD_DIM = 128

masked_fill = -1e30
norm_eps = 1e-06
log2_e = 1.4426950408889634

VMEM = pl.BlockSpec(memory_space=pltpu.VMEM)
SMEM = pl.BlockSpec(memory_space=pltpu.SMEM)
ANY = pl.BlockSpec(memory_space=pl.ANY)
COST = pl.CostEstimate(flops=1, bytes_accessed=1, transcendentals=0)
PARAMS = pltpu.CompilerParams(vmem_limit_bytes=32 * 1024 * 1024)


def iota(shape, dim):
    return lax.broadcasted_iota(jnp.int32, shape, dim)


def pick(index, table):
    value = jnp.int32(table[0])
    for i, entry in enumerate(table[1:], 1):
        value = jnp.where(index == i, jnp.int32(entry), value)
    return value


def one_hot(condition):
    return condition.astype(jnp.float32).astype(jnp.bfloat16)


class Plan:
    def __init__(self, mesh, seq, local_width):
        self.pipe, self.groups, self.tensor = (mesh.shape[a] for a in ("pipe", "dp", "tensor"))
        self.seq, self.block = seq, local_width // self.pipe
        self.cap = 5 * seq // (4 * self.groups)
        self.pairwise = self.groups == 4 and self.cap % 8 == 0
        self.parts = self.groups if self.pairwise else 1
        self.rows = self.groups * self.cap // self.parts
        self.steps = [0, 3, 1, 2] if self.pairwise else list(range(self.groups))
        n = self.pipe
        order = [0] + list(range(1, n, 2)) + [i for i in reversed(range(2, n)) if i % 2 == 0]
        self.ring = [(order[i], order[(i + 1) % n]) for i in range(n)]
        where = {d: i for i, d in enumerate(order)}
        self.behind = [[order[(where[p] - t) % n] for p in range(n)] for t in range(n)]

    def partner(self, own, i):
        step = jnp.int32(self.steps[i])
        return jnp.bitwise_xor(own, step) if self.pairwise else step

    def regroup(self, parts):
        if not self.pairwise:
            return [lax.all_to_all(parts[0], "dp", split_axis=0, concat_axis=0, tiled=True)]
        got = [parts[0]]
        for step, part in zip(self.steps[1:], parts[1:], strict=True):
            got.append(lax.ppermute(part, "dp", [(g, g ^ step) for g in range(self.groups)]))
        return got


def split_kernel(plan, query, *refs):
    outs, sems = refs[:-1], refs[-1]
    place = lax.axis_index("pipe")
    copies = []
    for t, out in enumerate(outs):
        begin = pl.multiple_of(pick(place, plan.behind[t]) * plan.block, plan.block)
        copies.append(
            pltpu.make_async_copy(query.at[:, pl.ds(begin, plan.block)], out, sems.at[t])
        )
        copies[-1].start()
    for copy in copies:
        copy.wait()


def split(plan, query):
    shape = jax.ShapeDtypeStruct((plan.seq, plan.block), query.dtype)
    return pl.pallas_call(
        functools.partial(split_kernel, plan),
        out_shape=[shape] * (plan.pipe - 1),
        in_specs=[ANY],
        out_specs=[VMEM] * (plan.pipe - 1),
        scratch_shapes=[pltpu.SemaphoreType.DMA((plan.pipe - 1,))],
        compiler_params=PARAMS,
        cost_estimate=COST,
        name="split",
    )(query)


def tables_kernel(plan, docs, counts, bias, send, *places):
    seq, cap, groups = plan.seq, plan.cap, plan.groups
    own = lax.axis_index("dp")
    rows, cols = iota((seq, seq), 0), iota((seq, seq), 1)
    row_doc = jnp.zeros((seq, seq), jnp.int32)
    col_doc = jnp.zeros((seq, seq), jnp.int32)
    end = jnp.int32(0)
    for k in range(docs.shape[1]):
        end = end + docs[0, k]
        row_doc = row_doc + (rows >= end).astype(jnp.int32)
        col_doc = col_doc + (cols >= end).astype(jnp.int32)
    bias[...] = jnp.where((row_doc == col_doc) & (rows <= cols), 0.0, masked_fill)
    rows, cols = iota((groups * cap, seq), 0), iota((groups * cap, seq), 1)
    target = jnp.full((groups * cap, seq), -1, jnp.int32)
    for i in range(groups):
        to = plan.partner(own, i)
        begin = jnp.int32(0)
        for j in range(groups):
            begin = begin + jnp.where(j < to, counts[own, j], 0)
        inside = (rows >= i * cap) & (rows < i * cap + counts[own, to])
        target = jnp.where(inside, rows - i * cap + begin, target)
    send[...] = one_hot(cols == target)
    per = groups // plan.parts
    for part, out in enumerate(places):
        rows, cols = iota(out.shape, 0), iota(out.shape, 1)
        target = jnp.full(out.shape, -1, jnp.int32)
        for slot in range(per):
            source = plan.partner(own, part * per + slot)
            begin = jnp.int32(0)
            for j in range(groups):
                begin = begin + jnp.where(j < source, counts[j, own], 0)
            inside = (cols >= slot * cap) & (cols < slot * cap + counts[source, own])
            target = jnp.where(inside, cols - slot * cap + begin, target)
        out[...] = one_hot(rows == target)


def tables(plan, docs, counts):
    shapes = [
        jax.ShapeDtypeStruct((plan.seq, plan.seq), jnp.float32),
        jax.ShapeDtypeStruct((plan.groups * plan.cap, plan.seq), jnp.bfloat16),
    ] + [jax.ShapeDtypeStruct((plan.seq, plan.rows), jnp.bfloat16)] * plan.parts
    bias, send, *places = pl.pallas_call(
        functools.partial(tables_kernel, plan),
        out_shape=shapes,
        in_specs=[SMEM] * 2,
        out_specs=[VMEM] * len(shapes),
        compiler_params=PARAMS,
        cost_estimate=COST,
        name="tables",
    )(docs, counts)
    return bias, send, places


def softmax(score, bias):
    score = score * (log2_e / HEAD_DIM**0.5) + bias
    weight = jnp.exp2(score - jnp.max(score, axis=0, keepdims=True))
    return weight.astype(jnp.bfloat16), 1.0 / jnp.sum(weight, axis=0, keepdims=True)


def head_columns(plan):
    return [slice(c, c + HEAD_DIM) for c in range(0, plan.block, HEAD_DIM)]


def all_weights(plan, q_ref, k_ref, bias):
    scores = [
        lax.dot_general(
            k_ref[:, cols], q_ref[:, cols], (((1,), (1,)), ((), ())), preferred_element_type=jnp.float32
        )
        for cols in head_columns(plan)
    ]
    return [softmax(score, bias[...]) for score in scores]


def weighted(v_ref, cols, weight, inverse):
    accum = lax.dot_general(
        v_ref[:, cols], weight, (((0,), (0,)), ((), ())), preferred_element_type=jnp.float32
    )
    return (accum * inverse).astype(jnp.bfloat16)


def pick_rows(plan, send, attn, outs):
    picked = lax.dot_general(
        send[...], attn[...], (((1,), (1,)), ((), ())), preferred_element_type=jnp.float32
    )
    for part, out in enumerate(outs):
        out[...] = picked[part * plan.rows : (part + 1) * plan.rows].astype(jnp.bfloat16)


def heads_kernel(plan, q_ref, k_ref, v_ref, bias, attn):
    weights = all_weights(plan, q_ref, k_ref, bias)
    for cols, (weight, inverse) in zip(head_columns(plan), weights, strict=True):
        attn[cols, :] = weighted(v_ref, cols, weight, inverse)


def heads(plan, query, k, v, bias):
    return pl.pallas_call(
        functools.partial(heads_kernel, plan),
        out_shape=jax.ShapeDtypeStruct((plan.block, plan.seq), jnp.bfloat16),
        in_specs=[VMEM] * 4,
        out_specs=VMEM,
        compiler_params=PARAMS,
        cost_estimate=COST,
        name="heads",
    )(query, k, v, bias)


def attend_kernel(plan, bases, q_ref, k_ref, v_ref, bias, send, *refs):
    outs, attn = refs[-1 - plan.parts : -1], refs[-1]
    for i, base in enumerate(refs[:bases]):
        attn[i * plan.block : (i + 1) * plan.block, :] = base[...]
    weights = all_weights(plan, q_ref, k_ref, bias)
    for cols, (weight, inverse) in zip(head_columns(plan), weights, strict=True):
        rows = slice(bases * plan.block + cols.start, bases * plan.block + cols.stop)
        attn[rows, :] = weighted(v_ref, cols, weight, inverse)
    pick_rows(plan, send, attn, outs)


def attend(plan, query, k, v, bias, send, bases=()):
    width = (len(bases) + 1) * plan.block
    return pl.pallas_call(
        functools.partial(attend_kernel, plan, len(bases)),
        out_shape=[jax.ShapeDtypeStruct((plan.rows, width), jnp.bfloat16)] * plan.parts,
        in_specs=[VMEM] * (5 + len(bases)),
        out_specs=[VMEM] * plan.parts,
        scratch_shapes=[pltpu.VMEM((width, plan.seq), jnp.bfloat16)],
        compiler_params=PARAMS,
        cost_estimate=COST,
        name="attend",
    )(query, k, v, bias, send, *bases)


def weigh_kernel(plan, q_ref, k_ref, bias, _, weights, spread, inverses):
    found = all_weights(plan, q_ref, k_ref, bias)
    for h, (cols, (weight, inverse)) in enumerate(zip(head_columns(plan), found, strict=True)):
        weights[:, cols] = weight.T
        spread[:, cols] = jnp.broadcast_to(inverse, (HEAD_DIM, plan.seq)).T
        inverses[h : h + 1, :] = inverse


def weigh(plan, query, k, bias, after):
    count = plan.block // HEAD_DIM
    return pl.pallas_call(
        functools.partial(weigh_kernel, plan),
        out_shape=[
            jax.ShapeDtypeStruct((plan.seq, plan.block), jnp.bfloat16),
            jax.ShapeDtypeStruct((plan.seq, plan.block), jnp.float32),
            jax.ShapeDtypeStruct((count, plan.seq), jnp.float32),
        ],
        in_specs=[VMEM] * 3 + [ANY],
        out_specs=[VMEM] * 3,
        compiler_params=PARAMS,
        cost_estimate=COST,
        name="weigh",
    )(query, k, bias, after)


def finish_kernel(plan, weights, spread, v_ref, send, _, *refs):
    outs, attn = refs[:-1], refs[-1]
    for cols in head_columns(plan):
        accum = jnp.dot(weights[:, cols], v_ref[:, cols], preferred_element_type=jnp.float32)
        attn[:, cols] = (accum * spread[:, cols]).astype(jnp.bfloat16)
    picked = jnp.dot(send[...], attn[...], preferred_element_type=jnp.float32)
    for part, out in enumerate(outs):
        out[...] = picked[part * plan.rows : (part + 1) * plan.rows].astype(jnp.bfloat16)


def finish(plan, weights, spread, v, send, after):
    return pl.pallas_call(
        functools.partial(finish_kernel, plan),
        out_shape=[jax.ShapeDtypeStruct((plan.rows, plan.block), jnp.bfloat16)] * plan.parts,
        in_specs=[VMEM] * 4 + [ANY],
        out_specs=[VMEM] * plan.parts,
        scratch_shapes=[pltpu.VMEM((plan.seq, plan.block), jnp.bfloat16)],
        compiler_params=PARAMS,
        cost_estimate=COST,
        name="finish",
    )(weights, spread, v, send, after)


def squares_of(ref):
    total = None
    for c in range(0, ref.shape[1], HEAD_DIM):
        wide = ref[:, c : c + HEAD_DIM].astype(jnp.float32)
        total = wide * wide if total is None else total + wide * wide
    return total


def place_kernel(plan, widths, summed, extra, sums, *refs):
    parts = plan.parts
    got, matrices, refs = refs[:parts], refs[parts : 2 * parts], refs[2 * parts :]
    blocks, earlier = refs[:extra], refs[extra : extra + sums]
    outs = refs[extra + sums :]
    totals = [squares_of(ref) for ref in blocks] + [ref[...] for ref in earlier]
    base = 0
    for n, (width, out) in enumerate(zip(widths, outs, strict=False)):
        placed = None
        for matrix, ref in zip(matrices, got, strict=True):
            more = jnp.dot(
                matrix[...], ref[:, base : base + width], preferred_element_type=jnp.float32
            )
            placed = more if placed is None else placed + more
        out[...] = placed.astype(jnp.bfloat16)
        if n < summed:
            for c in range(0, width, HEAD_DIM):
                totals.append(placed[:, c : c + HEAD_DIM] * placed[:, c : c + HEAD_DIM])
        base += width
    if summed:
        total = totals[0]
        for more in totals[1:]:
            total = total + more
        outs[-1][...] = total


def place(plan, got, matrices, widths, summed=1, blocks=(), sums=()):
    shapes = [jax.ShapeDtypeStruct((plan.seq, width), jnp.bfloat16) for width in widths]
    if summed:
        shapes.append(jax.ShapeDtypeStruct((plan.seq, HEAD_DIM), jnp.float32))
    args = (*got, *matrices, *blocks, *sums)
    return pl.pallas_call(
        functools.partial(place_kernel, plan, widths, summed, len(blocks), len(sums)),
        out_shape=shapes,
        in_specs=[VMEM] * len(args),
        out_specs=[VMEM] * len(shapes),
        compiler_params=PARAMS,
        cost_estimate=COST,
        name="place",
    )(*args)


def sums_kernel(plan, *refs):
    parts = plan.parts
    got, matrices, (block, earlier, out) = refs[:parts], refs[parts : 2 * parts], refs[2 * parts :]
    total = squares_of(block) + earlier[...]
    for matrix, ref in zip(matrices, got, strict=True):
        total = total + jnp.dot(
            matrix[...].astype(jnp.float32),
            squares_of(ref),
            preferred_element_type=jnp.float32,
            precision=lax.Precision.HIGHEST,
        )
    out[...] = total


def sums_of(plan, got, matrices, block, earlier):
    args = (*got, *matrices, block, earlier)
    return pl.pallas_call(
        functools.partial(sums_kernel, plan),
        out_shape=jax.ShapeDtypeStruct((plan.seq, HEAD_DIM), jnp.float32),
        in_specs=[VMEM] * len(args),
        out_specs=VMEM,
        compiler_params=PARAMS,
        cost_estimate=COST,
        name="sums",
    )(*args)


def norm_kernel(plan, spots, sums, *refs):
    count = len(spots)
    pieces, refs = refs[:count], refs[count:]
    squares, (gain, out, held, sems) = refs[:sums], refs[sums:]
    width = HEADS * HEAD_DIM
    lanes = squares[0][...]
    for ref in squares[1:]:
        lanes = lanes + ref[...]
    mean = jnp.sum(lanes, axis=1, keepdims=True) / width
    factor = jnp.broadcast_to(lax.rsqrt(mean + norm_eps), lanes.shape)
    device = lax.axis_index("pipe")
    copies = []
    for i, ((t, offset), ref) in enumerate(zip(spots, pieces, strict=True)):
        begin = pick(device, plan.behind[t]) * plan.block + offset
        size = ref.shape[1]
        for c in range(0, size, HEAD_DIM):
            at = pl.ds(pl.multiple_of(begin + c, HEAD_DIM), HEAD_DIM)
            wide = ref[:, c : c + HEAD_DIM].astype(jnp.float32)
            spot = slice(t * plan.block + offset + c, t * plan.block + offset + c + HEAD_DIM)
            held[:, spot] = (wide * factor * gain[:, at]).astype(jnp.bfloat16)
        spot = pl.ds(t * plan.block + offset, size)
        at = pl.ds(pl.multiple_of(begin, HEAD_DIM), size)
        copies.append(pltpu.make_async_copy(held.at[:, spot], out.at[:, at], sems.at[i]))
        copies[-1].start()
    for copy in copies:
        copy.wait()


def norm(plan, pieces, squares, gain):
    arrays, spots = [piece[0] for piece in pieces], tuple(piece[1:] for piece in pieces)
    return pl.pallas_call(
        functools.partial(norm_kernel, plan, spots, len(squares)),
        out_shape=jax.ShapeDtypeStruct((plan.seq, plan.pipe * plan.block), jnp.bfloat16),
        in_specs=[VMEM] * (len(arrays) + len(squares) + 1),
        out_specs=ANY,
        scratch_shapes=[
            pltpu.VMEM((plan.seq, plan.pipe * plan.block), jnp.bfloat16),
            pltpu.SemaphoreType.DMA((len(arrays),)),
        ],
        compiler_params=PARAMS,
        cost_estimate=COST,
        name="norm",
    )(*arrays, *squares, gain)


def body(mesh, queries, cache_keys, cache_values, doc_lengths, row_counts, out_gain):
    query = queries[0]
    seq, local_width = query.shape
    plan = Plan(mesh, seq, local_width)
    n, block = plan.pipe, plan.block
    forward, backward = plan.ring, [(b, a) for a, b in plan.ring]
    keys, values = cache_keys.reshape(seq, block), cache_values.reshape(seq, block)
    gain = out_gain.astype(jnp.float32).reshape(1, local_width)

    begin = pick(lax.axis_index("pipe"), plan.behind[n - 1]) * block
    ahead = lax.dynamic_slice_in_dim(query, begin, block, 1)
    asked = split(plan, query)
    bias, send, places = tables(plan, doc_lengths, row_counts)
    k, v = lax.ppermute(keys, "pipe", forward), lax.ppermute(values, "pipe", forward)
    lent = lax.ppermute(ahead, "pipe", forward)
    own = heads(plan, asked[0], keys, values, bias)
    arrived = plan.regroup(attend(plan, lent, keys, values, bias, send, bases=(own,)))
    mine, borrowed, total = place(plan, arrived, places, (block, block), summed=1)
    pieces = [(mine, 0, 0)]
    for t in range(1, n - 2):
        sent = attend(plan, asked[t], k, v, bias, send)
        v_out, _ = lax.optimization_barrier((v, sent[0]))
        *sent, _ = lax.optimization_barrier((*sent, arrived[1 % len(arrived)]))
        got = plan.regroup(sent)
        placed, total = place(plan, got, places, (block,), sums=(total,))
        pieces.append((placed, t, 0))
        k, v = lax.ppermute(k, "pipe", forward), lax.ppermute(v_out, "pipe", forward)
    weights, spread, inverses = weigh(plan, asked[n - 2], k, bias, borrowed)
    met = inverses
    if plan.tensor == 2:
        met = lax.ppermute(inverses, "tensor", [(0, 1), (1, 0)])
    borrowed, *_ = lax.optimization_barrier((borrowed, met, *got))
    returned = lax.ppermute(borrowed, "pipe", backward)
    got = plan.regroup(finish(plan, weights, spread, v, send, met))
    total = sums_of(plan, got, places, returned, total)
    (placed,) = place(plan, got, places, (block,), summed=0)
    pieces += [(placed, n - 2, 0), (returned, n - 1, 0)]
    if plan.tensor == 2:
        sums = (total, lax.ppermute(total, "tensor", [(0, 1), (1, 0)]))
    else:
        sums = (lax.psum(total, "tensor"),)
    return norm(plan, pieces, sums, gain)[None]


def solution(mesh):
    return jax.shard_map(
        functools.partial(body, mesh),
        mesh=mesh,
        in_specs=(
            P("pipe", "dp", "tensor"),
            P("dp", "tensor", "pipe", None),
            P("dp", "tensor", "pipe", None),
            P("dp", None),
            P(),
            P("tensor"),
        ),
        out_specs=P("pipe", "dp", "tensor"),
        check_vma=False,
    )
```
